32 devices in a mesh: opt: 8 (over z, y), layer: 4 (over x, core).
Axes of the slice: x: 2, y: 2, z: 4, core: 2. Of those that a mesh axis runs over, the one named last changes fastest.
Arguments:
- momentum: bfloat16 [4, 8, 1024, 512], P('layer', None, 'opt'), may hold values from -4000 to 4000
- weights: bfloat16 [4, 8, 1024, 512], P('layer', None, 'opt'), may hold values from -6 to 6
Outputs:
- new_weights: bfloat16 [4, 8, 1024, 512], P('layer', None, 'opt')
The draws below stay inside these ranges and needn't reach their ends.
All inputs are finite; a program needn't handle non-finite values.
Results may differ from the reference program's by a relative error of at most 0.0041.
Values may be sent and summed in bfloat16 or wider, within the bound.
No kernel may reach another device: no remote copies, remote signals or barrier semaphores. Data moves between devices by JAX's collectives and lax.ppermute only.
A program may use at most 64 MiB of HBM per device.

```python
import math
import jax
import jax.numpy as jnp
from jax import lax

D = 1024
FF = 512
ITERS = 3
EXPERTS = 8
LAYERS = 4


def draw_momentum(key, part):
    subkeys = jax.random.split(key, 3)
    full_shape = (LAYERS, EXPERTS, D, FF)
    row_scale = jnp.exp(jax.random.uniform(subkeys[0], (LAYERS, EXPERTS, D, 1), jnp.float32, 0.0, math.log(10.0)))
    col_scale = jnp.exp(jax.random.uniform(subkeys[1], (LAYERS, EXPERTS, 1, FF), jnp.float32, 0.0, math.log(10.0)))
    layer_ramp = lax.broadcasted_iota(jnp.float32, (LAYERS, 1, 1, 1), 0) / max(LAYERS - 1, 1)
    entries = jax.random.truncated_normal(subkeys[2], -4.0, 4.0, full_shape, jnp.float32)
    layer_scale = 1.0 + 2.0 * layer_ramp
    return (entries * row_scale * col_scale * layer_scale).astype(jnp.bfloat16)


def levels(key, dims, cuts, low, high):
    level = 1.0
    for position, shards_of in cuts:
        heights = jax.random.uniform(jax.random.fold_in(jax.random.fold_in(key, 6), position), (shards_of,), jnp.float32, low / len(cuts), high / len(cuts))
        level = level * jnp.repeat(jnp.exp(heights), dims[position] // shards_of).reshape((-1,) + (1,) * (len(dims) - 1 - position))
    return level


def scatter_about(rng, extent, deviation, reach, shards=(), held_as=jnp.bfloat16):
    values = jax.random.normal(rng, extent, jnp.float32) * deviation
    if len(shards) > 0:
        values = levels(rng, extent, shards, -0.22, 0.18) * values
    return jnp.clip(values, min=-reach, max=reach).astype(held_as)


def setup_inputs(seed: int = 0) -> dict:
    seeds = jax.random.split(jax.random.key(seed), 3)
    momentum = draw_momentum(jax.random.fold_in(seeds[2], 71), 0)
    weights = scatter_about(seeds[1], (LAYERS, EXPERTS, D, FF), 1.0, 6.0, ((0, 4), (2, 8)))
    return {"momentum": momentum, "weights": weights}


first_coef = 3.4445
second_coef = -4.775
third_coef = 2.0315
epsilon = 1e-06
step_rate = 0.5
decay_rate = 0.1

def newton(gram_sum, trace_sum):
    highest = lax.Precision.HIGHEST
    identity_matrix = jnp.eye(FF, dtype=jnp.float32)
    current = gram_sum / (trace_sum + epsilon)
    accum = identity_matrix
    for iteration in range(ITERS):
        squared = jnp.dot(current, current, precision=highest)
        polynomial = first_coef * identity_matrix + second_coef * current + third_coef * squared
        accum = jnp.dot(accum, polynomial, precision=highest)
        if iteration + 1 < ITERS:
            current = jnp.dot(jnp.dot(current, polynomial, precision=highest), polynomial, precision=highest)
    return accum

def reference(momentum, weights):

    def one_expert(expert):
        stacked = lax.dynamic_index_in_dim(momentum, expert, 1, keepdims=False)
        plates = lax.dynamic_index_in_dim(weights, expert, 1, keepdims=False)
        gram_sum = jnp.zeros((FF, FF), jnp.float32)
        for layer_index in range(LAYERS):
            gram_sum = gram_sum + jnp.dot(stacked[layer_index].T, stacked[layer_index], preferred_element_type=jnp.float32)
        trace_sum = jnp.trace(gram_sum)
        accum = newton(gram_sum, trace_sum)
        factor = (accum * jnp.sqrt(LAYERS * D / (trace_sum + epsilon))).astype(jnp.bfloat16)
        results = []
        for layer_index in range(LAYERS):
            update = jnp.dot(stacked[layer_index], factor, preferred_element_type=jnp.float32).astype(jnp.bfloat16)
            update = lax.optimization_barrier(update)
            shrink = 1.0 - step_rate * decay_rate
            fresh = shrink * plates[layer_index].astype(jnp.float32) - step_rate * update.astype(jnp.float32)
            results.append(fresh.astype(jnp.bfloat16))
        return jnp.stack(results)
    mapped = lax.map(one_expert, jnp.arange(EXPERTS, dtype=jnp.int32))
    return jnp.swapaxes(mapped, 0, 1)
```

```python
import functools

import jax
import jax.numpy as jnp
from jax import lax
from jax.experimental import pallas as pl
from jax.experimental.pallas import tpu as pltpu
from jax.sharding import PartitionSpec as P

ITERS = 3
BLOCK = 128
VMEM_BYTES = 48 << 20

first_coef = 3.4445
second_coef = -4.775
third_coef = 2.0315
epsilon = 1e-06
step_rate = 0.5
decay_rate = 0.1

AXES = ("opt", "layer")


def layout(opt, layer):
    lows, highs, shift = opt // 2, layer // 2, opt // 4

    def device(half, low, high, pair):
        low = (low + half * shift) % lows
        return (half * lows + low) * layer + high * 2 + pair

    places = [(low, high) for low in range(lows) for high in range(highs)]
    groups = [[device(half, *place, pair) for place in places] for half in range(2) for pair in range(2)]
    pair_swap = [
        (device(half, *place, pair), device(half, *place, 1 - pair))
        for half in range(2)
        for pair in range(2)
        for place in places
    ]
    half_swap = [
        (device(half, *place, pair), device(1 - half, *place, pair))
        for half in range(2)
        for pair in range(2)
        for place in places
    ]
    return groups, pair_swap, half_swap


def block_pairs(order):
    count = order // BLOCK
    upper = [(i, j) for i in range(count) for j in range(i, count)]
    first = [pair for pair in upper if pair[0] < count // 4 or pair[0] == pair[1] and pair[0] < count // 2]
    return first + [pair for pair in upper if pair not in first]


def call(kernel, out_shape, grid, in_specs, out_specs, *operands):
    return pl.pallas_call(
        kernel,
        out_shape=out_shape,
        grid=grid,
        in_specs=in_specs,
        out_specs=out_specs,
        compiler_params=pltpu.CompilerParams(vmem_limit_bytes=VMEM_BYTES),
    )(*operands)


def whole(array):
    rest = array.shape[1:]
    return pl.BlockSpec((None,) + rest, lambda expert: (expert,) + (0,) * len(rest))


SCALAR = pl.BlockSpec(memory_space=pltpu.SMEM)


def product(first, second):
    return jnp.dot(first, second, preferred_element_type=jnp.float32)


def gram_kernel(pairs, rows_ref, gram_ref):
    wide = 2 * BLOCK
    order = rows_ref.shape[1]
    place = {pair: index for index, pair in enumerate(pairs)}
    for row in range(0, order, wide):
        for column in range(row, order, wide):
            tile = lax.dot_general(
                rows_ref[:, row : row + wide],
                rows_ref[:, column : column + wide],
                (((0,), (0,)), ((), ())),
                preferred_element_type=jnp.float32,
            )
            for i in range(2):
                for j in range(2):
                    index = place.get((row // BLOCK + i, column // BLOCK + j))
                    if index is not None:
                        gram_ref[pl.ds(index * BLOCK, BLOCK), :] = tile[
                            i * BLOCK : (i + 1) * BLOCK, j * BLOCK : (j + 1) * BLOCK
                        ]


def pair_sum_kernel(pair_ref, own_ref, other_ref, total_ref, half_ref):
    total_ref[...] = own_ref[...] + other_ref[...]
    length = half_ref.shape[0]
    start = pl.multiple_of(pair_ref[0] * length, length)
    half_ref[...] = total_ref[pl.ds(start, length), :].astype(half_ref.dtype)


def split(matrix):
    high = matrix.astype(jnp.bfloat16)
    return high, (matrix - high.astype(jnp.float32)).astype(jnp.bfloat16)


def product_of_split(first, second):
    return product(first[0], second[0]) + (product(first[0], second[1]) + product(first[1], second[0]))


def newton(current, identity):
    accum = None
    for iteration in range(ITERS):
        halves = split(current)
        squared = product_of_split(halves, halves)
        polynomial = jnp.where(identity, first_coef, 0.0) + second_coef * current + third_coef * squared
        poly_halves = split(polynomial)
        accum = polynomial if accum is None else product_of_split(split(accum), poly_halves)
        if iteration + 1 < ITERS:
            current = product_of_split(split(product_of_split(halves, poly_halves)), poly_halves)
    return accum


def update_kernel(pairs, scale, pair_ref, total_ref, near_ref, far_ref, rows_ref, update_ref):
    order = rows_ref.shape[1]
    length = near_ref.shape[0]
    first_pair = pair_ref[0] == 0
    near, far = near_ref[...].astype(jnp.float32), far_ref[...].astype(jnp.float32)
    total = (
        total_ref[:length, :] + jnp.where(first_pair, near, far),
        total_ref[length:, :] + jnp.where(first_pair, far, near),
    )
    blocks = {}
    for index, (i, j) in enumerate(pairs):
        place = index * BLOCK % length
        tile = total[index * BLOCK // length][place : place + BLOCK]
        blocks[i, j] = tile
        if i != j:
            blocks[j, i] = tile.T
    count = order // BLOCK
    gram = jnp.concatenate(
        [jnp.concatenate([blocks[i, j] for j in range(count)], axis=1) for i in range(count)], axis=0
    )
    identity = lax.broadcasted_iota(jnp.int32, gram.shape, 0) == lax.broadcasted_iota(jnp.int32, gram.shape, 1)
    trace_sum = jnp.sum(jnp.where(identity, gram, 0.0))
    accum = newton(gram / (trace_sum + epsilon), identity)
    factor = (accum * jnp.sqrt(scale / (trace_sum + epsilon))).astype(jnp.bfloat16)
    update_ref[...] = product(rows_ref[...], factor).astype(update_ref.dtype)


def on_device(momentum, weights):
    _, experts, row_count, order = momentum.shape
    opt, layer = lax.axis_size("opt"), lax.axis_size("layer")
    groups, pair_swap, half_swap = layout(opt, layer)
    members = len(groups[0])
    owned = experts // members
    pairs = block_pairs(order)
    packed_rows = len(pairs) * BLOCK
    pair = (lax.axis_index("layer") % 2).astype(jnp.int32).reshape(1)
    exchange = functools.partial(
        lax.all_to_all, axis_name=AXES, split_axis=0, concat_axis=0, axis_index_groups=groups, tiled=True
    )

    arrived = exchange(momentum[0])
    rows = arrived.reshape(members, owned, row_count, order).swapaxes(0, 1)
    rows = rows.reshape(owned, members * row_count, order)

    packed = jax.ShapeDtypeStruct((owned, packed_rows, BLOCK), jnp.float32)
    half_shape = jax.ShapeDtypeStruct((owned, packed_rows // 2, BLOCK), jnp.bfloat16)
    own = call(
        functools.partial(gram_kernel, pairs), packed, (owned,), [whole(rows)], whole(packed), rows
    )
    other = lax.ppermute(own, AXES, pair_swap)
    total, half = call(
        pair_sum_kernel,
        (packed, half_shape),
        (owned,),
        [SCALAR, whole(packed), whole(packed)],
        (whole(packed), whole(half_shape)),
        pair,
        own,
        other,
    )
    near = lax.ppermute(half, AXES, half_swap)
    far = lax.ppermute(near, AXES, pair_swap)
    scale = float(layer * opt * row_count)
    update = call(
        functools.partial(update_kernel, pairs, scale),
        jax.ShapeDtypeStruct(rows.shape, jnp.bfloat16),
        (owned,),
        [SCALAR, whole(packed), whole(half_shape), whole(half_shape), whole(rows)],
        whole(rows),
        pair,
        total,
        near,
        far,
        rows,
    )
    update = update.reshape(owned, members, row_count, order).swapaxes(0, 1)
    returned = exchange(update.reshape(experts, row_count, order))[None]
    shrink = 1.0 - step_rate * decay_rate
    return (shrink * weights.astype(jnp.float32) - step_rate * returned.astype(jnp.float32)).astype(
        jnp.bfloat16
    )


def solution(mesh):
    in_specs = (P("layer", None, "opt", None), P("layer", None, "opt", None))
    out_specs = P("layer", None, "opt", None)
    return jax.shard_map(
        on_device, mesh=mesh, in_specs=in_specs, out_specs=out_specs, check_vma=False
    )
```

```python
import functools

import jax
import jax.numpy as jnp
from jax import lax
from jax.experimental import pallas as pl
from jax.experimental.pallas import tpu as pltpu
from jax.sharding import PartitionSpec as P

ITERS = 3
BLOCK = 128
WIDE = 256
F32_TILE = 8
BF16_TILE = 16
VMEM_BYTES = 48 << 20

first_coef = 3.4445
second_coef = -4.775
third_coef = 2.0315
epsilon = 1e-06
step_rate = 0.5
decay_rate = 0.1

AXES = ("opt", "layer")


def positions(opt, layer):
    rest_count = opt // 8
    spots = [
        (half, z, y, rest, x, pair)
        for half in range(2)
        for z in range(2)
        for y in range(2)
        for rest in range(rest_count)
        for x in range(2)
        for pair in range(2)
    ]

    def device(half, z, y, rest, x, pair):
        return (((half * 2 + z) * 2 + y) * rest_count + rest) * layer + x * 2 + pair

    def swap(flips):
        return [(device(*spot), device(*(value ^ flip for value, flip in zip(spot, flips)))) for spot in spots]

    return {
        "x": swap((0, 0, 0, 0, 1, 0)),
        "y": swap((0, 0, 1, 0, 0, 0)),
        "z": swap((0, 1, 0, 0, 0, 0)),
        "antipode": swap((0, 1, 1, 0, 1, 0)),
        "mirror": swap((1, 1, 0, 0, 0, 0)),
        "pair": swap((0, 0, 0, 0, 0, 1)),
    }


def own_place(rest_count):
    place = lax.axis_index("opt") // rest_count
    across, pair = lax.axis_index("layer") // 2, lax.axis_index("layer") % 2
    half, z, y = place // 4, place // 2 % 2, place % 2
    colour = across ^ (2 * y) ^ (3 * (z ^ half))
    return jnp.stack([colour, pair, across]).astype(jnp.int32)


def call(kernel, out_shape, place, *operands, scratch=()):
    vmem = pl.BlockSpec(memory_space=pltpu.VMEM)
    return pl.pallas_call(
        kernel,
        out_shape=out_shape,
        in_specs=[pl.BlockSpec(memory_space=pltpu.SMEM)] + [vmem] * len(operands),
        out_specs=jax.tree.map(lambda _: vmem, out_shape),
        scratch_shapes=list(scratch),
        compiler_params=pltpu.CompilerParams(vmem_limit_bytes=VMEM_BYTES),
    )(place, *operands)


def product(first, second):
    return jnp.dot(first, second, preferred_element_type=jnp.float32)


def halves_of(order):
    count = order // BLOCK
    folds = [(i, i + 1) for i in range(0, count, 2)]
    others = [(i, j) for i in range(count) for j in range(i + 1, count)]
    middle_fold, middle = len(folds) // 2, len(others) // 2
    return [(folds[:middle_fold], others[:middle]), (folds[middle_fold:], others[middle:])]


def half_blocks(order):
    folds, others = halves_of(order)[0]
    return len(folds), len(folds) + len(others)


def packed_shape(order):
    return jax.ShapeDtypeStruct((2, half_blocks(order)[1] * BLOCK + F32_TILE, BLOCK), jnp.float32)


def message_shape(order):
    return jax.ShapeDtypeStruct((half_blocks(order)[1] * BLOCK + BF16_TILE, BLOCK), jnp.bfloat16)


def grid_ids():
    shape = (BLOCK, BLOCK)
    return lax.broadcasted_iota(jnp.int32, shape, 0), lax.broadcasted_iota(jnp.int32, shape, 1)


def diagonal(block):
    row_ids, column_ids = grid_ids()
    return jnp.sum(jnp.where(row_ids == column_ids, block, 0.0), axis=0, keepdims=True)


def padded(rows, height):
    missing = height - sum(row.shape[0] for row in rows)
    return jnp.concatenate(rows + [jnp.zeros((missing, BLOCK), rows[0].dtype)], axis=0)


def pack(block, order):
    row_ids, column_ids = grid_ids()
    result = []
    for folds, others in halves_of(order):
        tiles, rows = [], []
        for i, j in folds:
            second = block(j, j)
            tiles.append(jnp.where(row_ids <= column_ids, block(i, i), second))
            rows.append(diagonal(second))
        tiles += [block(i, j) for i, j in others]
        result.append(jnp.concatenate(tiles + [padded(rows, F32_TILE)], axis=0))
    return result


def unpack(halves, order):
    row_ids, column_ids = grid_ids()
    blocks = {}
    for (folds, others), half in zip(halves_of(order), halves):
        tiles = [half[k * BLOCK : (k + 1) * BLOCK] for k in range(len(folds) + len(others))]
        tail = half[len(tiles) * BLOCK :]
        for k, (i, j) in enumerate(folds):
            mirrored = tiles[k].T
            blocks[i, i] = jnp.where(row_ids <= column_ids, tiles[k], mirrored)
            second = jnp.where(row_ids > column_ids, tiles[k], mirrored)
            blocks[j, j] = jnp.where(row_ids == column_ids, tail[k : k + 1], second)
        for k, (i, j) in enumerate(others):
            blocks[i, j] = tiles[len(folds) + k]
    return blocks


def to_message(half, order):
    fold_count, block_count = half_blocks(order)
    length = block_count * BLOCK
    body, tail = half[:length], half[length : length + fold_count]
    rounded = body.astype(jnp.bfloat16)
    rows = [
        diagonal(
            body[k * BLOCK : (k + 1) * BLOCK] - rounded[k * BLOCK : (k + 1) * BLOCK].astype(jnp.float32)
        )
        for k in range(fold_count)
    ]
    high = tail.astype(jnp.bfloat16).astype(jnp.float32)
    extra = padded(rows + [high, tail - high], BF16_TILE)
    return jnp.concatenate([rounded, extra.astype(jnp.bfloat16)], axis=0)


def from_message(message, order):
    fold_count, block_count = half_blocks(order)
    length = block_count * BLOCK
    row_ids, column_ids = grid_ids()
    values = message.astype(jnp.float32)
    body, extra = values[:length], values[length:]
    tiles = [
        body[k * BLOCK : (k + 1) * BLOCK] + jnp.where(row_ids == column_ids, extra[k : k + 1], 0.0)
        for k in range(fold_count)
    ]
    tail = extra[fold_count : 2 * fold_count] + extra[2 * fold_count : 3 * fold_count]
    return jnp.concatenate(tiles + [body[fold_count * BLOCK :], padded([tail], F32_TILE)], axis=0)


def deal_kernel(place_ref, momentum_ref, *piece_refs):
    for step, piece_ref in enumerate(piece_refs):
        piece_ref[...] = momentum_ref[place_ref[0] ^ (step + 1)]


def expert_rows(place_ref, momentum_ref, piece_refs, expert):
    count = momentum_ref.shape[1] // 2
    span = pl.ds(pl.multiple_of(expert * count, count), count)
    return [momentum_ref[place_ref[0], span, :]] + [piece_ref[span, :] for piece_ref in piece_refs]


def gram_kernel(place_ref, momentum_ref, x_ref, y_ref, z_ref, kept_ref, sent_ref):
    order = momentum_ref.shape[2]
    pair = place_ref[1]
    for expert, out_ref in ((1 - pair, sent_ref), (pair, kept_ref)):
        rows = jnp.concatenate(expert_rows(place_ref, momentum_ref, (x_ref, y_ref, z_ref), expert), axis=0)
        tiles = {}
        for row in range(0, order, WIDE):
            for column in range(row, order, WIDE):
                tiles[row, column] = lax.dot_general(
                    rows[:, row : row + WIDE],
                    rows[:, column : column + WIDE],
                    (((0,), (0,)), ((), ())),
                    preferred_element_type=jnp.float32,
                )

        def block(i, j):
            row, column = i * BLOCK, j * BLOCK
            tile = tiles[row // WIDE * WIDE, column // WIDE * WIDE]
            return tile[row % WIDE :, column % WIDE :][:BLOCK, :BLOCK]

        for half, value in enumerate(pack(block, order)):
            out_ref[half] = value


def place_sum_kernel(order, place_ref, own_ref, other_ref, sum_ref, message_ref):
    sum_ref[...] = own_ref[...] + other_ref[...]
    message_ref[...] = to_message(sum_ref[1 - place_ref[2]], order)


def cube_sum_kernel(order, place_ref, sum_ref, arrived_ref, half_ref, message_ref):
    half = sum_ref[place_ref[2]] + from_message(arrived_ref[...], order)
    half_ref[...] = half
    message_ref[...] = to_message(half, order)


def total_kernel(order, place_ref, half_ref, arrived_ref, far_ref, total_ref, message_ref):
    total = half_ref[...] + from_message(far_ref[...], order)
    total_ref[...] = total
    message_ref[...] = to_message(total - from_message(arrived_ref[...], order), order)


def split(matrix):
    high = matrix.astype(jnp.bfloat16)
    return high, (matrix - high.astype(jnp.float32)).astype(jnp.bfloat16)


def product_of_split(first, second):
    return product(first[0], second[0]) + (product(first[0], second[1]) + product(first[1], second[0]))


def assemble(upper, count):
    return jnp.concatenate(
        [
            jnp.concatenate([upper[i, j] if i <= j else upper[j, i].T for j in range(count)], axis=1)
            for i in range(count)
        ],
        axis=0,
    )


def split_whole(upper, count):
    parts = {key: split(value) for key, value in upper.items()}
    return tuple(assemble({key: value[part] for key, value in parts.items()}, count) for part in range(2))


def symmetric_product(first, second, count):
    size = first[0].shape[0] // count
    return {
        (i, j): product_of_split(
            tuple(part[i * size : (i + 1) * size, :] for part in first),
            tuple(part[:, j * size : (j + 1) * size] for part in second),
        )
        for i in range(count)
        for j in range(i, count)
    }


def newton(current, count):
    size = current[0, 0].shape[0]
    shape = (size, size)
    identity = lax.broadcasted_iota(jnp.int32, shape, 0) == lax.broadcasted_iota(jnp.int32, shape, 1)
    accum = None
    for iteration in range(ITERS):
        halves = split_whole(current, count)
        squared = symmetric_product(halves, halves, count)
        polynomial = {
            (i, j): (jnp.where(identity, first_coef, 0.0) if i == j else 0.0)
            + second_coef * current[i, j]
            + third_coef * squared[i, j]
            for i, j in current
        }
        poly_halves = split_whole(polynomial, count)
        if accum is None:
            accum = polynomial
        else:
            accum = symmetric_product(split_whole(accum, count), poly_halves, count)
        if iteration + 1 < ITERS:
            inner = symmetric_product(halves, poly_halves, count)
            current = symmetric_product(split_whole(inner, count), poly_halves, count)
    return accum


def factor_kernel(order, scale, place_ref, sum_ref, total_ref, rest_ref, factor_ref):
    kept = place_ref[2]
    total = total_ref[...]
    other = sum_ref[1 - kept] + from_message(rest_ref[...], order)
    halves = [jnp.where(kept == 0, total, other), jnp.where(kept == 0, other, total)]
    blocks = unpack(halves, order)
    trace_row = sum(diagonal(blocks[i, i]) for i in range(order // BLOCK))
    trace_sum = jnp.sum(trace_row)
    count, ratio = order // WIDE, WIDE // BLOCK
    current = {}
    for i in range(count):
        for j in range(i, count):
            tile = jnp.concatenate(
                [
                    jnp.concatenate(
                        [
                            blocks[row, column] if row <= column else blocks[column, row].T
                            for column in range(j * ratio, (j + 1) * ratio)
                        ],
                        axis=1,
                    )
                    for row in range(i * ratio, (i + 1) * ratio)
                ],
                axis=0,
            )
            current[i, j] = tile / (trace_sum + epsilon)
    accum = newton(current, count)
    growth = jnp.sqrt(scale / (trace_sum + epsilon))
    factor_ref[...] = assemble(
        {key: (value * growth).astype(jnp.bfloat16) for key, value in accum.items()}, count
    )


def update_kernel(place_ref, own_ref, other_ref, momentum_ref, x_ref, y_ref, z_ref, *update_refs):
    pair = place_ref[1]
    count = momentum_ref.shape[1] // 2
    for expert, factor_ref in ((pair, own_ref), (1 - pair, other_ref)):
        rows = jnp.concatenate(expert_rows(place_ref, momentum_ref, (x_ref, y_ref, z_ref), expert), axis=0)
        update = product(rows, factor_ref[...]).astype(jnp.bfloat16)
        span = pl.ds(pl.multiple_of(expert * count, count), count)
        for step, update_ref in enumerate(update_refs):
            update_ref[span, :] = update[step * count : (step + 1) * count]


def weights_kernel(place_ref, weights_ref, *refs):
    update_refs, out_ref = refs[:-1], refs[-1]
    shrink = 1.0 - step_rate * decay_rate
    for step, update_ref in enumerate(update_refs):
        colour = place_ref[0] ^ step
        out_ref[colour] = (
            shrink * weights_ref[colour].astype(jnp.float32) - step_rate * update_ref[...].astype(jnp.float32)
        ).astype(out_ref.dtype)


def on_device(momentum, weights):
    order = momentum.shape[3]
    opt, layer = lax.axis_size("opt"), lax.axis_size("layer")
    rest_count = opt // 8
    swaps = positions(opt, layer)
    place = own_place(rest_count)
    rest_groups = [[group * rest_count + rest for rest in range(rest_count)] for group in range(8)]

    def regroup(array, split_axis, concat_axis):
        if rest_count == 1:
            return array
        return lax.all_to_all(
            array,
            "opt",
            split_axis=split_axis,
            concat_axis=concat_axis,
            axis_index_groups=rest_groups,
            tiled=True,
        )

    def move(array, way):
        return lax.ppermute(array, AXES, swaps[way])

    spread = regroup(momentum[0], 0, 1)
    experts, row_count, _ = spread.shape
    by_colour = (experts // 2, 2 * row_count, order)
    spread = spread.reshape(by_colour)
    piece = jax.ShapeDtypeStruct(by_colour[1:], spread.dtype)
    packed, message = packed_shape(order), message_shape(order)
    half = jax.ShapeDtypeStruct(packed.shape[1:], packed.dtype)

    dealt = call(deal_kernel, (piece,) * 3, place, spread)
    arrived = [move(array, way) for array, way in zip(dealt, "xyz")]
    kept, sent = call(gram_kernel, (packed, packed), place, spread, *arrived)
    place_sum, first = call(
        functools.partial(place_sum_kernel, order), (packed, message), place, kept, move(sent, "pair")
    )
    near = move(first, "antipode")
    cube_half, second = call(
        functools.partial(cube_sum_kernel, order), (half, message), place, place_sum, near
    )
    total, third = call(
        functools.partial(total_kernel, order),
        (half, message),
        place,
        cube_half,
        near,
        move(second, "mirror"),
    )
    factor = call(
        functools.partial(factor_kernel, order, float(layer * opt * momentum.shape[2])),
        jax.ShapeDtypeStruct((order, order), jnp.bfloat16),
        place,
        place_sum,
        total,
        move(third, "antipode"),
    )
    updates = call(
        update_kernel, (piece,) * 4, place, factor, move(factor, "pair"), spread, *arrived
    )
    returned = [move(array, way) for array, way in zip(updates[1:], "xyz")]
    fresh = call(
        weights_kernel,
        jax.ShapeDtypeStruct(by_colour, weights.dtype),
        place,
        regroup(weights[0], 0, 1).reshape(by_colour),
        updates[0],
        *returned,
    )
    return regroup(fresh.reshape(experts, row_count, order), 1, 0)[None]


def solution(mesh):
    in_specs = (P("layer", None, "opt", None), P("layer", None, "opt", None))
    out_specs = P("layer", None, "opt", None)
    return jax.shard_map(
        on_device, mesh=mesh, in_specs=in_specs, out_specs=out_specs, check_vma=False
    )
```

```python
import functools
import itertools

import jax
import jax.numpy as jnp
from jax import lax
from jax.experimental import pallas as pl
from jax.experimental.pallas import tpu as pltpu
from jax.sharding import PartitionSpec as P

ITERS = 3
BLOCK = 128
WIDE = 256
F32_TILE = 8
BF16_TILE = 16
VMEM_BYTES = 48 << 20

first_coef = 3.4445
second_coef = -4.775
third_coef = 2.0315
epsilon = 1e-06
step_rate = 0.5
decay_rate = 0.1

AXES = ("opt", "layer")


X, Y, Z = (0, 0, 0, 0, 1, 0), (0, 0, 1, 0, 0, 0), (0, 1, 0, 0, 0, 0)
MIRROR, ANTIPODE, BOTH = (1, 1, 0, 0, 0, 0), (0, 1, 1, 0, 1, 0), (1, 0, 1, 0, 1, 0)
NEIGHBOURS = ((X, Y), (Z, X), (Y, Z))
OWNERS = ((MIRROR, BOTH), (BOTH, MIRROR), (ANTIPODE, ANTIPODE))
PAIR = (((0, 0, 0, 0, 0, 1),) * 2,)


def colour_step(flips):
    return flips[4] ^ 2 * flips[2] ^ 3 * (flips[1] ^ flips[0])


def quarter_step(flips):
    return flips[4] + 2 * flips[0]


def swaps(opt, layer, partners):
    rest_count = opt // 8
    sizes = (2, 2, 2, rest_count, 2, 2)

    def device(half, z, y, rest, x, pair):
        return (((half * 2 + z) * 2 + y) * rest_count + rest) * layer + x * 2 + pair

    return [
        [
            (device(*spot), device(*(value ^ flip for value, flip in zip(spot, flips[spot[5]]))))
            for spot in itertools.product(*map(range, sizes))
        ]
        for flips in partners
    ]


def by_pair(pair, values):
    return values[0] + pair * (values[1] - values[0])


class Place:
    def __init__(self, rest_count):
        index = lax.axis_index("opt") // rest_count
        x, self.pair = lax.axis_index("layer") // 2, lax.axis_index("layer") % 2
        half, z, y = index // 4, index // 2 % 2, index % 2
        self.colour = x ^ (2 * y) ^ (3 * (z ^ half))
        self.quarter = x + 2 * half

    def colour_at(self, step):
        return self.colour ^ by_pair(self.pair, [colour_step(flips) for flips in NEIGHBOURS[step]])

    def quarter_at(self, step):
        return self.quarter ^ by_pair(self.pair, [quarter_step(flips) for flips in OWNERS[step]])


def call(kernel, out_shape, *operands, spaces=None, scratch=()):
    vmem = pl.BlockSpec(memory_space=pltpu.VMEM)
    return pl.pallas_call(
        kernel,
        out_shape=out_shape,
        in_specs=[vmem] * len(operands) if spaces is None else [pl.BlockSpec(memory_space=space) for space in spaces],
        out_specs=jax.tree.map(lambda _: vmem, out_shape),
        scratch_shapes=list(scratch),
        compiler_params=pltpu.CompilerParams(vmem_limit_bytes=VMEM_BYTES),
    )(*operands)


def product(first, second):
    return jnp.dot(first, second, preferred_element_type=jnp.float32)


def quarters_of(order):
    count = order // BLOCK
    folds = [("fold", i, i + 1) for i in range(0, count, 2)]
    others = [("plain", i, j) for i in range(count) for j in range(i + 1, count)]
    length = (len(folds) + len(others)) // 4
    quarters = []
    for quarter in range(4):
        blocks = folds[quarter::4]
        missing = length - len(blocks)
        quarters.append(blocks + others[:missing])
        others = others[missing:]
    return quarters


def quarter_blocks(order):
    quarters = quarters_of(order)
    return max(sum(kind == "fold" for kind, _, _ in blocks) for blocks in quarters), len(quarters[0])


def packed_shape(order):
    return jax.ShapeDtypeStruct((4, quarter_blocks(order)[1] * BLOCK + F32_TILE, BLOCK), jnp.float32)


def message_shape(order):
    return jax.ShapeDtypeStruct((quarter_blocks(order)[1] * BLOCK + BF16_TILE, BLOCK), jnp.bfloat16)


def grid_ids():
    shape = (BLOCK, BLOCK)
    return lax.broadcasted_iota(jnp.int32, shape, 0), lax.broadcasted_iota(jnp.int32, shape, 1)


def diagonal(block):
    row_ids, column_ids = grid_ids()
    return jnp.sum(jnp.where(row_ids == column_ids, block, 0.0), axis=0, keepdims=True)


def padded(rows, height):
    missing = height - sum(row.shape[0] for row in rows)
    return jnp.concatenate(rows + [jnp.zeros((missing, BLOCK), jnp.float32)], axis=0)


def pack(block, order):
    row_ids, column_ids = grid_ids()
    result = []
    for blocks in quarters_of(order):
        tiles, rows = [], []
        for kind, i, j in blocks:
            if kind == "fold":
                second = block(j, j)
                tiles.append(jnp.where(row_ids <= column_ids, block(i, i), second))
                rows.append(diagonal(second))
            else:
                tiles.append(block(i, j))
        result.append(jnp.concatenate(tiles + [padded(rows, F32_TILE)], axis=0))
    return result


def unpack(quarters, order):
    row_ids, column_ids = grid_ids()
    result = {}
    for blocks, quarter in zip(quarters_of(order), quarters):
        tail = quarter[len(blocks) * BLOCK :]
        for k, (kind, i, j) in enumerate(blocks):
            tile = quarter[k * BLOCK : (k + 1) * BLOCK]
            if kind == "fold":
                mirrored = tile.T
                result[i, i] = jnp.where(row_ids <= column_ids, tile, mirrored)
                second = jnp.where(row_ids > column_ids, tile, mirrored)
                result[j, j] = jnp.where(row_ids == column_ids, tail[k : k + 1], second)
            else:
                result[i, j] = tile
    return result


def to_message(quarter, order):
    fold_count, block_count = quarter_blocks(order)
    length = block_count * BLOCK
    body, tail = quarter[:length], quarter[length : length + fold_count]
    rounded = body.astype(jnp.bfloat16)
    rows = [
        diagonal(
            body[k * BLOCK : (k + 1) * BLOCK] - rounded[k * BLOCK : (k + 1) * BLOCK].astype(jnp.float32)
        )
        for k in range(fold_count)
    ]
    high = tail.astype(jnp.bfloat16).astype(jnp.float32)
    extra = padded(rows + [high, tail - high], BF16_TILE)
    return jnp.concatenate([rounded, extra.astype(jnp.bfloat16)], axis=0)


def from_message(message, order):
    fold_count, block_count = quarter_blocks(order)
    length = block_count * BLOCK
    row_ids, column_ids = grid_ids()
    values = message.astype(jnp.float32)
    body, extra = values[:length], values[length:]
    tiles = [
        body[k * BLOCK : (k + 1) * BLOCK] + jnp.where(row_ids == column_ids, extra[k : k + 1], 0.0)
        for k in range(fold_count)
    ]
    tail = extra[fold_count : 2 * fold_count] + extra[2 * fold_count : 3 * fold_count]
    return jnp.concatenate(tiles + [body[fold_count * BLOCK :], padded([tail], F32_TILE)], axis=0)


def deal_kernel(rest_count, momentum_ref, *refs):
    piece_refs, semaphores = refs[:-1], refs[-1]
    place = Place(rest_count)
    copies = []
    for number, piece_ref in enumerate(piece_refs):
        colour = place.colour if number == 0 else place.colour_at(number - 1)
        copies.append(pltpu.make_async_copy(momentum_ref.at[colour], piece_ref, semaphores.at[number]))
    for copy in copies[1:] + copies[:1]:
        copy.start()
    for copy in copies:
        copy.wait()


def expert_rows(piece_refs, expert):
    count = piece_refs[0].shape[0] // 2
    span = pl.ds(pl.multiple_of(expert * count, count), count)
    return jnp.concatenate([piece_ref[span, :] for piece_ref in piece_refs], axis=0)


def gram_kernel(rest_count, *refs):
    piece_refs, (kept_ref, sent_ref) = refs[:4], refs[4:]
    order = piece_refs[0].shape[1]
    pair = Place(rest_count).pair
    for expert, out_ref in ((1 - pair, sent_ref), (pair, kept_ref)):
        rows = expert_rows(piece_refs, expert)
        tiles = {}
        for row in range(0, order, WIDE):
            for column in range(row, order, WIDE):
                tiles[row, column] = lax.dot_general(
                    rows[:, row : row + WIDE],
                    rows[:, column : column + WIDE],
                    (((0,), (0,)), ((), ())),
                    preferred_element_type=jnp.float32,
                )

        def block(i, j):
            row, column = i * BLOCK, j * BLOCK
            tile = tiles[row // WIDE * WIDE, column // WIDE * WIDE]
            return tile[row % WIDE :, column % WIDE :][:BLOCK, :BLOCK]

        for quarter, value in enumerate(pack(block, order)):
            out_ref[quarter] = value


def reduce_kernel(rest_count, order, own_ref, other_ref, sum_ref, *message_refs):
    place = Place(rest_count)
    sum_ref[...] = own_ref[...] + other_ref[...]
    for step, message_ref in enumerate(message_refs):
        message_ref[...] = to_message(sum_ref[place.quarter_at(step)], order)


def gather_kernel(rest_count, order, sum_ref, *refs):
    arrived_refs, total_ref, message_refs = refs[:3], refs[3], refs[4:]
    arrived = [from_message(arrived_ref[...], order) for arrived_ref in arrived_refs]
    total = sum_ref[Place(rest_count).quarter] + (arrived[0] + (arrived[1] + arrived[2]))
    total_ref[...] = total
    for value, message_ref in zip(arrived, message_refs):
        message_ref[...] = to_message(total - value, order)


def split(matrix):
    high = matrix.astype(jnp.bfloat16)
    return high, (matrix - high.astype(jnp.float32)).astype(jnp.bfloat16)


def product_of_split(first, second):
    return product(first[0], second[0]) + (product(first[0], second[1]) + product(first[1], second[0]))


def assemble(upper, count):
    return jnp.concatenate(
        [
            jnp.concatenate([upper[i, j] if i <= j else upper[j, i].T for j in range(count)], axis=1)
            for i in range(count)
        ],
        axis=0,
    )


def split_whole(upper, count):
    parts = {key: split(value) for key, value in upper.items()}
    return tuple(assemble({key: value[part] for key, value in parts.items()}, count) for part in range(2))


def symmetric_product(first, second, count):
    size = first[0].shape[0] // count
    return {
        (i, j): product_of_split(
            tuple(part[i * size : (i + 1) * size, :] for part in first),
            tuple(part[:, j * size : (j + 1) * size] for part in second),
        )
        for i in range(count)
        for j in range(i, count)
    }


def newton(current, count):
    size = current[0, 0].shape[0]
    shape = (size, size)
    identity = lax.broadcasted_iota(jnp.int32, shape, 0) == lax.broadcasted_iota(jnp.int32, shape, 1)
    accum = None
    for iteration in range(ITERS):
        halves = split_whole(current, count)
        squared = symmetric_product(halves, halves, count)
        polynomial = {
            (i, j): (jnp.where(identity, first_coef, 0.0) if i == j else 0.0)
            + second_coef * current[i, j]
            + third_coef * squared[i, j]
            for i, j in current
        }
        poly_halves = split_whole(polynomial, count)
        if accum is None:
            accum = polynomial
        else:
            accum = symmetric_product(split_whole(accum, count), poly_halves, count)
        if iteration + 1 < ITERS:
            inner = symmetric_product(halves, poly_halves, count)
            current = symmetric_product(split_whole(inner, count), poly_halves, count)
    return accum


def factor_kernel(rest_count, order, scale, sum_ref, total_ref, *refs):
    rest_refs, factor_ref, quarters_ref = refs[:3], refs[3], refs[4]
    place = Place(rest_count)
    quarters_ref[place.quarter] = total_ref[...]
    for step, rest_ref in enumerate(rest_refs):
        quarter = place.quarter_at(step)
        quarters_ref[quarter] = sum_ref[quarter] + from_message(rest_ref[...], order)
    blocks = unpack([quarters_ref[quarter] for quarter in range(4)], order)
    trace_sum = jnp.sum(sum(diagonal(blocks[i, i]) for i in range(order // BLOCK)))
    count, ratio = order // WIDE, WIDE // BLOCK
    current = {}
    for i in range(count):
        for j in range(i, count):
            tile = jnp.concatenate(
                [
                    jnp.concatenate(
                        [
                            blocks[row, column] if row <= column else blocks[column, row].T
                            for column in range(j * ratio, (j + 1) * ratio)
                        ],
                        axis=1,
                    )
                    for row in range(i * ratio, (i + 1) * ratio)
                ],
                axis=0,
            )
            current[i, j] = tile / (trace_sum + epsilon)
    accum = newton(current, count)
    growth = jnp.sqrt(scale / (trace_sum + epsilon))
    factor_ref[...] = assemble(
        {key: (value * growth).astype(jnp.bfloat16) for key, value in accum.items()}, count
    )


def update_kernel(rest_count, own_ref, other_ref, *refs):
    piece_refs, update_refs = refs[:4], refs[4:]
    pair = Place(rest_count).pair
    count = piece_refs[0].shape[0] // 2
    for expert, factor_ref in ((pair, own_ref), (1 - pair, other_ref)):
        update = product(expert_rows(piece_refs, expert), factor_ref[...]).astype(jnp.bfloat16)
        span = pl.ds(pl.multiple_of(expert * count, count), count)
        for number, update_ref in enumerate(update_refs):
            update_ref[span, :] = update[number * count : (number + 1) * count]


def weights_kernel(rest_count, weights_ref, *refs):
    update_refs, out_ref = refs[:4], refs[4]
    place = Place(rest_count)
    shrink = 1.0 - step_rate * decay_rate
    for number, update_ref in enumerate(update_refs):
        colour = place.colour if number == 0 else place.colour_at(number - 1)
        out_ref[colour] = (
            shrink * weights_ref[colour].astype(jnp.float32) - step_rate * update_ref[...].astype(jnp.float32)
        ).astype(out_ref.dtype)


def on_device(momentum, weights):
    order = momentum.shape[3]
    opt, layer = lax.axis_size("opt"), lax.axis_size("layer")
    rest_count = opt // 8
    rest_groups = [[group * rest_count + rest for rest in range(rest_count)] for group in range(8)]
    scale = float(layer * opt * momentum.shape[2])

    def regroup(array, split_axis, concat_axis):
        if rest_count == 1:
            return array
        return lax.all_to_all(
            array,
            "opt",
            split_axis=split_axis,
            concat_axis=concat_axis,
            axis_index_groups=rest_groups,
            tiled=True,
        )

    def swap(arrays, partners):
        return [lax.ppermute(array, AXES, perm) for array, perm in zip(arrays, swaps(opt, layer, partners))]

    spread = regroup(momentum[0], 0, 1)
    experts, row_count, _ = spread.shape
    by_colour = (experts // 2, 2 * row_count, order)
    piece = jax.ShapeDtypeStruct(by_colour[1:], spread.dtype)
    packed, message = packed_shape(order), message_shape(order)
    quarter = jax.ShapeDtypeStruct(packed.shape[1:], packed.dtype)

    own, *dealt = call(
        functools.partial(deal_kernel, rest_count),
        (piece,) * 4,
        spread.reshape(by_colour),
        spaces=[pltpu.HBM],
        scratch=[pltpu.SemaphoreType.DMA((4,))],
    )
    pieces = [own] + swap(dealt, NEIGHBOURS)
    kept, sent = call(functools.partial(gram_kernel, rest_count), (packed, packed), *pieces)
    place_sum, *parts = call(
        functools.partial(reduce_kernel, rest_count, order),
        (packed,) + (message,) * 3,
        kept,
        *swap([sent], PAIR),
    )
    total, *rests = call(
        functools.partial(gather_kernel, rest_count, order),
        (quarter,) + (message,) * 3,
        place_sum,
        *swap(parts, OWNERS),
    )
    factor = call(
        functools.partial(factor_kernel, rest_count, order, scale),
        jax.ShapeDtypeStruct((order, order), jnp.bfloat16),
        place_sum,
        total,
        *swap(rests, OWNERS),
        scratch=[pltpu.VMEM(packed.shape, packed.dtype)],
    )
    own_update, *updates = call(
        functools.partial(update_kernel, rest_count),
        (piece,) * 4,
        factor,
        *swap([factor], PAIR),
        *pieces,
    )
    fresh = call(
        functools.partial(weights_kernel, rest_count),
        jax.ShapeDtypeStruct(by_colour, weights.dtype),
        regroup(weights[0], 0, 1).reshape(by_colour),
        own_update,
        *swap(updates, NEIGHBOURS),
    )
    return regroup(fresh.reshape(experts, row_count, order), 1, 0)[None]


def solution(mesh):
    in_specs = (P("layer", None, "opt", None), P("layer", None, "opt", None))
    out_specs = P("layer", None, "opt", None)
    return jax.shard_map(
        on_device, mesh=mesh, in_specs=in_specs, out_specs=out_specs, check_vma=False
    )
```

```python
import functools
import itertools

import jax
import jax.numpy as jnp
from jax import lax
from jax.experimental import pallas as pl
from jax.experimental.pallas import tpu as pltpu
from jax.sharding import PartitionSpec as P

ITERS = 3
BLOCK = 128
WIDE = 256
F32_TILE = 8
BF16_TILE = 16
VMEM_BYTES = 48 << 20

first_coef = 3.4445
second_coef = -4.775
third_coef = 2.0315
epsilon = 1e-06
step_rate = 0.5
decay_rate = 0.1

AXES = ("opt", "layer")


def flips_of(z, y, x, pair=0, half=0):
    return (half, z, y, 0, x, pair)


def neighbour_steps():
    ways = [(0, 0, 1), (0, 1, 0), (1, 0, 0)]
    order = [(ways[step], ways[(step + 1) % 3]) for step in range(3)]
    return [tuple(flips_of(*way, pair=cross) for way in step) for cross in range(2) for step in order]


ROWS = neighbour_steps() + [(flips_of(0, 0, 0, pair=1),) * 2]
OWNERS = [(flips,) * 2 for flips in (flips_of(1, 0, 0, half=1), flips_of(0, 1, 1, half=1), flips_of(1, 1, 1))]


def colour_step(flips):
    return flips[4] ^ 2 * flips[2] ^ 3 * (flips[1] ^ flips[0])


def quarter_step(flips):
    return flips[4] + 2 * flips[0]


def swaps(opt, layer, partners):
    rest_count = opt // 8
    sizes = (2, 2, 2, rest_count, 2, 2)

    def device(half, z, y, rest, x, pair):
        return (((half * 2 + z) * 2 + y) * rest_count + rest) * layer + x * 2 + pair

    return [
        [
            (device(*spot), device(*(value ^ flip for value, flip in zip(spot, flips[spot[5]]))))
            for spot in itertools.product(*map(range, sizes))
        ]
        for flips in partners
    ]


def by_pair(pair, values):
    return values[0] + pair * (values[1] - values[0])


class Place:
    def __init__(self, rest_count):
        index = lax.axis_index("opt") // rest_count
        x, self.pair = lax.axis_index("layer") // 2, lax.axis_index("layer") % 2
        half, z, y = index // 4, index // 2 % 2, index % 2
        self.colour = x ^ (2 * y) ^ (3 * (z ^ half))
        self.quarter = x + 2 * half

    def block(self, number):
        if number == 0:
            return self.colour, self.pair
        flips = ROWS[number - 1]
        return self.colour ^ by_pair(self.pair, [colour_step(way) for way in flips]), self.pair ^ flips[0][5]

    def quarter_at(self, step):
        return self.quarter ^ by_pair(self.pair, [quarter_step(flips) for flips in OWNERS[step]])


def call(kernel, out_shape, *operands, spaces=None, scratch=()):
    vmem = pl.BlockSpec(memory_space=pltpu.VMEM)
    return pl.pallas_call(
        kernel,
        out_shape=out_shape,
        in_specs=[vmem] * len(operands) if spaces is None else [pl.BlockSpec(memory_space=space) for space in spaces],
        out_specs=jax.tree.map(lambda _: vmem, out_shape),
        scratch_shapes=list(scratch),
        compiler_params=pltpu.CompilerParams(vmem_limit_bytes=VMEM_BYTES),
    )(*operands)


def product(first, second):
    return jnp.dot(first, second, preferred_element_type=jnp.float32)


def quarters_of(order):
    count = order // BLOCK
    folds = [("fold", i, i + 1) for i in range(0, count, 2)]
    others = [("plain", i, j) for i in range(count) for j in range(i + 1, count)]
    length = (len(folds) + len(others)) // 4
    quarters = []
    for quarter in range(4):
        blocks = folds[quarter::4]
        missing = length - len(blocks)
        quarters.append(blocks + others[:missing])
        others = others[missing:]
    return quarters


def quarter_blocks(order):
    quarters = quarters_of(order)
    return max(sum(kind == "fold" for kind, _, _ in blocks) for blocks in quarters), len(quarters[0])


def packed_shape(order):
    return jax.ShapeDtypeStruct((4, quarter_blocks(order)[1] * BLOCK + F32_TILE, BLOCK), jnp.float32)


def message_shape(order):
    return jax.ShapeDtypeStruct((quarter_blocks(order)[1] * BLOCK + BF16_TILE, BLOCK), jnp.bfloat16)


def grid_ids():
    shape = (BLOCK, BLOCK)
    return lax.broadcasted_iota(jnp.int32, shape, 0), lax.broadcasted_iota(jnp.int32, shape, 1)


def diagonal(block):
    row_ids, column_ids = grid_ids()
    return jnp.sum(jnp.where(row_ids == column_ids, block, 0.0), axis=0, keepdims=True)


def padded(rows, height):
    missing = height - sum(row.shape[0] for row in rows)
    return jnp.concatenate(rows + [jnp.zeros((missing, BLOCK), jnp.float32)], axis=0)


def pack(block, order):
    row_ids, column_ids = grid_ids()
    result = []
    for blocks in quarters_of(order):
        tiles, rows = [], []
        for kind, i, j in blocks:
            if kind == "fold":
                second = block(j, j)
                tiles.append(jnp.where(row_ids <= column_ids, block(i, i), second))
                rows.append(diagonal(second))
            else:
                tiles.append(block(i, j))
        result.append(jnp.concatenate(tiles + [padded(rows, F32_TILE)], axis=0))
    return result


def unpack(quarters, order):
    row_ids, column_ids = grid_ids()
    result = {}
    for blocks, quarter in zip(quarters_of(order), quarters):
        tail = quarter[len(blocks) * BLOCK :]
        for k, (kind, i, j) in enumerate(blocks):
            tile = quarter[k * BLOCK : (k + 1) * BLOCK]
            if kind == "fold":
                mirrored = tile.T
                result[i, i] = jnp.where(row_ids <= column_ids, tile, mirrored)
                second = jnp.where(row_ids > column_ids, tile, mirrored)
                result[j, j] = jnp.where(row_ids == column_ids, tail[k : k + 1], second)
            else:
                result[i, j] = tile
    return result


def to_message(quarter, order):
    fold_count, block_count = quarter_blocks(order)
    length = block_count * BLOCK
    body, tail = quarter[:length], quarter[length : length + fold_count]
    rounded = body.astype(jnp.bfloat16)
    rows = [
        diagonal(
            body[k * BLOCK : (k + 1) * BLOCK] - rounded[k * BLOCK : (k + 1) * BLOCK].astype(jnp.float32)
        )
        for k in range(fold_count)
    ]
    high = tail.astype(jnp.bfloat16).astype(jnp.float32)
    extra = padded(rows + [high, tail - high], BF16_TILE)
    return jnp.concatenate([rounded, extra.astype(jnp.bfloat16)], axis=0)


def from_message(message, order):
    fold_count, block_count = quarter_blocks(order)
    length = block_count * BLOCK
    row_ids, column_ids = grid_ids()
    values = message.astype(jnp.float32)
    body, extra = values[:length], values[length:]
    tiles = [
        body[k * BLOCK : (k + 1) * BLOCK] + jnp.where(row_ids == column_ids, extra[k : k + 1], 0.0)
        for k in range(fold_count)
    ]
    tail = extra[fold_count : 2 * fold_count] + extra[2 * fold_count : 3 * fold_count]
    return jnp.concatenate(tiles + [body[fold_count * BLOCK :], padded([tail], F32_TILE)], axis=0)


def deal_kernel(rest_count, momentum_ref, *refs):
    place = Place(rest_count)
    for number, block_ref in enumerate(refs):
        block_ref[...] = momentum_ref[place.block(number)]


def gram_kernel(*refs):
    rows = jnp.concatenate([block_ref[...] for block_ref in refs[:-1]], axis=0)
    packed_ref = refs[-1]
    order = rows.shape[1]
    tiles = {}
    for row in range(0, order, WIDE):
        for column in range(row, order, WIDE):
            tiles[row, column] = lax.dot_general(
                rows[:, row : row + WIDE],
                rows[:, column : column + WIDE],
                (((0,), (0,)), ((), ())),
                preferred_element_type=jnp.float32,
            )

    def block(i, j):
        row, column = i * BLOCK, j * BLOCK
        tile = tiles[row // WIDE * WIDE, column // WIDE * WIDE]
        return tile[row % WIDE :, column % WIDE :][:BLOCK, :BLOCK]

    for quarter, value in enumerate(pack(block, order)):
        packed_ref[quarter] = value


def reduce_kernel(rest_count, order, sum_ref, *message_refs):
    place = Place(rest_count)
    for step, message_ref in enumerate(message_refs):
        message_ref[...] = to_message(sum_ref[place.quarter_at(step)], order)


def gather_kernel(rest_count, order, sum_ref, *refs):
    arrived_refs, total_ref, message_refs = refs[:3], refs[3], refs[4:]
    arrived = [from_message(arrived_ref[...], order) for arrived_ref in arrived_refs]
    total = sum_ref[Place(rest_count).quarter] + (arrived[0] + (arrived[1] + arrived[2]))
    total_ref[...] = total
    for value, message_ref in zip(arrived, message_refs):
        message_ref[...] = to_message(total - value, order)


def split(matrix):
    high = matrix.astype(jnp.bfloat16)
    return high, (matrix - high.astype(jnp.float32)).astype(jnp.bfloat16)


def product_of_split(first, second):
    return product(first[0], second[0]) + (product(first[0], second[1]) + product(first[1], second[0]))


def assemble(upper, count):
    return jnp.concatenate(
        [
            jnp.concatenate([upper[i, j] if i <= j else upper[j, i].T for j in range(count)], axis=1)
            for i in range(count)
        ],
        axis=0,
    )


def split_whole(upper, count):
    parts = {key: split(value) for key, value in upper.items()}
    return tuple(assemble({key: value[part] for key, value in parts.items()}, count) for part in range(2))


def symmetric_product(first, second, count):
    size = first[0].shape[0] // count
    return {
        (i, j): product_of_split(
            tuple(part[i * size : (i + 1) * size, :] for part in first),
            tuple(part[:, j * size : (j + 1) * size] for part in second),
        )
        for i in range(count)
        for j in range(i, count)
    }


def newton(current, count):
    size = current[0, 0].shape[0]
    shape = (size, size)
    identity = lax.broadcasted_iota(jnp.int32, shape, 0) == lax.broadcasted_iota(jnp.int32, shape, 1)
    accum = None
    for iteration in range(ITERS):
        halves = split_whole(current, count)
        squared = symmetric_product(halves, halves, count)
        polynomial = {
            (i, j): (jnp.where(identity, first_coef, 0.0) if i == j else 0.0)
            + second_coef * current[i, j]
            + third_coef * squared[i, j]
            for i, j in current
        }
        poly_halves = split_whole(polynomial, count)
        if accum is None:
            accum = polynomial
        else:
            accum = symmetric_product(split_whole(accum, count), poly_halves, count)
        if iteration + 1 < ITERS:
            inner = symmetric_product(halves, poly_halves, count)
            current = symmetric_product(split_whole(inner, count), poly_halves, count)
    return accum


def factor_kernel(rest_count, order, scale, sum_ref, total_ref, *refs):
    rest_refs, factor_ref, quarters_ref = refs[:3], refs[3], refs[4]
    place = Place(rest_count)
    quarters_ref[place.quarter] = total_ref[...]
    for step, rest_ref in enumerate(rest_refs):
        quarter = place.quarter_at(step)
        quarters_ref[quarter] = sum_ref[quarter] + from_message(rest_ref[...], order)
    blocks = unpack([quarters_ref[quarter] for quarter in range(4)], order)
    trace_sum = jnp.sum(sum(diagonal(blocks[i, i]) for i in range(order // BLOCK)))
    count, ratio = order // WIDE, WIDE // BLOCK
    current = {}
    for i in range(count):
        for j in range(i, count):
            tile = jnp.concatenate(
                [
                    jnp.concatenate(
                        [
                            blocks[row, column] if row <= column else blocks[column, row].T
                            for column in range(j * ratio, (j + 1) * ratio)
                        ],
                        axis=1,
                    )
                    for row in range(i * ratio, (i + 1) * ratio)
                ],
                axis=0,
            )
            current[i, j] = tile / (trace_sum + epsilon)
    accum = newton(current, count)
    growth = jnp.sqrt(scale / (trace_sum + epsilon))
    factor_ref[...] = assemble(
        {key: (value * growth).astype(jnp.bfloat16) for key, value in accum.items()}, count
    )


def update_kernel(factor_ref, *refs):
    block_refs, update_refs = refs[: len(refs) // 2], refs[len(refs) // 2 :]
    update = product(jnp.concatenate([block_ref[...] for block_ref in block_refs], axis=0), factor_ref[...])
    count = block_refs[0].shape[0]
    for number, update_ref in enumerate(update_refs):
        update_ref[...] = update[number * count : (number + 1) * count].astype(update_ref.dtype)


def weights_kernel(rest_count, weights_ref, *refs):
    update_refs, out_ref = refs[:-1], refs[-1]
    place = Place(rest_count)
    shrink = 1.0 - step_rate * decay_rate
    for number, update_ref in enumerate(update_refs):
        block = place.block(number)
        out_ref[block] = (
            shrink * weights_ref[block].astype(jnp.float32) - step_rate * update_ref[...].astype(jnp.float32)
        ).astype(out_ref.dtype)


def on_device(momentum, weights):
    order = momentum.shape[3]
    opt, layer = lax.axis_size("opt"), lax.axis_size("layer")
    rest_count = opt // 8
    rest_groups = [[group * rest_count + rest for rest in range(rest_count)] for group in range(8)]
    scale = float(layer * opt * momentum.shape[2])

    def regroup(array, split_axis, concat_axis):
        if rest_count == 1:
            return array
        return lax.all_to_all(
            array,
            "opt",
            split_axis=split_axis,
            concat_axis=concat_axis,
            axis_index_groups=rest_groups,
            tiled=True,
        )

    def swap(arrays, partners, back=False):
        permutes = swaps(opt, layer, partners)
        if back:
            permutes = [[(target, source) for source, target in permute] for permute in permutes]
        return [lax.ppermute(array, AXES, permute) for array, permute in zip(arrays, permutes)]

    spread = regroup(momentum[0], 0, 1)
    experts, row_count, _ = spread.shape
    by_block = (experts // 2, 2, row_count, order)
    blocks = (jax.ShapeDtypeStruct(by_block[2:], spread.dtype),) * (1 + len(ROWS))
    packed, message = packed_shape(order), message_shape(order)
    quarter = jax.ShapeDtypeStruct(packed.shape[1:], packed.dtype)

    own, *dealt = call(
        functools.partial(deal_kernel, rest_count),
        blocks,
        spread.reshape(by_block),
    )
    rows = [own] + swap(dealt, ROWS)
    place_sum = call(gram_kernel, packed, *rows)
    parts = call(functools.partial(reduce_kernel, rest_count, order), (message,) * 3, place_sum)
    total, *rests = call(
        functools.partial(gather_kernel, rest_count, order),
        (quarter,) + (message,) * 3,
        place_sum,
        *swap(parts, OWNERS),
    )
    factor = call(
        functools.partial(factor_kernel, rest_count, order, scale),
        jax.ShapeDtypeStruct((order, order), jnp.bfloat16),
        place_sum,
        total,
        *swap(rests, OWNERS),
        scratch=[pltpu.VMEM(packed.shape, packed.dtype)],
    )
    own_update, *updates = call(update_kernel, blocks, factor, *rows)
    fresh = call(
        functools.partial(weights_kernel, rest_count),
        jax.ShapeDtypeStruct(by_block, weights.dtype),
        regroup(weights[0], 0, 1).reshape(by_block),
        own_update,
        *swap(updates, ROWS, back=True),
    )
    return regroup(fresh.reshape(experts, row_count, order), 1, 0)[None]


def solution(mesh):
    in_specs = (P("layer", None, "opt", None), P("layer", None, "opt", None))
    out_specs = P("layer", None, "opt", None)
    return jax.shard_map(
        on_device, mesh=mesh, in_specs=in_specs, out_specs=out_specs, check_vma=False
    )
```

```python
import functools
import itertools

import jax
import jax.numpy as jnp
from jax import lax
from jax.experimental import pallas as pl
from jax.experimental.pallas import tpu as pltpu
from jax.sharding import PartitionSpec as P

ITERS = 3
BLOCK = 128
WIDE = 256
F32_TILE = 8
BF16_TILE = 16
VMEM_BYTES = 48 << 20
EARLY = 5

first_coef = 3.4445
second_coef = -4.775
third_coef = 2.0315
epsilon = 1e-06
step_rate = 0.5
decay_rate = 0.1

AXES = ("opt", "layer")


def flips_of(z, y, x, pair=0, half=0):
    return (half, z, y, 0, x, pair)


def neighbour_steps():
    ways = [(0, 0, 1), (0, 1, 0), (1, 0, 0)]
    order = [(ways[step], ways[(step + 1) % 3]) for step in range(3)]
    return [tuple(flips_of(*way, pair=cross) for way in step) for cross in (1, 0) for step in order]


ROWS = neighbour_steps() + [(flips_of(0, 0, 0, pair=1),) * 2]
OWNERS = [(flips,) * 2 for flips in (flips_of(1, 0, 0, half=1), flips_of(0, 1, 1, half=1), flips_of(1, 1, 1))]


def colour_step(flips):
    return flips[4] ^ 2 * flips[2] ^ 3 * (flips[1] ^ flips[0])


def quarter_step(flips):
    return flips[4] + 2 * flips[0]


def swaps(opt, layer, partners):
    rest_count = opt // 8
    sizes = (2, 2, 2, rest_count, 2, 2)

    def device(half, z, y, rest, x, pair):
        return (((half * 2 + z) * 2 + y) * rest_count + rest) * layer + x * 2 + pair

    return [
        [
            (device(*spot), device(*(value ^ flip for value, flip in zip(spot, flips[spot[5]]))))
            for spot in itertools.product(*map(range, sizes))
        ]
        for flips in partners
    ]


def by_pair(pair, values):
    return values[0] + pair * (values[1] - values[0])


class Place:
    def __init__(self, rest_count):
        index = lax.axis_index("opt") // rest_count
        x, self.pair = lax.axis_index("layer") // 2, lax.axis_index("layer") % 2
        half, z, y = index // 4, index // 2 % 2, index % 2
        self.colour = x ^ (2 * y) ^ (3 * (z ^ half))
        self.quarter = x + 2 * half

    def block(self, number):
        if number == 0:
            return self.colour, self.pair
        flips = ROWS[number - 1]
        return self.colour ^ by_pair(self.pair, [colour_step(way) for way in flips]), self.pair ^ flips[0][5]

    def quarter_at(self, step):
        return self.quarter ^ by_pair(self.pair, [quarter_step(flips) for flips in OWNERS[step]])


def call(kernel, out_shape, *operands, scratch=()):
    vmem = pl.BlockSpec(memory_space=pltpu.VMEM)
    return pl.pallas_call(
        kernel,
        out_shape=out_shape,
        in_specs=[vmem] * len(operands),
        out_specs=jax.tree.map(lambda _: vmem, out_shape),
        scratch_shapes=list(scratch),
        compiler_params=pltpu.CompilerParams(vmem_limit_bytes=VMEM_BYTES),
    )(*operands)


def product(first, second):
    return jnp.dot(first, second, preferred_element_type=jnp.float32)


def quarters_of(order):
    count = order // BLOCK
    folds = [("fold", i, i + 1) for i in range(0, count, 2)]
    others = [("plain", i, j) for i in range(count) for j in range(i + 1, count)]
    length = (len(folds) + len(others)) // 4
    quarters = []
    for quarter in range(4):
        blocks = folds[quarter::4]
        missing = length - len(blocks)
        quarters.append(blocks + others[:missing])
        others = others[missing:]
    return quarters


def quarter_blocks(order):
    quarters = quarters_of(order)
    return max(sum(kind == "fold" for kind, _, _ in blocks) for blocks in quarters), len(quarters[0])


def packed_shape(order):
    return jax.ShapeDtypeStruct((4, quarter_blocks(order)[1] * BLOCK + F32_TILE, BLOCK), jnp.float32)


def message_shape(order):
    return jax.ShapeDtypeStruct((quarter_blocks(order)[1] * BLOCK + BF16_TILE, BLOCK), jnp.bfloat16)


def grid_ids():
    shape = (BLOCK, BLOCK)
    return lax.broadcasted_iota(jnp.int32, shape, 0), lax.broadcasted_iota(jnp.int32, shape, 1)


def diagonal(block):
    row_ids, column_ids = grid_ids()
    return jnp.sum(jnp.where(row_ids == column_ids, block, 0.0), axis=0, keepdims=True)


def padded(rows, height):
    missing = height - sum(row.shape[0] for row in rows)
    return jnp.concatenate(rows + [jnp.zeros((missing, BLOCK), jnp.float32)], axis=0)


def pack(block, order):
    row_ids, column_ids = grid_ids()
    result = []
    for blocks in quarters_of(order):
        tiles, rows = [], []
        for kind, i, j in blocks:
            if kind == "fold":
                second = block(j, j)
                tiles.append(jnp.where(row_ids <= column_ids, block(i, i), second))
                rows.append(diagonal(second))
            else:
                tiles.append(block(i, j))
        result.append(jnp.concatenate(tiles + [padded(rows, F32_TILE)], axis=0))
    return result


def unpack(quarters, order):
    row_ids, column_ids = grid_ids()
    result = {}
    for blocks, quarter in zip(quarters_of(order), quarters):
        tail = quarter[len(blocks) * BLOCK :]
        for k, (kind, i, j) in enumerate(blocks):
            tile = quarter[k * BLOCK : (k + 1) * BLOCK]
            if kind == "fold":
                mirrored = tile.T
                result[i, i] = jnp.where(row_ids <= column_ids, tile, mirrored)
                second = jnp.where(row_ids > column_ids, tile, mirrored)
                result[j, j] = jnp.where(row_ids == column_ids, tail[k : k + 1], second)
            else:
                result[i, j] = tile
    return result


def to_message(quarter, order):
    fold_count, block_count = quarter_blocks(order)
    length = block_count * BLOCK
    body, tail = quarter[:length], quarter[length : length + fold_count]
    rounded = body.astype(jnp.bfloat16)
    rows = [
        diagonal(
            body[k * BLOCK : (k + 1) * BLOCK] - rounded[k * BLOCK : (k + 1) * BLOCK].astype(jnp.float32)
        )
        for k in range(fold_count)
    ]
    high = tail.astype(jnp.bfloat16).astype(jnp.float32)
    extra = padded(rows + [high, tail - high], BF16_TILE)
    return jnp.concatenate([rounded, extra.astype(jnp.bfloat16)], axis=0)


def from_message(message, order):
    fold_count, block_count = quarter_blocks(order)
    length = block_count * BLOCK
    row_ids, column_ids = grid_ids()
    values = message.astype(jnp.float32)
    body, extra = values[:length], values[length:]
    tiles = [
        body[k * BLOCK : (k + 1) * BLOCK] + jnp.where(row_ids == column_ids, extra[k : k + 1], 0.0)
        for k in range(fold_count)
    ]
    tail = extra[fold_count : 2 * fold_count] + extra[2 * fold_count : 3 * fold_count]
    return jnp.concatenate(tiles + [body[fold_count * BLOCK :], padded([tail], F32_TILE)], axis=0)


def deal_kernel(rest_count, momentum_ref, *refs):
    place = Place(rest_count)
    for number, block_ref in enumerate(refs):
        block_ref[...] = momentum_ref[place.block(number)]


def packed_gram(block_refs):
    rows = jnp.concatenate([block_ref[...] for block_ref in block_refs], axis=0)
    order = rows.shape[1]
    tiles = {}
    for row in range(0, order, WIDE):
        for column in range(row, order, WIDE):
            tiles[row, column] = lax.dot_general(
                rows[:, row : row + WIDE],
                rows[:, column : column + WIDE],
                (((0,), (0,)), ((), ())),
                preferred_element_type=jnp.float32,
            )

    def block(i, j):
        row, column = i * BLOCK, j * BLOCK
        tile = tiles[row // WIDE * WIDE, column // WIDE * WIDE]
        return tile[row % WIDE :, column % WIDE :][:BLOCK, :BLOCK]

    return pack(block, order)


def early_gram_kernel(*refs):
    for quarter, value in enumerate(packed_gram(refs[:-1])):
        refs[-1][quarter] = value


def gram_kernel(early_ref, *refs):
    for quarter, value in enumerate(packed_gram(refs[:-1])):
        refs[-1][quarter] = early_ref[quarter] + value


def reduce_kernel(rest_count, order, sum_ref, *message_refs):
    place = Place(rest_count)
    for step, message_ref in enumerate(message_refs):
        message_ref[...] = to_message(sum_ref[place.quarter_at(step)], order)


def gather_kernel(rest_count, order, sum_ref, *refs):
    arrived_refs, total_ref, message_refs = refs[:3], refs[3], refs[4:]
    arrived = [from_message(arrived_ref[...], order) for arrived_ref in arrived_refs]
    total = sum_ref[Place(rest_count).quarter] + (arrived[0] + (arrived[1] + arrived[2]))
    total_ref[...] = total
    for value, message_ref in zip(arrived, message_refs):
        message_ref[...] = to_message(total - value, order)


def split(matrix):
    high = matrix.astype(jnp.bfloat16)
    return high, (matrix - high.astype(jnp.float32)).astype(jnp.bfloat16)


def product_of_split(first, second):
    return product(first[0], second[0]) + (product(first[0], second[1]) + product(first[1], second[0]))


def assemble(upper, count):
    return jnp.concatenate(
        [
            jnp.concatenate([upper[i, j] if i <= j else upper[j, i].T for j in range(count)], axis=1)
            for i in range(count)
        ],
        axis=0,
    )


def split_whole(upper, count):
    parts = {key: split(value) for key, value in upper.items()}
    return tuple(assemble({key: value[part] for key, value in parts.items()}, count) for part in range(2))


def symmetric_product(first, second, count):
    size = first[0].shape[0] // count
    return {
        (i, j): product_of_split(
            tuple(part[i * size : (i + 1) * size, :] for part in first),
            tuple(part[:, j * size : (j + 1) * size] for part in second),
        )
        for i in range(count)
        for j in range(i, count)
    }


def newton(current, count):
    size = current[0, 0].shape[0]
    shape = (size, size)
    identity = lax.broadcasted_iota(jnp.int32, shape, 0) == lax.broadcasted_iota(jnp.int32, shape, 1)
    accum = None
    for iteration in range(ITERS):
        halves = split_whole(current, count)
        squared = symmetric_product(halves, halves, count)
        polynomial = {
            (i, j): (jnp.where(identity, first_coef, 0.0) if i == j else 0.0)
            + second_coef * current[i, j]
            + third_coef * squared[i, j]
            for i, j in current
        }
        poly_halves = split_whole(polynomial, count)
        if accum is None:
            accum = polynomial
        else:
            accum = symmetric_product(split_whole(accum, count), poly_halves, count)
        if iteration + 1 < ITERS:
            inner = symmetric_product(halves, poly_halves, count)
            current = symmetric_product(split_whole(inner, count), poly_halves, count)
    return accum


def factor_kernel(rest_count, order, scale, sum_ref, total_ref, *refs):
    rest_refs, factor_ref, quarters_ref = refs[:3], refs[3], refs[4]
    place = Place(rest_count)
    quarters_ref[place.quarter] = total_ref[...]
    for step, rest_ref in enumerate(rest_refs):
        quarter = place.quarter_at(step)
        quarters_ref[quarter] = sum_ref[quarter] + from_message(rest_ref[...], order)
    blocks = unpack([quarters_ref[quarter] for quarter in range(4)], order)
    trace_sum = jnp.sum(sum(diagonal(blocks[i, i]) for i in range(order // BLOCK)))
    count, ratio = order // WIDE, WIDE // BLOCK
    current = {}
    for i in range(count):
        for j in range(i, count):
            tile = jnp.concatenate(
                [
                    jnp.concatenate(
                        [
                            blocks[row, column] if row <= column else blocks[column, row].T
                            for column in range(j * ratio, (j + 1) * ratio)
                        ],
                        axis=1,
                    )
                    for row in range(i * ratio, (i + 1) * ratio)
                ],
                axis=0,
            )
            current[i, j] = tile / (trace_sum + epsilon)
    accum = newton(current, count)
    growth = jnp.sqrt(scale / (trace_sum + epsilon))
    factor_ref[...] = assemble(
        {key: (value * growth).astype(jnp.bfloat16) for key, value in accum.items()}, count
    )


def update_kernel(factor_ref, *refs):
    block_refs, update_refs = refs[: len(refs) // 2], refs[len(refs) // 2 :]
    update = product(jnp.concatenate([block_ref[...] for block_ref in block_refs], axis=0), factor_ref[...])
    count = block_refs[0].shape[0]
    for number, update_ref in enumerate(update_refs):
        update_ref[...] = update[number * count : (number + 1) * count].astype(update_ref.dtype)


def weights_kernel(rest_count, numbers, weights_ref, *refs):
    out_ref, fresh_ref, semaphores = refs[-3:]
    place = Place(rest_count)
    shrink = 1.0 - step_rate * decay_rate
    copies = []
    for slot, (number, update_ref) in enumerate(zip(numbers, refs)):
        block = place.block(number)
        fresh_ref[slot] = (
            shrink * weights_ref[block].astype(jnp.float32) - step_rate * update_ref[...].astype(jnp.float32)
        ).astype(fresh_ref.dtype)
        copies.append(pltpu.make_async_copy(fresh_ref.at[slot], out_ref.at[block], semaphores.at[slot]))
        copies[-1].start()
    for copy in copies:
        copy.wait()


def new_weights(rest_count, numbers, weights, updates, so_far=None):
    vmem, whole = pl.BlockSpec(memory_space=pltpu.VMEM), pl.BlockSpec(memory_space=pltpu.HBM)
    operands = [weights, *updates] + ([] if so_far is None else [so_far])
    return pl.pallas_call(
        functools.partial(weights_kernel, rest_count, numbers),
        out_shape=jax.ShapeDtypeStruct(weights.shape, weights.dtype),
        in_specs=[vmem] * (1 + len(updates)) + ([] if so_far is None else [whole]),
        out_specs=whole,
        scratch_shapes=[
            pltpu.VMEM((len(numbers),) + weights.shape[2:], weights.dtype),
            pltpu.SemaphoreType.DMA((len(numbers),)),
        ],
        input_output_aliases={} if so_far is None else {len(operands) - 1: 0},
        compiler_params=pltpu.CompilerParams(vmem_limit_bytes=VMEM_BYTES),
    )(*operands)


def on_device(momentum, weights):
    order = momentum.shape[3]
    opt, layer = lax.axis_size("opt"), lax.axis_size("layer")
    rest_count = opt // 8
    rest_groups = [[group * rest_count + rest for rest in range(rest_count)] for group in range(8)]
    scale = float(layer * opt * momentum.shape[2])

    def regroup(array, split_axis, concat_axis):
        if rest_count == 1:
            return array
        return lax.all_to_all(
            array,
            "opt",
            split_axis=split_axis,
            concat_axis=concat_axis,
            axis_index_groups=rest_groups,
            tiled=True,
        )

    def swap(arrays, partners, back=False):
        permutes = swaps(opt, layer, partners)
        if back:
            permutes = [[(target, source) for source, target in permute] for permute in permutes]
        return [lax.ppermute(array, AXES, permute) for array, permute in zip(arrays, permutes)]

    spread = regroup(momentum[0], 0, 1)
    experts, row_count, _ = spread.shape
    by_block = (experts // 2, 2, row_count, order)
    blocks = (jax.ShapeDtypeStruct(by_block[2:], spread.dtype),) * (1 + len(ROWS))
    packed, message = packed_shape(order), message_shape(order)
    quarter = jax.ShapeDtypeStruct(packed.shape[1:], packed.dtype)

    own, *dealt = call(
        functools.partial(deal_kernel, rest_count),
        blocks,
        spread.reshape(by_block),
    )
    rows = [own] + swap(dealt, ROWS)
    early_gram = call(early_gram_kernel, packed, *rows[:EARLY])
    place_sum = call(gram_kernel, packed, early_gram, *rows[EARLY:])
    parts = call(functools.partial(reduce_kernel, rest_count, order), (message,) * 3, place_sum)
    total, *rests = call(
        functools.partial(gather_kernel, rest_count, order),
        (quarter,) + (message,) * 3,
        place_sum,
        *swap(parts, OWNERS),
    )
    factor = call(
        functools.partial(factor_kernel, rest_count, order, scale),
        jax.ShapeDtypeStruct((order, order), jnp.bfloat16),
        place_sum,
        total,
        *swap(rests, OWNERS),
        scratch=[pltpu.VMEM(packed.shape, packed.dtype)],
    )
    own_update, *updates = call(update_kernel, blocks, factor, *rows)
    held = regroup(weights[0], 0, 1).reshape(by_block)
    returned = [own_update] + swap(updates, ROWS, back=True)
    numbers = range(len(blocks))
    fresh = new_weights(rest_count, numbers[:EARLY], held, returned[:EARLY])
    fresh = new_weights(rest_count, numbers[EARLY:], held, returned[EARLY:], fresh)
    return regroup(fresh.reshape(experts, row_count, order), 1, 0)[None]


def solution(mesh):
    in_specs = (P("layer", None, "opt", None), P("layer", None, "opt", None))
    out_specs = P("layer", None, "opt", None)
    return jax.shard_map(
        on_device, mesh=mesh, in_specs=in_specs, out_specs=out_specs, check_vma=False
    )
```

```python
import functools
import itertools

import jax
import jax.numpy as jnp
from jax import lax
from jax.experimental import pallas as pl
from jax.experimental.pallas import tpu as pltpu
from jax.sharding import PartitionSpec as P

ITERS = 3
BLOCK = 128
WIDE = 256
F32_TILE = 8
BF16_TILE = 16
VMEM_BYTES = 48 << 20
EARLY = 5

first_coef = 3.4445
second_coef = -4.775
third_coef = 2.0315
epsilon = 1e-06
step_rate = 0.5
decay_rate = 0.1

AXES = ("opt", "layer")


def flips_of(z, y, x, pair=0, half=0):
    return (half, z, y, 0, x, pair)


def neighbour_steps():
    ways = [(0, 0, 1), (0, 1, 0), (1, 0, 0)]
    order = [(ways[step], ways[(step + 1) % 3]) for step in range(3)]
    return [tuple(flips_of(*way, pair=cross) for way in step) for cross in (1, 0) for step in order]


ROWS = neighbour_steps() + [(flips_of(0, 0, 0, pair=1),) * 2]
OWNERS = [(flips,) * 2 for flips in (flips_of(1, 0, 0, half=1), flips_of(0, 1, 1, half=1), flips_of(1, 1, 1))]


def colour_step(flips):
    return flips[4] ^ 2 * flips[2] ^ 3 * (flips[1] ^ flips[0])


def quarter_step(flips):
    return flips[4] + 2 * flips[0]


def swaps(opt, layer, partners):
    rest_count = opt // 8
    sizes = (2, 2, 2, rest_count, 2, 2)

    def device(half, z, y, rest, x, pair):
        return (((half * 2 + z) * 2 + y) * rest_count + rest) * layer + x * 2 + pair

    return [
        [
            (device(*spot), device(*(value ^ flip for value, flip in zip(spot, flips[spot[5]]))))
            for spot in itertools.product(*map(range, sizes))
        ]
        for flips in partners
    ]


def by_pair(pair, values):
    return values[0] + pair * (values[1] - values[0])


class Place:
    def __init__(self, rest_count):
        index = lax.axis_index("opt") // rest_count
        x, self.pair = lax.axis_index("layer") // 2, lax.axis_index("layer") % 2
        half, z, y = index // 4, index // 2 % 2, index % 2
        self.colour = x ^ (2 * y) ^ (3 * (z ^ half))
        self.quarter = x + 2 * half

    def block(self, number):
        if number == 0:
            return self.colour, self.pair
        flips = ROWS[number - 1]
        return self.colour ^ by_pair(self.pair, [colour_step(way) for way in flips]), self.pair ^ flips[0][5]

    def quarter_at(self, step):
        return self.quarter ^ by_pair(self.pair, [quarter_step(flips) for flips in OWNERS[step]])


def call(kernel, out_shape, *operands, scratch=()):
    vmem = pl.BlockSpec(memory_space=pltpu.VMEM)
    return pl.pallas_call(
        kernel,
        out_shape=out_shape,
        in_specs=[vmem] * len(operands),
        out_specs=jax.tree.map(lambda _: vmem, out_shape),
        scratch_shapes=list(scratch),
        compiler_params=pltpu.CompilerParams(vmem_limit_bytes=VMEM_BYTES),
    )(*operands)


def product(first, second):
    return jnp.dot(first, second, preferred_element_type=jnp.float32)


def quarters_of(order):
    count = order // BLOCK
    folds = [("fold", i, i + 1) for i in range(0, count, 2)]
    others = [("plain", i, j) for i in range(count) for j in range(i + 1, count)]
    length = (len(folds) + len(others)) // 4
    quarters = []
    for quarter in range(4):
        blocks = folds[quarter::4]
        missing = length - len(blocks)
        quarters.append(blocks + others[:missing])
        others = others[missing:]
    return quarters


def quarter_blocks(order):
    quarters = quarters_of(order)
    return max(sum(kind == "fold" for kind, _, _ in blocks) for blocks in quarters), len(quarters[0])


def packed_shape(order):
    return jax.ShapeDtypeStruct((4, quarter_blocks(order)[1] * BLOCK + F32_TILE, BLOCK), jnp.float32)


def message_shape(order):
    return jax.ShapeDtypeStruct((quarter_blocks(order)[1] * BLOCK + BF16_TILE, BLOCK), jnp.bfloat16)


def grid_ids():
    shape = (BLOCK, BLOCK)
    return lax.broadcasted_iota(jnp.int32, shape, 0), lax.broadcasted_iota(jnp.int32, shape, 1)


def diagonal(block):
    row_ids, column_ids = grid_ids()
    return jnp.sum(jnp.where(row_ids == column_ids, block, 0.0), axis=0, keepdims=True)


def padded(rows, height):
    missing = height - sum(row.shape[0] for row in rows)
    return jnp.concatenate(rows + [jnp.zeros((missing, BLOCK), jnp.float32)], axis=0)


def pack(block, order):
    row_ids, column_ids = grid_ids()
    result = []
    for blocks in quarters_of(order):
        tiles, rows = [], []
        for kind, i, j in blocks:
            if kind == "fold":
                second = block(j, j)
                tiles.append(jnp.where(row_ids <= column_ids, block(i, i), second))
                rows.append(diagonal(second))
            else:
                tiles.append(block(i, j))
        result.append(jnp.concatenate(tiles + [padded(rows, F32_TILE)], axis=0))
    return result


def unpack(quarters, order):
    row_ids, column_ids = grid_ids()
    result = {}
    for blocks, quarter in zip(quarters_of(order), quarters):
        tail = quarter[len(blocks) * BLOCK :]
        for k, (kind, i, j) in enumerate(blocks):
            tile = quarter[k * BLOCK : (k + 1) * BLOCK]
            if kind == "fold":
                mirrored = tile.T
                result[i, i] = jnp.where(row_ids <= column_ids, tile, mirrored)
                second = jnp.where(row_ids > column_ids, tile, mirrored)
                result[j, j] = jnp.where(row_ids == column_ids, tail[k : k + 1], second)
            else:
                result[i, j] = tile
    return result


def to_message(quarter, order):
    fold_count, block_count = quarter_blocks(order)
    length = block_count * BLOCK
    body, tail = quarter[:length], quarter[length : length + fold_count]
    rounded = body.astype(jnp.bfloat16)
    rows = [
        diagonal(
            body[k * BLOCK : (k + 1) * BLOCK] - rounded[k * BLOCK : (k + 1) * BLOCK].astype(jnp.float32)
        )
        for k in range(fold_count)
    ]
    high = tail.astype(jnp.bfloat16).astype(jnp.float32)
    extra = padded(rows + [high, tail - high], BF16_TILE)
    return jnp.concatenate([rounded, extra.astype(jnp.bfloat16)], axis=0)


def from_message(message, order):
    fold_count, block_count = quarter_blocks(order)
    length = block_count * BLOCK
    row_ids, column_ids = grid_ids()
    values = message.astype(jnp.float32)
    body, extra = values[:length], values[length:]
    tiles = [
        body[k * BLOCK : (k + 1) * BLOCK] + jnp.where(row_ids == column_ids, extra[k : k + 1], 0.0)
        for k in range(fold_count)
    ]
    tail = extra[fold_count : 2 * fold_count] + extra[2 * fold_count : 3 * fold_count]
    return jnp.concatenate(tiles + [body[fold_count * BLOCK :], padded([tail], F32_TILE)], axis=0)


def deal_kernel(rest_count, momentum_ref, *refs):
    place = Place(rest_count)
    for number, block_ref in enumerate(refs):
        block_ref[...] = momentum_ref[place.block(number)]


def packed_gram(block_refs):
    rows = jnp.concatenate([block_ref[...] for block_ref in block_refs], axis=0)
    order = rows.shape[1]
    tiles = {}
    for row in range(0, order, WIDE):
        for column in range(row, order, WIDE):
            tiles[row, column] = lax.dot_general(
                rows[:, row : row + WIDE],
                rows[:, column : column + WIDE],
                (((0,), (0,)), ((), ())),
                preferred_element_type=jnp.float32,
            )

    def block(i, j):
        row, column = i * BLOCK, j * BLOCK
        tile = tiles[row // WIDE * WIDE, column // WIDE * WIDE]
        return tile[row % WIDE :, column % WIDE :][:BLOCK, :BLOCK]

    return pack(block, order)


def early_gram_kernel(*refs):
    for quarter, value in enumerate(packed_gram(refs[:-1])):
        refs[-1][quarter] = value


def gram_kernel(early_ref, *refs):
    for quarter, value in enumerate(packed_gram(refs[:-1])):
        refs[-1][quarter] = early_ref[quarter] + value


def reduce_kernel(rest_count, order, sum_ref, *message_refs):
    place = Place(rest_count)
    for step, message_ref in enumerate(message_refs):
        message_ref[...] = to_message(sum_ref[place.quarter_at(step)], order)


def gather_kernel(rest_count, order, sum_ref, *refs):
    arrived_refs, total_ref, message_refs = refs[:3], refs[3], refs[4:]
    arrived = [from_message(arrived_ref[...], order) for arrived_ref in arrived_refs]
    total = sum_ref[Place(rest_count).quarter] + (arrived[0] + (arrived[1] + arrived[2]))
    total_ref[...] = total
    for value, message_ref in zip(arrived, message_refs):
        message_ref[...] = to_message(total - value, order)


def assemble(upper, count):
    return jnp.concatenate(
        [
            jnp.concatenate([upper[i, j] if i <= j else upper[j, i].T for j in range(count)], axis=1)
            for i in range(count)
        ],
        axis=0,
    )


def rounded(upper, count):
    return assemble({key: value.astype(jnp.bfloat16) for key, value in upper.items()}, count)


def symmetric_product(first, second, count):
    size = first.shape[0] // count
    return {
        (i, j): product(first[i * size : (i + 1) * size, :], second[:, j * size : (j + 1) * size])
        for i in range(count)
        for j in range(i, count)
    }


def exact_square(upper, count):
    high = rounded(upper, count)
    low = rounded(
        {key: value - value.astype(jnp.bfloat16).astype(jnp.float32) for key, value in upper.items()}, count
    )
    return combine(
        (1.0, symmetric_product(high, high, count)),
        (1.0, combine((1.0, symmetric_product(high, low, count)), (1.0, symmetric_product(low, high, count)))),
    )


def combine(*terms):
    return {
        key: functools.reduce(jnp.add, [value[key] if factor == 1.0 else factor * value[key] for factor, value in terms])
        for key in terms[0][1]
    }


def newton(current, count):
    accum_identity, accum = 1.0, None
    for iteration in range(ITERS):
        last = iteration + 1 == ITERS
        current_high = None if last else rounded(current, count)
        squared = exact_square(current, count) if last else symmetric_product(current_high, current_high, count)
        rest = combine((second_coef, current), (third_coef, squared))
        rest_high = rounded(rest, count)
        if accum is None:
            accum = rest
        else:
            accum = combine(
                (accum_identity, rest),
                (first_coef, accum),
                (1.0, symmetric_product(rounded(accum, count), rest_high, count)),
            )
        accum_identity *= first_coef
        if not last:
            inner = combine((first_coef, current), (1.0, symmetric_product(current_high, rest_high, count)))
            current = combine(
                (first_coef, inner), (1.0, symmetric_product(rounded(inner, count), rest_high, count))
            )
    return accum_identity, accum


def factor_kernel(rest_count, order, scale, sum_ref, total_ref, *refs):
    rest_refs, factor_ref, quarters_ref = refs[:3], refs[3], refs[4]
    place = Place(rest_count)
    quarters_ref[place.quarter] = total_ref[...]
    for step, rest_ref in enumerate(rest_refs):
        quarter = place.quarter_at(step)
        quarters_ref[quarter] = sum_ref[quarter] + from_message(rest_ref[...], order)
    blocks = unpack([quarters_ref[quarter] for quarter in range(4)], order)
    trace_sum = jnp.sum(sum(diagonal(blocks[i, i]) for i in range(order // BLOCK)))
    shrink = 1.0 / (trace_sum + epsilon)
    count, ratio = order // WIDE, WIDE // BLOCK
    current = {}
    for i in range(count):
        for j in range(i, count):
            tile = jnp.concatenate(
                [
                    jnp.concatenate(
                        [
                            blocks[row, column] if row <= column else blocks[column, row].T
                            for column in range(j * ratio, (j + 1) * ratio)
                        ],
                        axis=1,
                    )
                    for row in range(i * ratio, (i + 1) * ratio)
                ],
                axis=0,
            )
            current[i, j] = tile * shrink
    accum_identity, accum = newton(current, count)
    growth = jnp.sqrt(scale / (trace_sum + epsilon))
    shape = (WIDE, WIDE)
    identity = lax.broadcasted_iota(jnp.int32, shape, 0) == lax.broadcasted_iota(jnp.int32, shape, 1)
    factor_ref[...] = rounded(
        {
            (i, j): (value + jnp.where(identity, accum_identity, 0.0) if i == j else value) * growth
            for (i, j), value in accum.items()
        },
        count,
    )


def update_kernel(factor_ref, *refs):
    block_refs, update_refs = refs[: len(refs) // 2], refs[len(refs) // 2 :]
    update = product(jnp.concatenate([block_ref[...] for block_ref in block_refs], axis=0), factor_ref[...])
    count = block_refs[0].shape[0]
    for number, update_ref in enumerate(update_refs):
        update_ref[...] = update[number * count : (number + 1) * count].astype(update_ref.dtype)


def weights_kernel(rest_count, numbers, weights_ref, *refs):
    out_ref, fresh_ref, semaphores = refs[-3:]
    place = Place(rest_count)
    shrink = 1.0 - step_rate * decay_rate
    copies = []
    for slot, (number, update_ref) in enumerate(zip(numbers, refs)):
        block = place.block(number)
        fresh_ref[slot] = (
            shrink * weights_ref[block].astype(jnp.float32) - step_rate * update_ref[...].astype(jnp.float32)
        ).astype(fresh_ref.dtype)
        copies.append(pltpu.make_async_copy(fresh_ref.at[slot], out_ref.at[block], semaphores.at[slot]))
        copies[-1].start()
    for copy in copies:
        copy.wait()


def new_weights(rest_count, numbers, weights, updates, so_far=None):
    vmem, whole = pl.BlockSpec(memory_space=pltpu.VMEM), pl.BlockSpec(memory_space=pltpu.HBM)
    operands = [weights, *updates] + ([] if so_far is None else [so_far])
    return pl.pallas_call(
        functools.partial(weights_kernel, rest_count, numbers),
        out_shape=jax.ShapeDtypeStruct(weights.shape, weights.dtype),
        in_specs=[vmem] * (1 + len(updates)) + ([] if so_far is None else [whole]),
        out_specs=whole,
        scratch_shapes=[
            pltpu.VMEM((len(numbers),) + weights.shape[2:], weights.dtype),
            pltpu.SemaphoreType.DMA((len(numbers),)),
        ],
        input_output_aliases={} if so_far is None else {len(operands) - 1: 0},
        compiler_params=pltpu.CompilerParams(vmem_limit_bytes=VMEM_BYTES),
    )(*operands)


def on_device(momentum, weights):
    order = momentum.shape[3]
    opt, layer = lax.axis_size("opt"), lax.axis_size("layer")
    rest_count = opt // 8
    rest_groups = [[group * rest_count + rest for rest in range(rest_count)] for group in range(8)]
    scale = float(layer * opt * momentum.shape[2])

    def regroup(array, split_axis, concat_axis):
        if rest_count == 1:
            return array
        return lax.all_to_all(
            array,
            "opt",
            split_axis=split_axis,
            concat_axis=concat_axis,
            axis_index_groups=rest_groups,
            tiled=True,
        )

    def swap(arrays, partners, back=False):
        permutes = swaps(opt, layer, partners)
        if back:
            permutes = [[(target, source) for source, target in permute] for permute in permutes]
        return [lax.ppermute(array, AXES, permute) for array, permute in zip(arrays, permutes)]

    spread = regroup(momentum[0], 0, 1)
    experts, row_count, _ = spread.shape
    by_block = (experts // 2, 2, row_count, order)
    blocks = (jax.ShapeDtypeStruct(by_block[2:], spread.dtype),) * (1 + len(ROWS))
    packed, message = packed_shape(order), message_shape(order)
    quarter = jax.ShapeDtypeStruct(packed.shape[1:], packed.dtype)

    own, *dealt = call(
        functools.partial(deal_kernel, rest_count),
        blocks,
        spread.reshape(by_block),
    )
    rows = [own] + swap(dealt, ROWS)
    early_gram = call(early_gram_kernel, packed, *rows[:EARLY])
    place_sum = call(gram_kernel, packed, early_gram, *rows[EARLY:])
    parts = call(functools.partial(reduce_kernel, rest_count, order), (message,) * 3, place_sum)
    total, *rests = call(
        functools.partial(gather_kernel, rest_count, order),
        (quarter,) + (message,) * 3,
        place_sum,
        *swap(parts, OWNERS),
    )
    factor = call(
        functools.partial(factor_kernel, rest_count, order, scale),
        jax.ShapeDtypeStruct((order, order), jnp.bfloat16),
        place_sum,
        total,
        *swap(rests, OWNERS),
        scratch=[pltpu.VMEM(packed.shape, packed.dtype)],
    )
    own_update, *updates = call(update_kernel, blocks, factor, *rows)
    held = regroup(weights[0], 0, 1).reshape(by_block)
    returned = [own_update] + swap(updates, ROWS, back=True)
    numbers = range(len(blocks))
    fresh = new_weights(rest_count, numbers[:EARLY], held, returned[:EARLY])
    fresh = new_weights(rest_count, numbers[EARLY:], held, returned[EARLY:], fresh)
    return regroup(fresh.reshape(experts, row_count, order), 1, 0)[None]


def solution(mesh):
    in_specs = (P("layer", None, "opt", None), P("layer", None, "opt", None))
    out_specs = P("layer", None, "opt", None)
    return jax.shard_map(
        on_device, mesh=mesh, in_specs=in_specs, out_specs=out_specs, check_vma=False
    )
```

```python
import functools
import itertools

import jax
import jax.numpy as jnp
from jax import lax
from jax.experimental import pallas as pl
from jax.experimental.pallas import tpu as pltpu
from jax.sharding import PartitionSpec as P

ITERS = 3
BLOCK = 128
WIDE = 256
F32_TILE = 8
BF16_TILE = 16
SMALLEST = 1e-30
VMEM_BYTES = 48 << 20
EARLY = 5

first_coef = 3.4445
second_coef = -4.775
third_coef = 2.0315
epsilon = 1e-06
step_rate = 0.5
decay_rate = 0.1

AXES = ("opt", "layer")


def flips_of(z, y, x, pair=0, half=0):
    return (half, z, y, 0, x, pair)


def neighbour_steps():
    ways = [(0, 0, 1), (0, 1, 0), (1, 0, 0)]
    order = [(ways[step], ways[(step + 1) % 3]) for step in range(3)]
    return [tuple(flips_of(*way, pair=cross) for way in step) for cross in (1, 0) for step in order]


ROWS = neighbour_steps() + [(flips_of(0, 0, 0, pair=1),) * 2]
OWNERS = [(flips,) * 2 for flips in (flips_of(1, 0, 0, half=1), flips_of(0, 1, 1, half=1), flips_of(1, 1, 1))]


def colour_step(flips):
    return flips[4] ^ 2 * flips[2] ^ 3 * (flips[1] ^ flips[0])


def quarter_step(flips):
    return flips[4] + 2 * flips[0]


def swaps(opt, layer, partners):
    rest_count = opt // 8
    sizes = (2, 2, 2, rest_count, 2, 2)

    def device(half, z, y, rest, x, pair):
        return (((half * 2 + z) * 2 + y) * rest_count + rest) * layer + x * 2 + pair

    return [
        [
            (device(*spot), device(*(value ^ flip for value, flip in zip(spot, flips[spot[5]]))))
            for spot in itertools.product(*map(range, sizes))
        ]
        for flips in partners
    ]


def by_pair(pair, values):
    return values[0] + pair * (values[1] - values[0])


class Place:
    def __init__(self, rest_count):
        index = lax.axis_index("opt") // rest_count
        x, self.pair = lax.axis_index("layer") // 2, lax.axis_index("layer") % 2
        half, z, y = index // 4, index // 2 % 2, index % 2
        self.colour = x ^ (2 * y) ^ (3 * (z ^ half))
        self.quarter = x + 2 * half

    def block(self, number):
        if number == 0:
            return self.colour, self.pair
        flips = ROWS[number - 1]
        return self.colour ^ by_pair(self.pair, [colour_step(way) for way in flips]), self.pair ^ flips[0][5]

    def quarter_at(self, step):
        return self.quarter ^ by_pair(self.pair, [quarter_step(flips) for flips in OWNERS[step]])


def call(kernel, out_shape, *operands, scratch=()):
    vmem = pl.BlockSpec(memory_space=pltpu.VMEM)
    return pl.pallas_call(
        kernel,
        out_shape=out_shape,
        in_specs=[vmem] * len(operands),
        out_specs=jax.tree.map(lambda _: vmem, out_shape),
        scratch_shapes=list(scratch),
        compiler_params=pltpu.CompilerParams(vmem_limit_bytes=VMEM_BYTES),
    )(*operands)


def product(first, second):
    return jnp.dot(first, second, preferred_element_type=jnp.float32)


def quarters_of(order):
    count = order // BLOCK
    folds = [("fold", i, i + 1) for i in range(0, count, 2)]
    others = [("plain", i, j) for i in range(count) for j in range(i + 1, count)]
    length = (len(folds) + len(others)) // 4
    quarters = []
    for quarter in range(4):
        blocks = folds[quarter::4]
        missing = length - len(blocks)
        quarters.append(blocks + others[:missing])
        others = others[missing:]
    return quarters


def quarter_blocks(order):
    quarters = quarters_of(order)
    return max(sum(kind == "fold" for kind, _, _ in blocks) for blocks in quarters), len(quarters[0])


def packed_shape(order):
    return jax.ShapeDtypeStruct((4, quarter_blocks(order)[1] * BLOCK + F32_TILE, BLOCK), jnp.float32)


def message_shape(order):
    return jax.ShapeDtypeStruct((quarter_blocks(order)[1] * BLOCK + BF16_TILE, BLOCK), jnp.bfloat16)


def grid_ids():
    shape = (BLOCK, BLOCK)
    return lax.broadcasted_iota(jnp.int32, shape, 0), lax.broadcasted_iota(jnp.int32, shape, 1)


def diagonal(block):
    row_ids, column_ids = grid_ids()
    return jnp.sum(jnp.where(row_ids == column_ids, block, 0.0), axis=0, keepdims=True)


def padded(rows, height):
    missing = height - sum(row.shape[0] for row in rows)
    return jnp.concatenate(rows + [jnp.zeros((missing, BLOCK), jnp.float32)], axis=0)


def pack(block, order):
    row_ids, column_ids = grid_ids()
    result = []
    for blocks in quarters_of(order):
        tiles, rows = [], []
        for kind, i, j in blocks:
            if kind == "fold":
                second = block(j, j)
                tiles.append(jnp.where(row_ids <= column_ids, block(i, i), second))
                rows.append(diagonal(second))
            else:
                tiles.append(block(i, j))
        result.append(jnp.concatenate(tiles + [padded(rows, F32_TILE)], axis=0))
    return result


def unpack(quarters, order):
    row_ids, column_ids = grid_ids()
    result = {}
    for blocks, quarter in zip(quarters_of(order), quarters):
        tail = quarter[len(blocks) * BLOCK :]
        for k, (kind, i, j) in enumerate(blocks):
            tile = quarter[k * BLOCK : (k + 1) * BLOCK]
            if kind == "fold":
                mirrored = tile.T
                result[i, i] = jnp.where(row_ids <= column_ids, tile, mirrored)
                second = jnp.where(row_ids > column_ids, tile, mirrored)
                result[j, j] = jnp.where(row_ids == column_ids, tail[k : k + 1], second)
            else:
                result[i, j] = tile
    return result


def to_message(quarter, order, vector=None):
    fold_count, block_count = quarter_blocks(order)
    length = block_count * BLOCK
    body, tail = quarter[:length], quarter[length : length + fold_count]
    rounded_body = body.astype(jnp.bfloat16)
    rows = [
        diagonal(
            body[k * BLOCK : (k + 1) * BLOCK] - rounded_body[k * BLOCK : (k + 1) * BLOCK].astype(jnp.float32)
        )
        for k in range(fold_count)
    ]
    high = tail.astype(jnp.bfloat16).astype(jnp.float32)
    rows += [high, tail - high]
    if vector is not None:
        rows += [vector[:, k : k + BLOCK] for k in range(0, order, BLOCK)]
    return jnp.concatenate([rounded_body, padded(rows, BF16_TILE).astype(jnp.bfloat16)], axis=0)


def from_message(message, order):
    fold_count, block_count = quarter_blocks(order)
    length = block_count * BLOCK
    row_ids, column_ids = grid_ids()
    values = message.astype(jnp.float32)
    body, extra = values[:length], values[length:]
    tiles = [
        body[k * BLOCK : (k + 1) * BLOCK] + jnp.where(row_ids == column_ids, extra[k : k + 1], 0.0)
        for k in range(fold_count)
    ]
    tail = extra[fold_count : 2 * fold_count] + extra[2 * fold_count : 3 * fold_count]
    return jnp.concatenate(tiles + [body[fold_count * BLOCK :], padded([tail], F32_TILE)], axis=0)


def vector_of(message, order):
    fold_count, block_count = quarter_blocks(order)
    start = block_count * BLOCK + 3 * fold_count
    values = message.astype(jnp.float32)
    return jnp.concatenate([values[start + k : start + k + 1] for k in range(order // BLOCK)], axis=1)


def stacked(vectors):
    rows = jnp.concatenate(vectors, axis=0)
    filler = jnp.zeros((BF16_TILE - rows.shape[0], rows.shape[1]), jnp.float32)
    return jnp.concatenate([rows, filler], axis=0).astype(jnp.bfloat16)


def outer_products(vectors):
    order = vectors.shape[1]
    result = {}
    for start in range(0, order, BLOCK):
        band = lax.dot_general(
            vectors[:, start : start + BLOCK],
            vectors[:, start:],
            (((0,), (0,)), ((), ())),
            preferred_element_type=jnp.float32,
        )
        for offset in range(0, order - start, BLOCK):
            place = start // BLOCK, (start + offset) // BLOCK
            result[place] = band[:, offset : offset + BLOCK]
    return result


def main_direction(first_row):
    signs = jnp.where(first_row[0][:, :1] < 0.0, -1.0, 1.0)
    rows = [jnp.sum(signs * block, axis=0, keepdims=True) for block in first_row]
    size = jnp.sum(jnp.where(first_row[0][:1, :] < 0.0, -rows[0], rows[0]))
    growth = jnp.where(size > 0.0, lax.rsqrt(jnp.maximum(size, SMALLEST)), 0.0)
    return (jnp.concatenate(rows, axis=1) * growth).astype(jnp.bfloat16).astype(jnp.float32)


def deal_kernel(rest_count, momentum_ref, *refs):
    place = Place(rest_count)
    for number, block_ref in enumerate(refs):
        block_ref[...] = momentum_ref[place.block(number)]


def packed_gram(block_refs):
    rows = jnp.concatenate([block_ref[...] for block_ref in block_refs], axis=0)
    order = rows.shape[1]
    tiles = {}
    for row in range(0, order, WIDE):
        for column in range(row, order, WIDE):
            tiles[row, column] = lax.dot_general(
                rows[:, row : row + WIDE],
                rows[:, column : column + WIDE],
                (((0,), (0,)), ((), ())),
                preferred_element_type=jnp.float32,
            )

    def block(i, j):
        row, column = i * BLOCK, j * BLOCK
        tile = tiles[row // WIDE * WIDE, column // WIDE * WIDE]
        return tile[row % WIDE :, column % WIDE :][:BLOCK, :BLOCK]

    return pack(block, order), [block(0, k) for k in range(order // BLOCK)]


def early_gram_kernel(*refs):
    block_refs, packed_ref, first_row_ref = refs[:-2], refs[-2], refs[-1]
    packed, first_row = packed_gram(block_refs)
    for quarter, value in enumerate(packed):
        packed_ref[quarter] = value
    for number, value in enumerate(first_row):
        first_row_ref[number] = value


def gram_kernel(early_ref, early_row_ref, *refs):
    block_refs, left_ref, direction_ref = refs[:-2], refs[-2], refs[-1]
    order = block_refs[0].shape[1]
    packed, first_row = packed_gram(block_refs)
    direction = main_direction([early_row_ref[number] + value for number, value in enumerate(first_row)])
    direction_ref[...] = stacked([direction])
    outer = outer_products(stacked([direction]))
    for quarter, (value, known) in enumerate(zip(packed, pack(lambda i, j: outer[i, j], order))):
        left_ref[quarter] = early_ref[quarter] + (value - known)


def reduce_kernel(rest_count, order, left_ref, direction_ref, *message_refs):
    place = Place(rest_count)
    direction = direction_ref[...].astype(jnp.float32)[:1]
    for step, message_ref in enumerate(message_refs):
        message_ref[...] = to_message(left_ref[place.quarter_at(step)], order, direction)


def gather_kernel(rest_count, order, left_ref, direction_ref, *refs):
    arrived_refs, total_ref, directions_ref, message_refs = refs[:3], refs[3], refs[4], refs[5:]
    arrived = [from_message(arrived_ref[...], order) for arrived_ref in arrived_refs]
    total = left_ref[Place(rest_count).quarter] + (arrived[0] + (arrived[1] + arrived[2]))
    total_ref[...] = total
    for value, message_ref in zip(arrived, message_refs):
        message_ref[...] = to_message(total - value, order)
    own = direction_ref[...].astype(jnp.float32)[:1]
    directions_ref[...] = stacked([own] + [vector_of(arrived_ref[...], order) for arrived_ref in arrived_refs])


def assemble(upper, count):
    return jnp.concatenate(
        [
            jnp.concatenate([upper[i, j] if i <= j else upper[j, i].T for j in range(count)], axis=1)
            for i in range(count)
        ],
        axis=0,
    )


def rounded(upper, count):
    return assemble({key: value.astype(jnp.bfloat16) for key, value in upper.items()}, count)


def symmetric_product(first, second, count):
    size = first.shape[0] // count
    return {
        (i, j): product(first[i * size : (i + 1) * size, :], second[:, j * size : (j + 1) * size])
        for i in range(count)
        for j in range(i, count)
    }


def exact_square(upper, count):
    high = rounded(upper, count)
    low = rounded(
        {key: value - value.astype(jnp.bfloat16).astype(jnp.float32) for key, value in upper.items()}, count
    )
    return combine(
        (1.0, symmetric_product(high, high, count)),
        (1.0, combine((1.0, symmetric_product(high, low, count)), (1.0, symmetric_product(low, high, count)))),
    )


def combine(*terms):
    return {
        key: functools.reduce(jnp.add, [value[key] if factor == 1.0 else factor * value[key] for factor, value in terms])
        for key in terms[0][1]
    }


def newton(current, count):
    accum_identity, accum = 1.0, None
    for iteration in range(ITERS):
        last = iteration + 1 == ITERS
        current_high = None if last else rounded(current, count)
        squared = exact_square(current, count) if last else symmetric_product(current_high, current_high, count)
        rest = combine((second_coef, current), (third_coef, squared))
        rest_high = rounded(rest, count)
        if accum is None:
            accum = rest
        else:
            accum = combine(
                (accum_identity, rest),
                (first_coef, accum),
                (1.0, symmetric_product(rounded(accum, count), rest_high, count)),
            )
        accum_identity *= first_coef
        if not last:
            inner = combine((first_coef, current), (1.0, symmetric_product(current_high, rest_high, count)))
            current = combine(
                (first_coef, inner), (1.0, symmetric_product(rounded(inner, count), rest_high, count))
            )
    return accum_identity, accum


def factor_kernel(rest_count, order, scale, left_ref, total_ref, directions_ref, *refs):
    rest_refs, factor_ref, quarters_ref = refs[:3], refs[3], refs[4]
    place = Place(rest_count)
    quarters_ref[place.quarter] = total_ref[...]
    for step, rest_ref in enumerate(rest_refs):
        quarter = place.quarter_at(step)
        quarters_ref[quarter] = left_ref[quarter] + from_message(rest_ref[...], order)
    outer = outer_products(directions_ref[...])
    blocks = {
        key: value + outer[key]
        for key, value in unpack([quarters_ref[quarter] for quarter in range(4)], order).items()
    }
    trace_sum = jnp.sum(sum(diagonal(blocks[i, i]) for i in range(order // BLOCK)))
    shrink = 1.0 / (trace_sum + epsilon)
    count, ratio = order // WIDE, WIDE // BLOCK
    current = {}
    for i in range(count):
        for j in range(i, count):
            tile = jnp.concatenate(
                [
                    jnp.concatenate(
                        [
                            blocks[row, column] if row <= column else blocks[column, row].T
                            for column in range(j * ratio, (j + 1) * ratio)
                        ],
                        axis=1,
                    )
                    for row in range(i * ratio, (i + 1) * ratio)
                ],
                axis=0,
            )
            current[i, j] = tile * shrink
    accum_identity, accum = newton(current, count)
    growth = jnp.sqrt(scale / (trace_sum + epsilon))
    shape = (WIDE, WIDE)
    identity = lax.broadcasted_iota(jnp.int32, shape, 0) == lax.broadcasted_iota(jnp.int32, shape, 1)
    factor_ref[...] = rounded(
        {
            (i, j): (value + jnp.where(identity, accum_identity, 0.0) if i == j else value) * growth
            for (i, j), value in accum.items()
        },
        count,
    )


def update_kernel(factor_ref, *refs):
    block_refs, update_refs = refs[: len(refs) // 2], refs[len(refs) // 2 :]
    update = product(jnp.concatenate([block_ref[...] for block_ref in block_refs], axis=0), factor_ref[...])
    count = block_refs[0].shape[0]
    for number, update_ref in enumerate(update_refs):
        update_ref[...] = update[number * count : (number + 1) * count].astype(update_ref.dtype)


def weights_kernel(rest_count, numbers, weights_ref, *refs):
    out_ref, fresh_ref, semaphores = refs[-3:]
    place = Place(rest_count)
    shrink = 1.0 - step_rate * decay_rate
    copies = []
    for slot, (number, update_ref) in enumerate(zip(numbers, refs)):
        block = place.block(number)
        fresh_ref[slot] = (
            shrink * weights_ref[block].astype(jnp.float32) - step_rate * update_ref[...].astype(jnp.float32)
        ).astype(fresh_ref.dtype)
        copies.append(pltpu.make_async_copy(fresh_ref.at[slot], out_ref.at[block], semaphores.at[slot]))
        copies[-1].start()
    for copy in copies:
        copy.wait()


def new_weights(rest_count, numbers, weights, updates, so_far=None):
    vmem, whole = pl.BlockSpec(memory_space=pltpu.VMEM), pl.BlockSpec(memory_space=pltpu.HBM)
    operands = [weights, *updates] + ([] if so_far is None else [so_far])
    return pl.pallas_call(
        functools.partial(weights_kernel, rest_count, numbers),
        out_shape=jax.ShapeDtypeStruct(weights.shape, weights.dtype),
        in_specs=[vmem] * (1 + len(updates)) + ([] if so_far is None else [whole]),
        out_specs=whole,
        scratch_shapes=[
            pltpu.VMEM((len(numbers),) + weights.shape[2:], weights.dtype),
            pltpu.SemaphoreType.DMA((len(numbers),)),
        ],
        input_output_aliases={} if so_far is None else {len(operands) - 1: 0},
        compiler_params=pltpu.CompilerParams(vmem_limit_bytes=VMEM_BYTES),
    )(*operands)


def on_device(momentum, weights):
    order = momentum.shape[3]
    opt, layer = lax.axis_size("opt"), lax.axis_size("layer")
    rest_count = opt // 8
    rest_groups = [[group * rest_count + rest for rest in range(rest_count)] for group in range(8)]
    scale = float(layer * opt * momentum.shape[2])

    def regroup(array, split_axis, concat_axis):
        if rest_count == 1:
            return array
        return lax.all_to_all(
            array,
            "opt",
            split_axis=split_axis,
            concat_axis=concat_axis,
            axis_index_groups=rest_groups,
            tiled=True,
        )

    def swap(arrays, partners, back=False):
        permutes = swaps(opt, layer, partners)
        if back:
            permutes = [[(target, source) for source, target in permute] for permute in permutes]
        return [lax.ppermute(array, AXES, permute) for array, permute in zip(arrays, permutes)]

    spread = regroup(momentum[0], 0, 1)
    experts, row_count, _ = spread.shape
    by_block = (experts // 2, 2, row_count, order)
    blocks = (jax.ShapeDtypeStruct(by_block[2:], spread.dtype),) * (1 + len(ROWS))
    packed, message = packed_shape(order), message_shape(order)
    quarter = jax.ShapeDtypeStruct(packed.shape[1:], packed.dtype)

    own, *dealt = call(
        functools.partial(deal_kernel, rest_count),
        blocks,
        spread.reshape(by_block),
    )
    rows = [own] + swap(dealt, ROWS)
    first_row = jax.ShapeDtypeStruct((order // BLOCK, BLOCK, BLOCK), jnp.float32)
    direction = jax.ShapeDtypeStruct((BF16_TILE, order), jnp.bfloat16)
    early = call(early_gram_kernel, (packed, first_row), *rows[:EARLY])
    left, own_direction = call(gram_kernel, (packed, direction), *early, *rows[EARLY:])
    parts = call(functools.partial(reduce_kernel, rest_count, order), (message,) * 3, left, own_direction)
    total, directions, *rests = call(
        functools.partial(gather_kernel, rest_count, order),
        (quarter, direction) + (message,) * 3,
        left,
        own_direction,
        *swap(parts, OWNERS),
    )
    factor = call(
        functools.partial(factor_kernel, rest_count, order, scale),
        jax.ShapeDtypeStruct((order, order), jnp.bfloat16),
        left,
        total,
        directions,
        *swap(rests, OWNERS),
        scratch=[pltpu.VMEM(packed.shape, packed.dtype)],
    )
    own_update, *updates = call(update_kernel, blocks, factor, *rows)
    held = regroup(weights[0], 0, 1).reshape(by_block)
    returned = [own_update] + swap(updates, ROWS, back=True)
    numbers = range(len(blocks))
    fresh = new_weights(rest_count, numbers[:EARLY], held, returned[:EARLY])
    fresh = new_weights(rest_count, numbers[EARLY:], held, returned[EARLY:], fresh)
    return regroup(fresh.reshape(experts, row_count, order), 1, 0)[None]


def solution(mesh):
    in_specs = (P("layer", None, "opt", None), P("layer", None, "opt", None))
    out_specs = P("layer", None, "opt", None)
    return jax.shard_map(
        on_device, mesh=mesh, in_specs=in_specs, out_specs=out_specs, check_vma=False
    )
```

```python
import functools
import itertools

import jax
import jax.numpy as jnp
from jax import lax
from jax.experimental import pallas as pl
from jax.experimental.pallas import tpu as pltpu
from jax.sharding import PartitionSpec as P

ITERS = 3
BLOCK = 128
WIDE = 256
F32_TILE = 8
BF16_TILE = 16
SMALLEST = 1e-30
VMEM_BYTES = 48 << 20
EARLY = 5

first_coef = 3.4445
second_coef = -4.775
third_coef = 2.0315
epsilon = 1e-06
step_rate = 0.5
decay_rate = 0.1

AXES = ("opt", "layer")


def flips_of(z, y, x, pair=0, half=0):
    return (half, z, y, 0, x, pair)


def neighbour_steps():
    ways = [(0, 0, 1), (0, 1, 0), (1, 0, 0)]
    order = [(ways[step], ways[(step + 1) % 3]) for step in range(3)]
    return [tuple(flips_of(*way, pair=cross) for way in step) for cross in (1, 0) for step in order]


ROWS = neighbour_steps() + [(flips_of(0, 0, 0, pair=1),) * 2]
OWNERS = [(flips,) * 2 for flips in (flips_of(1, 0, 0, half=1), flips_of(0, 1, 1, half=1), flips_of(1, 1, 1))]


def colour_step(flips):
    return flips[4] ^ 2 * flips[2] ^ 3 * (flips[1] ^ flips[0])


def quarter_step(flips):
    return flips[4] + 2 * flips[0]


def swaps(opt, layer, partners):
    rest_count = opt // 8
    sizes = (2, 2, 2, rest_count, 2, 2)

    def device(half, z, y, rest, x, pair):
        return (((half * 2 + z) * 2 + y) * rest_count + rest) * layer + x * 2 + pair

    return [
        [
            (device(*spot), device(*(value ^ flip for value, flip in zip(spot, flips[spot[5]]))))
            for spot in itertools.product(*map(range, sizes))
        ]
        for flips in partners
    ]


def by_pair(pair, values):
    return values[0] + pair * (values[1] - values[0])


class Place:
    def __init__(self, rest_count):
        index = lax.axis_index("opt") // rest_count
        x, self.pair = lax.axis_index("layer") // 2, lax.axis_index("layer") % 2
        half, z, y = index // 4, index // 2 % 2, index % 2
        self.colour = x ^ (2 * y) ^ (3 * (z ^ half))
        self.quarter = x + 2 * half

    def block(self, number):
        if number == 0:
            return self.colour, self.pair
        flips = ROWS[number - 1]
        return self.colour ^ by_pair(self.pair, [colour_step(way) for way in flips]), self.pair ^ flips[0][5]

    def quarter_at(self, step):
        return self.quarter ^ by_pair(self.pair, [quarter_step(flips) for flips in OWNERS[step]])


def call(kernel, out_shape, *operands, scratch=()):
    vmem = pl.BlockSpec(memory_space=pltpu.VMEM)
    return pl.pallas_call(
        kernel,
        out_shape=out_shape,
        in_specs=[vmem] * len(operands),
        out_specs=jax.tree.map(lambda _: vmem, out_shape),
        scratch_shapes=list(scratch),
        compiler_params=pltpu.CompilerParams(vmem_limit_bytes=VMEM_BYTES),
    )(*operands)


def product(first, second):
    return jnp.dot(first, second, preferred_element_type=jnp.float32)


def quarters_of(order):
    count = order // BLOCK
    folds = [("fold", i, i + 1) for i in range(0, count, 2)]
    others = [("plain", i, j) for i in range(count) for j in range(i + 1, count)]
    length = (len(folds) + len(others)) // 4
    quarters = []
    for quarter in range(4):
        blocks = folds[quarter::4]
        missing = length - len(blocks)
        quarters.append(blocks + others[:missing])
        others = others[missing:]
    return quarters


def quarter_blocks(order):
    quarters = quarters_of(order)
    return max(sum(kind == "fold" for kind, _, _ in blocks) for blocks in quarters), len(quarters[0])


def packed_shape(order):
    return jax.ShapeDtypeStruct((4, quarter_blocks(order)[1] * BLOCK + F32_TILE, BLOCK), jnp.float32)


def message_shape(order):
    return jax.ShapeDtypeStruct((quarter_blocks(order)[1] * BLOCK + BF16_TILE, BLOCK), jnp.bfloat16)


def grid_ids():
    shape = (BLOCK, BLOCK)
    return lax.broadcasted_iota(jnp.int32, shape, 0), lax.broadcasted_iota(jnp.int32, shape, 1)


def diagonal(block):
    row_ids, column_ids = grid_ids()
    return jnp.sum(jnp.where(row_ids == column_ids, block, 0.0), axis=0, keepdims=True)


def padded(rows, height):
    missing = height - sum(row.shape[0] for row in rows)
    return jnp.concatenate(rows + [jnp.zeros((missing, BLOCK), jnp.float32)], axis=0)


def pack(block, order):
    row_ids, column_ids = grid_ids()
    result = []
    for blocks in quarters_of(order):
        tiles, rows = [], []
        for kind, i, j in blocks:
            if kind == "fold":
                second = block(j, j)
                tiles.append(jnp.where(row_ids <= column_ids, block(i, i), second))
                rows.append(diagonal(second))
            else:
                tiles.append(block(i, j))
        result.append(jnp.concatenate(tiles + [padded(rows, F32_TILE)], axis=0))
    return result


def unpack(quarters, order):
    row_ids, column_ids = grid_ids()
    result = {}
    for blocks, quarter in zip(quarters_of(order), quarters):
        tail = quarter[len(blocks) * BLOCK :]
        for k, (kind, i, j) in enumerate(blocks):
            tile = quarter[k * BLOCK : (k + 1) * BLOCK]
            if kind == "fold":
                mirrored = tile.T
                result[i, i] = jnp.where(row_ids <= column_ids, tile, mirrored)
                second = jnp.where(row_ids > column_ids, tile, mirrored)
                result[j, j] = jnp.where(row_ids == column_ids, tail[k : k + 1], second)
            else:
                result[i, j] = tile
    return result


def to_message(quarter, order, vector=None):
    fold_count, block_count = quarter_blocks(order)
    length = block_count * BLOCK
    body, tail = quarter[:length], quarter[length : length + fold_count]
    rounded_body = body.astype(jnp.bfloat16)
    rows = [
        diagonal(
            body[k * BLOCK : (k + 1) * BLOCK] - rounded_body[k * BLOCK : (k + 1) * BLOCK].astype(jnp.float32)
        )
        for k in range(fold_count)
    ]
    high = tail.astype(jnp.bfloat16).astype(jnp.float32)
    rows += [high, tail - high]
    if vector is not None:
        rows += [vector[:, k : k + BLOCK] for k in range(0, order, BLOCK)]
    return jnp.concatenate([rounded_body, padded(rows, BF16_TILE).astype(jnp.bfloat16)], axis=0)


def from_message(message, order):
    fold_count, block_count = quarter_blocks(order)
    length = block_count * BLOCK
    row_ids, column_ids = grid_ids()
    values = message.astype(jnp.float32)
    body, extra = values[:length], values[length:]
    tiles = [
        body[k * BLOCK : (k + 1) * BLOCK] + jnp.where(row_ids == column_ids, extra[k : k + 1], 0.0)
        for k in range(fold_count)
    ]
    tail = extra[fold_count : 2 * fold_count] + extra[2 * fold_count : 3 * fold_count]
    return jnp.concatenate(tiles + [body[fold_count * BLOCK :], padded([tail], F32_TILE)], axis=0)


def vector_of(message, order):
    fold_count, block_count = quarter_blocks(order)
    start = block_count * BLOCK + 3 * fold_count
    values = message.astype(jnp.float32)
    return jnp.concatenate([values[start + k : start + k + 1] for k in range(order // BLOCK)], axis=1)


def stacked(vectors):
    rows = jnp.concatenate(vectors, axis=0)
    filler = jnp.zeros((BF16_TILE - rows.shape[0], rows.shape[1]), jnp.float32)
    return jnp.concatenate([rows, filler], axis=0).astype(jnp.bfloat16)


def outer_products(vectors):
    order = vectors.shape[1]
    result = {}
    for start in range(0, order, BLOCK):
        band = lax.dot_general(
            vectors[:, start : start + BLOCK],
            vectors[:, start:],
            (((0,), (0,)), ((), ())),
            preferred_element_type=jnp.float32,
        )
        for offset in range(0, order - start, BLOCK):
            place = start // BLOCK, (start + offset) // BLOCK
            result[place] = band[:, offset : offset + BLOCK]
    return result


def main_direction(first_row):
    signs = jnp.where(first_row[0][:, :1] < 0.0, -1.0, 1.0)
    rows = [jnp.sum(signs * block, axis=0, keepdims=True) for block in first_row]
    size = jnp.sum(jnp.where(first_row[0][:1, :] < 0.0, -rows[0], rows[0]))
    growth = jnp.where(size > 0.0, lax.rsqrt(jnp.maximum(size, SMALLEST)), 0.0)
    return (jnp.concatenate(rows, axis=1) * growth).astype(jnp.bfloat16).astype(jnp.float32)


def deal_kernel(rest_count, momentum_ref, *refs):
    place = Place(rest_count)
    for number, block_ref in enumerate(refs):
        block_ref[...] = momentum_ref[place.block(number)]


def packed_gram(block_refs):
    rows = jnp.concatenate([block_ref[...] for block_ref in block_refs], axis=0)
    order = rows.shape[1]
    tiles = {}
    for row in range(0, order, WIDE):
        for column in range(row, order, WIDE):
            tiles[row, column] = lax.dot_general(
                rows[:, row : row + WIDE],
                rows[:, column : column + WIDE],
                (((0,), (0,)), ((), ())),
                preferred_element_type=jnp.float32,
            )

    def block(i, j):
        row, column = i * BLOCK, j * BLOCK
        tile = tiles[row // WIDE * WIDE, column // WIDE * WIDE]
        return tile[row % WIDE :, column % WIDE :][:BLOCK, :BLOCK]

    return pack(block, order), [block(0, k) for k in range(order // BLOCK)]


def early_gram_kernel(*refs):
    block_refs, packed_ref, first_row_ref = refs[:-2], refs[-2], refs[-1]
    packed, first_row = packed_gram(block_refs)
    for quarter, value in enumerate(packed):
        packed_ref[quarter] = value
    for number, value in enumerate(first_row):
        first_row_ref[number] = value


def gram_kernel(rest_count, early_ref, early_row_ref, *refs):
    block_refs, left_ref, direction_ref, message_refs = refs[:-5], refs[-5], refs[-4], refs[-3:]
    order = block_refs[0].shape[1]
    packed, first_row = packed_gram(block_refs)
    direction = main_direction([early_row_ref[number] + value for number, value in enumerate(first_row)])
    direction_ref[...] = stacked([direction])
    outer = outer_products(stacked([direction]))
    for quarter, (value, known) in enumerate(zip(packed, pack(lambda i, j: outer[i, j], order))):
        left_ref[quarter] = early_ref[quarter] + (value - known)
    place = Place(rest_count)
    for step, message_ref in enumerate(message_refs):
        message_ref[...] = to_message(left_ref[place.quarter_at(step)], order, direction)


def gather_kernel(rest_count, order, left_ref, direction_ref, *refs):
    arrived_refs, total_ref, directions_ref, message_refs = refs[:3], refs[3], refs[4], refs[5:]
    arrived = [from_message(arrived_ref[...], order) for arrived_ref in arrived_refs]
    total = left_ref[Place(rest_count).quarter] + (arrived[0] + (arrived[1] + arrived[2]))
    total_ref[...] = total
    for value, message_ref in zip(arrived, message_refs):
        message_ref[...] = to_message(total - value, order)
    own = direction_ref[...].astype(jnp.float32)[:1]
    directions_ref[...] = stacked([own] + [vector_of(arrived_ref[...], order) for arrived_ref in arrived_refs])


def assemble(upper, count):
    return jnp.concatenate(
        [
            jnp.concatenate([upper[i, j] if i <= j else upper[j, i].T for j in range(count)], axis=1)
            for i in range(count)
        ],
        axis=0,
    )


def rounded(upper, count):
    return assemble({key: value.astype(jnp.bfloat16) for key, value in upper.items()}, count)


def symmetric_product(first, second, count):
    size = first.shape[0] // count
    return {
        (i, j): product(first[i * size : (i + 1) * size, :], second[:, j * size : (j + 1) * size])
        for i in range(count)
        for j in range(i, count)
    }


def combine(*terms):
    return {
        key: functools.reduce(jnp.add, [value[key] if factor == 1.0 else factor * value[key] for factor, value in terms])
        for key in terms[0][1]
    }


def square_beside_diagonal(upper, count):
    shape = upper[0, 0].shape
    identity = lax.broadcasted_iota(jnp.int32, shape, 0) == lax.broadcasted_iota(jnp.int32, shape, 1)
    diagonals = [jnp.where(identity, upper[i, i], 0.0) for i in range(count)]
    columns = [jnp.sum(value, axis=1, keepdims=True) for value in diagonals]
    rows = [jnp.sum(value, axis=0, keepdims=True) for value in diagonals]
    beside = {
        (i, j): jnp.where(identity, 0.0, value) if i == j else value for (i, j), value in upper.items()
    }
    beside_high = rounded(beside, count)
    entries = {(i, j): (columns[i] + rows[j]) * value for (i, j), value in beside.items()}
    for i in range(count):
        entries[i, i] = entries[i, i] + diagonals[i] * diagonals[i]
    return combine((1.0, entries), (1.0, symmetric_product(beside_high, beside_high, count)))


def newton(current, count):
    accum_identity, accum = 1.0, None
    for iteration in range(ITERS):
        last = iteration + 1 == ITERS
        current_high = None if last else rounded(current, count)
        if last:
            squared = square_beside_diagonal(current, count)
        else:
            squared = symmetric_product(current_high, current_high, count)
        rest = combine((second_coef, current), (third_coef, squared))
        rest_high = rounded(rest, count)
        if not last:
            inner = symmetric_product(current_high, rest_high, count)
            current = combine(
                (first_coef * first_coef, current),
                (2.0 * first_coef, inner),
                (1.0, symmetric_product(rounded(inner, count), rest_high, count)),
            )
        if accum is None:
            accum = rest
        else:
            accum = combine(
                (accum_identity, rest),
                (first_coef, accum),
                (1.0, symmetric_product(rounded(accum, count), rest_high, count)),
            )
        accum_identity *= first_coef
    return accum_identity, accum


def update_kernel(rest_count, order, scale, left_ref, total_ref, directions_ref, *refs):
    rest_refs, quarters_ref = refs[:3], refs[-1]
    block_refs, update_refs = refs[3 : 3 + len(refs[4:]) // 2], refs[3 + len(refs[4:]) // 2 : -1]
    place = Place(rest_count)
    quarters_ref[place.quarter] = total_ref[...]
    for step, rest_ref in enumerate(rest_refs):
        quarter = place.quarter_at(step)
        quarters_ref[quarter] = left_ref[quarter] + from_message(rest_ref[...], order)
    outer = outer_products(directions_ref[...])
    blocks = {
        key: value + outer[key]
        for key, value in unpack([quarters_ref[quarter] for quarter in range(4)], order).items()
    }
    trace_sum = jnp.sum(sum(diagonal(blocks[i, i]) for i in range(order // BLOCK)))
    shrink = 1.0 / (trace_sum + epsilon)
    count, ratio = order // WIDE, WIDE // BLOCK
    current = {}
    for i in range(count):
        for j in range(i, count):
            tile = jnp.concatenate(
                [
                    jnp.concatenate(
                        [
                            blocks[row, column] if row <= column else blocks[column, row].T
                            for column in range(j * ratio, (j + 1) * ratio)
                        ],
                        axis=1,
                    )
                    for row in range(i * ratio, (i + 1) * ratio)
                ],
                axis=0,
            )
            current[i, j] = tile * shrink
    accum_identity, accum = newton(current, count)
    growth = jnp.sqrt(scale / (trace_sum + epsilon))
    shape = (WIDE, WIDE)
    identity = lax.broadcasted_iota(jnp.int32, shape, 0) == lax.broadcasted_iota(jnp.int32, shape, 1)
    factor = rounded(
        {
            (i, j): (value + jnp.where(identity, accum_identity, 0.0) if i == j else value) * growth
            for (i, j), value in accum.items()
        },
        count,
    )
    update = product(jnp.concatenate([block_ref[...] for block_ref in block_refs], axis=0), factor)
    row_count = block_refs[0].shape[0]
    for number, update_ref in enumerate(update_refs):
        update_ref[...] = update[number * row_count : (number + 1) * row_count].astype(update_ref.dtype)


def weights_kernel(rest_count, numbers, weights_ref, *refs):
    out_ref, fresh_ref, semaphores = refs[-3:]
    place = Place(rest_count)
    shrink = 1.0 - step_rate * decay_rate
    copies = []
    for slot, (number, update_ref) in enumerate(zip(numbers, refs)):
        block = place.block(number)
        fresh_ref[slot] = (
            shrink * weights_ref[block].astype(jnp.float32) - step_rate * update_ref[...].astype(jnp.float32)
        ).astype(fresh_ref.dtype)
        copies.append(pltpu.make_async_copy(fresh_ref.at[slot], out_ref.at[block], semaphores.at[slot]))
        copies[-1].start()
    for copy in copies:
        copy.wait()


def new_weights(rest_count, numbers, weights, updates, so_far=None):
    vmem, whole = pl.BlockSpec(memory_space=pltpu.VMEM), pl.BlockSpec(memory_space=pltpu.HBM)
    operands = [weights, *updates] + ([] if so_far is None else [so_far])
    return pl.pallas_call(
        functools.partial(weights_kernel, rest_count, numbers),
        out_shape=jax.ShapeDtypeStruct(weights.shape, weights.dtype),
        in_specs=[vmem] * (1 + len(updates)) + ([] if so_far is None else [whole]),
        out_specs=whole,
        scratch_shapes=[
            pltpu.VMEM((len(numbers),) + weights.shape[2:], weights.dtype),
            pltpu.SemaphoreType.DMA((len(numbers),)),
        ],
        input_output_aliases={} if so_far is None else {len(operands) - 1: 0},
        compiler_params=pltpu.CompilerParams(vmem_limit_bytes=VMEM_BYTES),
    )(*operands)


def on_device(momentum, weights):
    order = momentum.shape[3]
    opt, layer = lax.axis_size("opt"), lax.axis_size("layer")
    rest_count = opt // 8
    rest_groups = [[group * rest_count + rest for rest in range(rest_count)] for group in range(8)]
    scale = float(layer * opt * momentum.shape[2])

    def regroup(array, split_axis, concat_axis):
        if rest_count == 1:
            return array
        return lax.all_to_all(
            array,
            "opt",
            split_axis=split_axis,
            concat_axis=concat_axis,
            axis_index_groups=rest_groups,
            tiled=True,
        )

    def swap(arrays, partners, back=False):
        permutes = swaps(opt, layer, partners)
        if back:
            permutes = [[(target, source) for source, target in permute] for permute in permutes]
        return [lax.ppermute(array, AXES, permute) for array, permute in zip(arrays, permutes)]

    spread = regroup(momentum[0], 0, 1)
    experts, row_count, _ = spread.shape
    by_block = (experts // 2, 2, row_count, order)
    blocks = (jax.ShapeDtypeStruct(by_block[2:], spread.dtype),) * (1 + len(ROWS))
    packed, message = packed_shape(order), message_shape(order)
    quarter = jax.ShapeDtypeStruct(packed.shape[1:], packed.dtype)

    own, *dealt = call(
        functools.partial(deal_kernel, rest_count),
        blocks,
        spread.reshape(by_block),
    )
    rows = [own] + swap(dealt, ROWS)
    first_row = jax.ShapeDtypeStruct((order // BLOCK, BLOCK, BLOCK), jnp.float32)
    direction = jax.ShapeDtypeStruct((BF16_TILE, order), jnp.bfloat16)
    early = call(early_gram_kernel, (packed, first_row), *rows[:EARLY])
    left, own_direction, *parts = call(
        functools.partial(gram_kernel, rest_count),
        (packed, direction) + (message,) * 3,
        *early,
        *rows[EARLY:],
    )
    total, directions, *rests = call(
        functools.partial(gather_kernel, rest_count, order),
        (quarter, direction) + (message,) * 3,
        left,
        own_direction,
        *swap(parts, OWNERS),
    )
    own_update, *updates = call(
        functools.partial(update_kernel, rest_count, order, scale),
        blocks,
        left,
        total,
        directions,
        *swap(rests, OWNERS),
        *rows,
        scratch=[pltpu.VMEM(packed.shape, packed.dtype)],
    )
    held = regroup(weights[0], 0, 1).reshape(by_block)
    returned = [own_update] + swap(updates, ROWS, back=True)
    numbers = range(len(blocks))
    fresh = new_weights(rest_count, numbers[:EARLY], held, returned[:EARLY])
    fresh = new_weights(rest_count, numbers[EARLY:], held, returned[EARLY:], fresh)
    return regroup(fresh.reshape(experts, row_count, order), 1, 0)[None]


def solution(mesh):
    in_specs = (P("layer", None, "opt", None), P("layer", None, "opt", None))
    out_specs = P("layer", None, "opt", None)
    return jax.shard_map(
        on_device, mesh=mesh, in_specs=in_specs, out_specs=out_specs, check_vma=False
    )
```

```python
import functools
import itertools

import jax
import jax.numpy as jnp
from jax import lax
from jax.experimental import pallas as pl
from jax.experimental.pallas import tpu as pltpu
from jax.sharding import PartitionSpec as P

ITERS = 3
BLOCK = 128
WIDE = 256
F32_TILE = 8
BF16_TILE = 16
SMALLEST = 1e-30
VMEM_BYTES = 48 << 20
EARLY = 5

first_coef = 3.4445
second_coef = -4.775
third_coef = 2.0315
epsilon = 1e-06
step_rate = 0.5
decay_rate = 0.1

AXES = ("opt", "layer")


def flips_of(z, y, x, pair=0, half=0):
    return (half, z, y, 0, x, pair)


def neighbour_steps():
    x, y, z = (0, 0, 1), (0, 1, 0), (1, 0, 0)
    order = [(x, y), (z, x), (y, z)]
    return [tuple(flips_of(*way, pair=cross) for way in step) for cross in (1, 0) for step in order]


ROWS = neighbour_steps() + [(flips_of(0, 0, 0, pair=1),) * 2]
BOTH, ANTIPODE, MIRROR = flips_of(0, 1, 1, half=1), flips_of(1, 1, 1), flips_of(1, 0, 0, half=1)
OWNERS = [(flips,) * 2 for flips in (BOTH, ANTIPODE, MIRROR)]


def colour_step(flips):
    return flips[4] ^ 2 * flips[2] ^ 3 * (flips[1] ^ flips[0])


def quarter_step(flips):
    return flips[4] + 2 * flips[0]


def swaps(opt, layer, partners):
    rest_count = opt // 8
    sizes = (2, 2, 2, rest_count, 2, 2)

    def device(half, z, y, rest, x, pair):
        return (((half * 2 + z) * 2 + y) * rest_count + rest) * layer + x * 2 + pair

    return [
        [
            (device(*spot), device(*(value ^ flip for value, flip in zip(spot, flips[spot[5]]))))
            for spot in itertools.product(*map(range, sizes))
        ]
        for flips in partners
    ]


def by_pair(pair, values):
    return values[0] + pair * (values[1] - values[0])


class Place:
    def __init__(self, rest_count):
        index = lax.axis_index("opt") // rest_count
        x, self.pair = lax.axis_index("layer") // 2, lax.axis_index("layer") % 2
        half, z, y = index // 4, index // 2 % 2, index % 2
        self.colour = x ^ (2 * y) ^ (3 * (z ^ half))
        self.quarter = x + 2 * half

    def block(self, number):
        if number == 0:
            return self.colour, self.pair
        flips = ROWS[number - 1]
        return self.colour ^ by_pair(self.pair, [colour_step(way) for way in flips]), self.pair ^ flips[0][5]

    def quarter_at(self, step):
        return self.quarter ^ by_pair(self.pair, [quarter_step(flips) for flips in OWNERS[step]])


def call(kernel, out_shape, *operands, scratch=()):
    vmem = pl.BlockSpec(memory_space=pltpu.VMEM)
    return pl.pallas_call(
        kernel,
        out_shape=out_shape,
        in_specs=[vmem] * len(operands),
        out_specs=jax.tree.map(lambda _: vmem, out_shape),
        scratch_shapes=list(scratch),
        compiler_params=pltpu.CompilerParams(vmem_limit_bytes=VMEM_BYTES),
    )(*operands)


def product(first, second):
    return jnp.dot(first, second, preferred_element_type=jnp.float32)


def quarters_of(order):
    count = order // BLOCK
    folds = [("fold", i, i + 1) for i in range(0, count, 2)]
    others = [("plain", i, j) for i in range(count) for j in range(i + 1, count)]
    length = (len(folds) + len(others)) // 4
    quarters = []
    for quarter in range(4):
        blocks = folds[quarter::4]
        missing = length - len(blocks)
        quarters.append(blocks + others[:missing])
        others = others[missing:]
    return quarters


def quarter_blocks(order):
    quarters = quarters_of(order)
    return max(sum(kind == "fold" for kind, _, _ in blocks) for blocks in quarters), len(quarters[0])


def packed_shape(order):
    return jax.ShapeDtypeStruct((4, quarter_blocks(order)[1] * BLOCK + F32_TILE, BLOCK), jnp.float32)


def message_shape(order):
    return jax.ShapeDtypeStruct((quarter_blocks(order)[1] * BLOCK + BF16_TILE, BLOCK), jnp.bfloat16)


def grid_ids():
    shape = (BLOCK, BLOCK)
    return lax.broadcasted_iota(jnp.int32, shape, 0), lax.broadcasted_iota(jnp.int32, shape, 1)


def diagonal(block):
    row_ids, column_ids = grid_ids()
    return jnp.sum(jnp.where(row_ids == column_ids, block, 0.0), axis=0, keepdims=True)


def padded(rows, height):
    missing = height - sum(row.shape[0] for row in rows)
    return jnp.concatenate(rows + [jnp.zeros((missing, BLOCK), jnp.float32)], axis=0)


def pack(block, order):
    row_ids, column_ids = grid_ids()
    result = []
    for blocks in quarters_of(order):
        tiles, rows = [], []
        for kind, i, j in blocks:
            if kind == "fold":
                second = block(j, j)
                tiles.append(jnp.where(row_ids <= column_ids, block(i, i), second))
                rows.append(diagonal(second))
            else:
                tiles.append(block(i, j))
        result.append(jnp.concatenate(tiles + [padded(rows, F32_TILE)], axis=0))
    return result


def unpack(quarters, order):
    row_ids, column_ids = grid_ids()
    result = {}
    for blocks, quarter in zip(quarters_of(order), quarters):
        tail = quarter[len(blocks) * BLOCK :]
        for k, (kind, i, j) in enumerate(blocks):
            tile = quarter[k * BLOCK : (k + 1) * BLOCK]
            if kind == "fold":
                mirrored = tile.T
                result[i, i] = jnp.where(row_ids <= column_ids, tile, mirrored)
                second = jnp.where(row_ids > column_ids, tile, mirrored)
                result[j, j] = jnp.where(row_ids == column_ids, tail[k : k + 1], second)
            else:
                result[i, j] = tile
    return result


def to_message(quarter, order, vector=None):
    fold_count, block_count = quarter_blocks(order)
    length = block_count * BLOCK
    body, tail = quarter[:length], quarter[length : length + fold_count]
    rounded_body = body.astype(jnp.bfloat16)
    rows = [
        diagonal(
            body[k * BLOCK : (k + 1) * BLOCK] - rounded_body[k * BLOCK : (k + 1) * BLOCK].astype(jnp.float32)
        )
        for k in range(fold_count)
    ]
    high = tail.astype(jnp.bfloat16).astype(jnp.float32)
    rows += [high, tail - high]
    if vector is not None:
        rows += [vector[:, k : k + BLOCK] for k in range(0, order, BLOCK)]
    return jnp.concatenate([rounded_body, padded(rows, BF16_TILE).astype(jnp.bfloat16)], axis=0)


def from_message(message, order):
    fold_count, block_count = quarter_blocks(order)
    length = block_count * BLOCK
    row_ids, column_ids = grid_ids()
    values = message.astype(jnp.float32)
    body, extra = values[:length], values[length:]
    tiles = [
        body[k * BLOCK : (k + 1) * BLOCK] + jnp.where(row_ids == column_ids, extra[k : k + 1], 0.0)
        for k in range(fold_count)
    ]
    tail = extra[fold_count : 2 * fold_count] + extra[2 * fold_count : 3 * fold_count]
    return jnp.concatenate(tiles + [body[fold_count * BLOCK :], padded([tail], F32_TILE)], axis=0)


def vector_of(message, order):
    fold_count, block_count = quarter_blocks(order)
    start = block_count * BLOCK + 3 * fold_count
    values = message.astype(jnp.float32)
    return jnp.concatenate([values[start + k : start + k + 1] for k in range(order // BLOCK)], axis=1)


def stacked(vectors):
    rows = jnp.concatenate(vectors, axis=0)
    filler = jnp.zeros((BF16_TILE - rows.shape[0], rows.shape[1]), jnp.float32)
    return jnp.concatenate([rows, filler], axis=0).astype(jnp.bfloat16)


def outer_products(vectors):
    order = vectors.shape[1]
    result = {}
    for start in range(0, order, BLOCK):
        band = lax.dot_general(
            vectors[:, start : start + BLOCK],
            vectors[:, start:],
            (((0,), (0,)), ((), ())),
            preferred_element_type=jnp.float32,
        )
        for offset in range(0, order - start, BLOCK):
            place = start // BLOCK, (start + offset) // BLOCK
            result[place] = band[:, offset : offset + BLOCK]
    return result


def main_direction(first_row):
    signs = jnp.where(first_row[0][:, :1] < 0.0, -1.0, 1.0)
    rows = [jnp.sum(signs * block, axis=0, keepdims=True) for block in first_row]
    size = jnp.sum(jnp.where(first_row[0][:1, :] < 0.0, -rows[0], rows[0]))
    growth = jnp.where(size > 0.0, lax.rsqrt(jnp.maximum(size, SMALLEST)), 0.0)
    return (jnp.concatenate(rows, axis=1) * growth).astype(jnp.bfloat16).astype(jnp.float32)


def deal_kernel(rest_count, momentum_ref, *refs):
    place = Place(rest_count)
    for number, block_ref in enumerate(refs):
        block_ref[...] = momentum_ref[place.block(number)]


def packed_gram(block_refs):
    rows = jnp.concatenate([block_ref[...] for block_ref in block_refs], axis=0)
    order = rows.shape[1]
    tiles = {}
    for row in range(0, order, WIDE):
        for column in range(row, order, WIDE):
            tiles[row, column] = lax.dot_general(
                rows[:, row : row + WIDE],
                rows[:, column : column + WIDE],
                (((0,), (0,)), ((), ())),
                preferred_element_type=jnp.float32,
            )

    def block(i, j):
        row, column = i * BLOCK, j * BLOCK
        tile = tiles[row // WIDE * WIDE, column // WIDE * WIDE]
        return tile[row % WIDE :, column % WIDE :][:BLOCK, :BLOCK]

    return pack(block, order), [block(0, k) for k in range(order // BLOCK)]


def early_gram_kernel(*refs):
    block_refs, packed_ref, first_row_ref = refs[:-2], refs[-2], refs[-1]
    packed, first_row = packed_gram(block_refs)
    for quarter, value in enumerate(packed):
        packed_ref[quarter] = value
    for number, value in enumerate(first_row):
        first_row_ref[number] = value


def gram_kernel(rest_count, early_ref, early_row_ref, *refs):
    block_refs, left_ref, direction_ref, message_refs = refs[:-5], refs[-5], refs[-4], refs[-3:]
    order = block_refs[0].shape[1]
    packed, first_row = packed_gram(block_refs)
    direction = main_direction([early_row_ref[number] + value for number, value in enumerate(first_row)])
    direction_ref[...] = stacked([direction])
    outer = outer_products(stacked([direction]))
    for quarter, (value, known) in enumerate(zip(packed, pack(lambda i, j: outer[i, j], order))):
        left_ref[quarter] = early_ref[quarter] + (value - known)
    place = Place(rest_count)
    for step, message_ref in enumerate(message_refs):
        message_ref[...] = to_message(left_ref[place.quarter_at(step)], order, direction)


def gather_kernel(rest_count, order, left_ref, direction_ref, *refs):
    arrived_refs, total_ref, directions_ref, message_refs = refs[:3], refs[3], refs[4], refs[5:]
    arrived = [from_message(arrived_ref[...], order) for arrived_ref in arrived_refs]
    total = left_ref[Place(rest_count).quarter] + (arrived[0] + (arrived[1] + arrived[2]))
    total_ref[...] = total
    for value, message_ref in zip(arrived, message_refs):
        message_ref[...] = to_message(total - value, order)
    own = direction_ref[...].astype(jnp.float32)[:1]
    directions_ref[...] = stacked([own] + [vector_of(arrived_ref[...], order) for arrived_ref in arrived_refs])


def assemble(upper, count):
    return jnp.concatenate(
        [
            jnp.concatenate([upper[i, j] if i <= j else upper[j, i].T for j in range(count)], axis=1)
            for i in range(count)
        ],
        axis=0,
    )


def rounded(upper, count):
    return assemble({key: value.astype(jnp.bfloat16) for key, value in upper.items()}, count)


def symmetric_product(first, second, count):
    size = first.shape[0] // count
    return {
        (i, j): product(first[i * size : (i + 1) * size, :], second[:, j * size : (j + 1) * size])
        for i in range(count)
        for j in range(i, count)
    }


def combine(*terms):
    return {
        key: functools.reduce(jnp.add, [value[key] if factor == 1.0 else factor * value[key] for factor, value in terms])
        for key in terms[0][1]
    }


def square_beside_diagonal(upper, count):
    shape = upper[0, 0].shape
    identity = lax.broadcasted_iota(jnp.int32, shape, 0) == lax.broadcasted_iota(jnp.int32, shape, 1)
    diagonals = [jnp.where(identity, upper[i, i], 0.0) for i in range(count)]
    columns = [jnp.sum(value, axis=1, keepdims=True) for value in diagonals]
    rows = [jnp.sum(value, axis=0, keepdims=True) for value in diagonals]
    beside = {
        (i, j): jnp.where(identity, 0.0, value) if i == j else value for (i, j), value in upper.items()
    }
    beside_high = rounded(beside, count)
    entries = {(i, j): (columns[i] + rows[j]) * value for (i, j), value in beside.items()}
    for i in range(count):
        entries[i, i] = entries[i, i] + diagonals[i] * diagonals[i]
    return combine((1.0, entries), (1.0, symmetric_product(beside_high, beside_high, count)))


def newton(current, count):
    accum_identity, accum = 1.0, None
    for iteration in range(ITERS):
        last = iteration + 1 == ITERS
        current_high = None if last else rounded(current, count)
        if last:
            squared = square_beside_diagonal(current, count)
        else:
            squared = symmetric_product(current_high, current_high, count)
        rest = combine((second_coef, current), (third_coef, squared))
        rest_high = rounded(rest, count)
        if not last:
            inner = symmetric_product(current_high, rest_high, count)
            current = combine(
                (first_coef * first_coef, current),
                (2.0 * first_coef, inner),
                (1.0, symmetric_product(rounded(inner, count), rest_high, count)),
            )
        if accum is None:
            accum = rest
        else:
            accum = combine(
                (accum_identity, rest),
                (first_coef, accum),
                (1.0, symmetric_product(rounded(accum, count), rest_high, count)),
            )
        accum_identity *= first_coef
    return accum_identity, accum


def update_kernel(rest_count, order, scale, left_ref, total_ref, directions_ref, *refs):
    rest_refs, quarters_ref = refs[:3], refs[-1]
    block_refs, update_refs = refs[3 : 3 + len(refs[4:]) // 2], refs[3 + len(refs[4:]) // 2 : -1]
    place = Place(rest_count)
    quarters_ref[place.quarter] = total_ref[...]
    for step, rest_ref in enumerate(rest_refs):
        quarter = place.quarter_at(step)
        quarters_ref[quarter] = left_ref[quarter] + from_message(rest_ref[...], order)
    outer = outer_products(directions_ref[...])
    blocks = {
        key: value + outer[key]
        for key, value in unpack([quarters_ref[quarter] for quarter in range(4)], order).items()
    }
    trace_sum = jnp.sum(sum(diagonal(blocks[i, i]) for i in range(order // BLOCK)))
    shrink = 1.0 / (trace_sum + epsilon)
    count, ratio = order // WIDE, WIDE // BLOCK
    current = {}
    for i in range(count):
        for j in range(i, count):
            tile = jnp.concatenate(
                [
                    jnp.concatenate(
                        [
                            blocks[row, column] if row <= column else blocks[column, row].T
                            for column in range(j * ratio, (j + 1) * ratio)
                        ],
                        axis=1,
                    )
                    for row in range(i * ratio, (i + 1) * ratio)
                ],
                axis=0,
            )
            current[i, j] = tile * shrink
    accum_identity, accum = newton(current, count)
    growth = jnp.sqrt(scale / (trace_sum + epsilon))
    shape = (WIDE, WIDE)
    identity = lax.broadcasted_iota(jnp.int32, shape, 0) == lax.broadcasted_iota(jnp.int32, shape, 1)
    factor = rounded(
        {
            (i, j): (value + jnp.where(identity, accum_identity, 0.0) if i == j else value) * growth
            for (i, j), value in accum.items()
        },
        count,
    )
    update = product(jnp.concatenate([block_ref[...] for block_ref in block_refs], axis=0), factor)
    row_count = block_refs[0].shape[0]
    for number, update_ref in enumerate(update_refs):
        update_ref[...] = update[number * row_count : (number + 1) * row_count].astype(update_ref.dtype)


def weights_kernel(rest_count, numbers, weights_ref, *refs):
    out_ref, fresh_ref, semaphores = refs[-3:]
    place = Place(rest_count)
    shrink = 1.0 - step_rate * decay_rate
    copies = []
    for slot, (number, update_ref) in enumerate(zip(numbers, refs)):
        block = place.block(number)
        fresh_ref[slot] = (
            shrink * weights_ref[block].astype(jnp.float32) - step_rate * update_ref[...].astype(jnp.float32)
        ).astype(fresh_ref.dtype)
        copies.append(pltpu.make_async_copy(fresh_ref.at[slot], out_ref.at[block], semaphores.at[slot]))
        copies[-1].start()
    for copy in copies:
        copy.wait()


def new_weights(rest_count, numbers, weights, updates, so_far=None):
    vmem, whole = pl.BlockSpec(memory_space=pltpu.VMEM), pl.BlockSpec(memory_space=pltpu.HBM)
    operands = [weights, *updates] + ([] if so_far is None else [so_far])
    return pl.pallas_call(
        functools.partial(weights_kernel, rest_count, numbers),
        out_shape=jax.ShapeDtypeStruct(weights.shape, weights.dtype),
        in_specs=[vmem] * (1 + len(updates)) + ([] if so_far is None else [whole]),
        out_specs=whole,
        scratch_shapes=[
            pltpu.VMEM((len(numbers),) + weights.shape[2:], weights.dtype),
            pltpu.SemaphoreType.DMA((len(numbers),)),
        ],
        input_output_aliases={} if so_far is None else {len(operands) - 1: 0},
        compiler_params=pltpu.CompilerParams(vmem_limit_bytes=VMEM_BYTES),
    )(*operands)


def on_device(momentum, weights):
    order = momentum.shape[3]
    opt, layer = lax.axis_size("opt"), lax.axis_size("layer")
    rest_count = opt // 8
    rest_groups = [[group * rest_count + rest for rest in range(rest_count)] for group in range(8)]
    scale = float(layer * opt * momentum.shape[2])

    def regroup(array, split_axis, concat_axis):
        if rest_count == 1:
            return array
        return lax.all_to_all(
            array,
            "opt",
            split_axis=split_axis,
            concat_axis=concat_axis,
            axis_index_groups=rest_groups,
            tiled=True,
        )

    def swap(arrays, partners, back=False):
        permutes = swaps(opt, layer, partners)
        if back:
            permutes = [[(target, source) for source, target in permute] for permute in permutes]
        return [lax.ppermute(array, AXES, permute) for array, permute in zip(arrays, permutes)]

    spread = regroup(momentum[0], 0, 1)
    experts, row_count, _ = spread.shape
    by_block = (experts // 2, 2, row_count, order)
    blocks = (jax.ShapeDtypeStruct(by_block[2:], spread.dtype),) * (1 + len(ROWS))
    packed, message = packed_shape(order), message_shape(order)
    quarter = jax.ShapeDtypeStruct(packed.shape[1:], packed.dtype)

    own, *dealt = call(
        functools.partial(deal_kernel, rest_count),
        blocks,
        spread.reshape(by_block),
    )
    rows = [own] + swap(dealt, ROWS)
    first_row = jax.ShapeDtypeStruct((order // BLOCK, BLOCK, BLOCK), jnp.float32)
    direction = jax.ShapeDtypeStruct((BF16_TILE, order), jnp.bfloat16)
    early = call(early_gram_kernel, (packed, first_row), *rows[:EARLY])
    left, own_direction, *parts = call(
        functools.partial(gram_kernel, rest_count),
        (packed, direction) + (message,) * 3,
        *early,
        *rows[EARLY:],
    )
    total, directions, *rests = call(
        functools.partial(gather_kernel, rest_count, order),
        (quarter, direction) + (message,) * 3,
        left,
        own_direction,
        *swap(parts, OWNERS),
    )
    own_update, *updates = call(
        functools.partial(update_kernel, rest_count, order, scale),
        blocks,
        left,
        total,
        directions,
        *swap(rests, OWNERS),
        *rows,
        scratch=[pltpu.VMEM(packed.shape, packed.dtype)],
    )
    held = regroup(weights[0], 0, 1).reshape(by_block)
    returned = [own_update] + swap(updates, ROWS, back=True)
    numbers = range(len(blocks))
    fresh = new_weights(rest_count, numbers[:EARLY], held, returned[:EARLY])
    fresh = new_weights(rest_count, numbers[EARLY:], held, returned[EARLY:], fresh)
    return regroup(fresh.reshape(experts, row_count, order), 1, 0)[None]


def solution(mesh):
    in_specs = (P("layer", None, "opt", None), P("layer", None, "opt", None))
    out_specs = P("layer", None, "opt", None)
    return jax.shard_map(
        on_device, mesh=mesh, in_specs=in_specs, out_specs=out_specs, check_vma=False
    )
```

```python
import functools
import itertools

import jax
import jax.numpy as jnp
from jax import lax
from jax.experimental import pallas as pl
from jax.experimental.pallas import tpu as pltpu
from jax.sharding import PartitionSpec as P

ITERS = 3
BLOCK = 128
WIDE = 256
F32_TILE = 8
BF16_TILE = 16
SMALLEST = 1e-30
VMEM_BYTES = 48 << 20
EARLY = 5

first_coef = 3.4445
second_coef = -4.775
third_coef = 2.0315
epsilon = 1e-06
step_rate = 0.5
decay_rate = 0.1

AXES = ("opt", "layer")


def flips_of(z, y, x, pair=0, half=0):
    return (half, z, y, 0, x, pair)


def neighbour_steps():
    x, y, z = (0, 0, 1), (0, 1, 0), (1, 0, 0)
    order = [(x, y), (z, x), (y, z)]
    return [tuple(flips_of(*way, pair=cross) for way in step) for cross in (1, 0) for step in order]


ROWS = neighbour_steps() + [(flips_of(0, 0, 0, pair=1),) * 2]
BOTH, ANTIPODE, MIRROR = flips_of(0, 1, 1, half=1), flips_of(1, 1, 1), flips_of(1, 0, 0, half=1)
OWNERS = [(flips,) * 2 for flips in (BOTH, ANTIPODE, MIRROR)]


def colour_step(flips):
    return flips[4] ^ 2 * flips[2] ^ 3 * (flips[1] ^ flips[0])


def quarter_step(flips):
    return flips[4] + 2 * flips[0]


def swaps(opt, layer, partners):
    rest_count = opt // 8
    sizes = (2, 2, 2, rest_count, 2, 2)

    def device(half, z, y, rest, x, pair):
        return (((half * 2 + z) * 2 + y) * rest_count + rest) * layer + x * 2 + pair

    return [
        [
            (device(*spot), device(*(value ^ flip for value, flip in zip(spot, flips[spot[5]]))))
            for spot in itertools.product(*map(range, sizes))
        ]
        for flips in partners
    ]


def by_pair(pair, values):
    return values[0] + pair * (values[1] - values[0])


class Place:
    def __init__(self, rest_count):
        index = lax.axis_index("opt") // rest_count
        x, self.pair = lax.axis_index("layer") // 2, lax.axis_index("layer") % 2
        half, z, y = index // 4, index // 2 % 2, index % 2
        self.colour = x ^ (2 * y) ^ (3 * (z ^ half))
        self.quarter = x + 2 * half

    def block(self, number):
        if number == 0:
            return self.colour, self.pair
        flips = ROWS[number - 1]
        return self.colour ^ by_pair(self.pair, [colour_step(way) for way in flips]), self.pair ^ flips[0][5]

    def quarter_at(self, step):
        return self.quarter ^ by_pair(self.pair, [quarter_step(flips) for flips in OWNERS[step]])


def call(kernel, out_shape, *operands, scratch=()):
    vmem = pl.BlockSpec(memory_space=pltpu.VMEM)
    return pl.pallas_call(
        kernel,
        out_shape=out_shape,
        in_specs=[vmem] * len(operands),
        out_specs=jax.tree.map(lambda _: vmem, out_shape),
        scratch_shapes=list(scratch),
        compiler_params=pltpu.CompilerParams(vmem_limit_bytes=VMEM_BYTES),
    )(*operands)


def product(first, second):
    return jnp.dot(first, second, preferred_element_type=jnp.float32)


def quarters_of(order):
    count = order // BLOCK
    folds = [("fold", i, i + 1) for i in range(0, count, 2)]
    others = [("plain", i, j) for i in range(count) for j in range(i + 1, count)]
    length = (len(folds) + len(others)) // 4
    quarters = []
    for quarter in range(4):
        blocks = folds[quarter::4]
        missing = length - len(blocks)
        quarters.append(blocks + others[:missing])
        others = others[missing:]
    return quarters


def quarter_blocks(order):
    quarters = quarters_of(order)
    return max(sum(kind == "fold" for kind, _, _ in blocks) for blocks in quarters), len(quarters[0])


def packed_shape(order):
    return jax.ShapeDtypeStruct((4, quarter_blocks(order)[1] * BLOCK + F32_TILE, BLOCK), jnp.float32)


def message_shape(order):
    return jax.ShapeDtypeStruct((quarter_blocks(order)[1] * BLOCK + BF16_TILE, BLOCK), jnp.bfloat16)


def grid_ids():
    shape = (BLOCK, BLOCK)
    return lax.broadcasted_iota(jnp.int32, shape, 0), lax.broadcasted_iota(jnp.int32, shape, 1)


def diagonal(block):
    row_ids, column_ids = grid_ids()
    return jnp.sum(jnp.where(row_ids == column_ids, block, 0.0), axis=0, keepdims=True)


def padded(rows, height):
    missing = height - sum(row.shape[0] for row in rows)
    return jnp.concatenate(rows + [jnp.zeros((missing, BLOCK), jnp.float32)], axis=0)


def pack(block, order):
    row_ids, column_ids = grid_ids()
    result = []
    for blocks in quarters_of(order):
        tiles, rows = [], []
        for kind, i, j in blocks:
            if kind == "fold":
                second = block(j, j)
                tiles.append(jnp.where(row_ids <= column_ids, block(i, i), second))
                rows.append(diagonal(second))
            else:
                tiles.append(block(i, j))
        result.append(jnp.concatenate(tiles + [padded(rows, F32_TILE)], axis=0))
    return result


def unpack(quarters, order):
    row_ids, column_ids = grid_ids()
    result = {}
    for blocks, quarter in zip(quarters_of(order), quarters):
        tail = quarter[len(blocks) * BLOCK :]
        for k, (kind, i, j) in enumerate(blocks):
            tile = quarter[k * BLOCK : (k + 1) * BLOCK]
            if kind == "fold":
                mirrored = tile.T
                result[i, i] = jnp.where(row_ids <= column_ids, tile, mirrored)
                second = jnp.where(row_ids > column_ids, tile, mirrored)
                result[j, j] = jnp.where(row_ids == column_ids, tail[k : k + 1], second)
            else:
                result[i, j] = tile
    return result


def to_message(quarter, order, vector=None):
    fold_count, block_count = quarter_blocks(order)
    length = block_count * BLOCK
    body, tail = quarter[:length], quarter[length : length + fold_count]
    rounded_body = body.astype(jnp.bfloat16)
    rows = [
        diagonal(
            body[k * BLOCK : (k + 1) * BLOCK] - rounded_body[k * BLOCK : (k + 1) * BLOCK].astype(jnp.float32)
        )
        for k in range(fold_count)
    ]
    high = tail.astype(jnp.bfloat16).astype(jnp.float32)
    rows += [high, tail - high]
    if vector is not None:
        rows += [vector[:, k : k + BLOCK] for k in range(0, order, BLOCK)]
    return jnp.concatenate([rounded_body, padded(rows, BF16_TILE).astype(jnp.bfloat16)], axis=0)


def from_message(message, order):
    fold_count, block_count = quarter_blocks(order)
    length = block_count * BLOCK
    row_ids, column_ids = grid_ids()
    values = message.astype(jnp.float32)
    body, extra = values[:length], values[length:]
    tiles = [
        body[k * BLOCK : (k + 1) * BLOCK] + jnp.where(row_ids == column_ids, extra[k : k + 1], 0.0)
        for k in range(fold_count)
    ]
    tail = extra[fold_count : 2 * fold_count] + extra[2 * fold_count : 3 * fold_count]
    return jnp.concatenate(tiles + [body[fold_count * BLOCK :], padded([tail], F32_TILE)], axis=0)


def vector_of(message, order):
    fold_count, block_count = quarter_blocks(order)
    start = block_count * BLOCK + 3 * fold_count
    values = message.astype(jnp.float32)
    return jnp.concatenate([values[start + k : start + k + 1] for k in range(order // BLOCK)], axis=1)


def stacked(vectors):
    rows = jnp.concatenate(vectors, axis=0)
    filler = jnp.zeros((BF16_TILE - rows.shape[0], rows.shape[1]), jnp.float32)
    return jnp.concatenate([rows, filler], axis=0).astype(jnp.bfloat16)


def outer_products(vectors):
    order = vectors.shape[1]
    result = {}
    for start in range(0, order, BLOCK):
        band = lax.dot_general(
            vectors[:, start : start + BLOCK],
            vectors[:, start:],
            (((0,), (0,)), ((), ())),
            preferred_element_type=jnp.float32,
        )
        for offset in range(0, order - start, BLOCK):
            place = start // BLOCK, (start + offset) // BLOCK
            result[place] = band[:, offset : offset + BLOCK]
    return result


def main_direction(first_row, share):
    signs = jnp.where(first_row[0][:, :1] < 0.0, -1.0, 1.0)
    rows = [jnp.sum(signs * block, axis=0, keepdims=True) for block in first_row]
    size = jnp.sum(jnp.where(first_row[0][:1, :] < 0.0, -rows[0], rows[0]))
    growth = jnp.where(size > 0.0, lax.rsqrt(jnp.maximum(share * size, SMALLEST)), 0.0)
    return (jnp.concatenate(rows, axis=1) * growth).astype(jnp.bfloat16).astype(jnp.float32)


def deal_kernel(rest_count, momentum_ref, *refs):
    place = Place(rest_count)
    for number, block_ref in enumerate(refs):
        block_ref[...] = momentum_ref[place.block(number)]


def packed_gram(block_refs):
    rows = jnp.concatenate([block_ref[...] for block_ref in block_refs], axis=0)
    order = rows.shape[1]
    tiles = {}
    for row in range(0, order, WIDE):
        for column in range(row, order, WIDE):
            tiles[row, column] = lax.dot_general(
                rows[:, row : row + WIDE],
                rows[:, column : column + WIDE],
                (((0,), (0,)), ((), ())),
                preferred_element_type=jnp.float32,
            )

    def block(i, j):
        row, column = i * BLOCK, j * BLOCK
        tile = tiles[row // WIDE * WIDE, column // WIDE * WIDE]
        return tile[row % WIDE :, column % WIDE :][:BLOCK, :BLOCK]

    return pack(block, order), [block(0, k) for k in range(order // BLOCK)]


def early_gram_kernel(share, *refs):
    block_refs, left_ref, direction_ref = refs[:-2], refs[-2], refs[-1]
    order = block_refs[0].shape[1]
    packed, first_row = packed_gram(block_refs)
    direction = main_direction(first_row, share)
    direction_ref[...] = stacked([direction])
    outer = outer_products(stacked([direction]))
    for quarter, (value, known) in enumerate(zip(packed, pack(lambda i, j: outer[i, j], order))):
        left_ref[quarter] = value - known


def gram_kernel(rest_count, early_ref, direction_ref, *refs):
    block_refs, left_ref, message_refs = refs[:-4], refs[-4], refs[-3:]
    order = block_refs[0].shape[1]
    for quarter, value in enumerate(packed_gram(block_refs)[0]):
        left_ref[quarter] = early_ref[quarter] + value
    place = Place(rest_count)
    direction = direction_ref[...].astype(jnp.float32)[:1]
    for step, message_ref in enumerate(message_refs):
        message_ref[...] = to_message(left_ref[place.quarter_at(step)], order, direction)


def gather_kernel(rest_count, order, left_ref, direction_ref, *refs):
    arrived_refs, total_ref, directions_ref, message_refs = refs[:3], refs[3], refs[4], refs[5:]
    arrived = [from_message(arrived_ref[...], order) for arrived_ref in arrived_refs]
    total = left_ref[Place(rest_count).quarter] + (arrived[0] + (arrived[1] + arrived[2]))
    total_ref[...] = total
    for value, message_ref in zip(arrived, message_refs):
        message_ref[...] = to_message(total - value, order)
    own = direction_ref[...].astype(jnp.float32)[:1]
    directions_ref[...] = stacked([own] + [vector_of(arrived_ref[...], order) for arrived_ref in arrived_refs])


def assemble(upper, count):
    return jnp.concatenate(
        [
            jnp.concatenate([upper[i, j] if i <= j else upper[j, i].T for j in range(count)], axis=1)
            for i in range(count)
        ],
        axis=0,
    )


def rounded(upper, count):
    return assemble({key: value.astype(jnp.bfloat16) for key, value in upper.items()}, count)


def symmetric_product(first, second, count):
    size = first.shape[0] // count
    return {
        (i, j): product(first[i * size : (i + 1) * size, :], second[:, j * size : (j + 1) * size])
        for i in range(count)
        for j in range(i, count)
    }


def combine(*terms):
    return {
        key: functools.reduce(jnp.add, [value[key] if factor == 1.0 else factor * value[key] for factor, value in terms])
        for key in terms[0][1]
    }


def square_beside_diagonal(upper, count):
    shape = upper[0, 0].shape
    identity = lax.broadcasted_iota(jnp.int32, shape, 0) == lax.broadcasted_iota(jnp.int32, shape, 1)
    diagonals = [jnp.where(identity, upper[i, i], 0.0) for i in range(count)]
    columns = [jnp.sum(value, axis=1, keepdims=True) for value in diagonals]
    rows = [jnp.sum(value, axis=0, keepdims=True) for value in diagonals]
    beside = {
        (i, j): jnp.where(identity, 0.0, value) if i == j else value for (i, j), value in upper.items()
    }
    beside_high = rounded(beside, count)
    entries = {(i, j): (columns[i] + rows[j]) * value for (i, j), value in beside.items()}
    for i in range(count):
        entries[i, i] = entries[i, i] + diagonals[i] * diagonals[i]
    return combine((1.0, entries), (1.0, symmetric_product(beside_high, beside_high, count)))


def newton(current, count):
    accum_identity, accum = 1.0, None
    for iteration in range(ITERS):
        last = iteration + 1 == ITERS
        current_high = None if last else rounded(current, count)
        if last:
            squared = square_beside_diagonal(current, count)
        else:
            squared = symmetric_product(current_high, current_high, count)
        rest = combine((second_coef, current), (third_coef, squared))
        rest_high = rounded(rest, count)
        if not last:
            inner = symmetric_product(current_high, rest_high, count)
            current = combine(
                (first_coef * first_coef, current),
                (2.0 * first_coef, inner),
                (1.0, symmetric_product(rounded(inner, count), rest_high, count)),
            )
        if accum is None:
            accum = rest
        else:
            accum = combine(
                (accum_identity, rest),
                (first_coef, accum),
                (1.0, symmetric_product(rounded(accum, count), rest_high, count)),
            )
        accum_identity *= first_coef
    return accum_identity, accum


def update_kernel(rest_count, order, scale, left_ref, total_ref, directions_ref, *refs):
    rest_refs, quarters_ref = refs[:3], refs[-1]
    block_refs, update_refs = refs[3 : 3 + len(refs[4:]) // 2], refs[3 + len(refs[4:]) // 2 : -1]
    place = Place(rest_count)
    quarters_ref[place.quarter] = total_ref[...]
    for step, rest_ref in enumerate(rest_refs):
        quarter = place.quarter_at(step)
        quarters_ref[quarter] = left_ref[quarter] + from_message(rest_ref[...], order)
    outer = outer_products(directions_ref[...])
    blocks = {
        key: value + outer[key]
        for key, value in unpack([quarters_ref[quarter] for quarter in range(4)], order).items()
    }
    trace_sum = jnp.sum(sum(diagonal(blocks[i, i]) for i in range(order // BLOCK)))
    shrink = 1.0 / (trace_sum + epsilon)
    count, ratio = order // WIDE, WIDE // BLOCK
    current = {}
    for i in range(count):
        for j in range(i, count):
            tile = jnp.concatenate(
                [
                    jnp.concatenate(
                        [
                            blocks[row, column] if row <= column else blocks[column, row].T
                            for column in range(j * ratio, (j + 1) * ratio)
                        ],
                        axis=1,
                    )
                    for row in range(i * ratio, (i + 1) * ratio)
                ],
                axis=0,
            )
            current[i, j] = tile * shrink
    accum_identity, accum = newton(current, count)
    growth = jnp.sqrt(scale / (trace_sum + epsilon))
    shape = (WIDE, WIDE)
    identity = lax.broadcasted_iota(jnp.int32, shape, 0) == lax.broadcasted_iota(jnp.int32, shape, 1)
    factor = rounded(
        {
            (i, j): (value + jnp.where(identity, accum_identity, 0.0) if i == j else value) * growth
            for (i, j), value in accum.items()
        },
        count,
    )
    update = product(jnp.concatenate([block_ref[...] for block_ref in block_refs], axis=0), factor)
    row_count = block_refs[0].shape[0]
    for number, update_ref in enumerate(update_refs):
        update_ref[...] = update[number * row_count : (number + 1) * row_count].astype(update_ref.dtype)


def weights_kernel(rest_count, numbers, weights_ref, *refs):
    out_ref, fresh_ref, semaphores = refs[-3:]
    place = Place(rest_count)
    shrink = 1.0 - step_rate * decay_rate
    copies = []
    for slot, (number, update_ref) in enumerate(zip(numbers, refs)):
        block = place.block(number)
        fresh_ref[slot] = (
            shrink * weights_ref[block].astype(jnp.float32) - step_rate * update_ref[...].astype(jnp.float32)
        ).astype(fresh_ref.dtype)
        copies.append(pltpu.make_async_copy(fresh_ref.at[slot], out_ref.at[block], semaphores.at[slot]))
        copies[-1].start()
    for copy in copies:
        copy.wait()


def new_weights(rest_count, numbers, weights, updates, so_far=None):
    vmem, whole = pl.BlockSpec(memory_space=pltpu.VMEM), pl.BlockSpec(memory_space=pltpu.HBM)
    operands = [weights, *updates] + ([] if so_far is None else [so_far])
    return pl.pallas_call(
        functools.partial(weights_kernel, rest_count, numbers),
        out_shape=jax.ShapeDtypeStruct(weights.shape, weights.dtype),
        in_specs=[vmem] * (1 + len(updates)) + ([] if so_far is None else [whole]),
        out_specs=whole,
        scratch_shapes=[
            pltpu.VMEM((len(numbers),) + weights.shape[2:], weights.dtype),
            pltpu.SemaphoreType.DMA((len(numbers),)),
        ],
        input_output_aliases={} if so_far is None else {len(operands) - 1: 0},
        compiler_params=pltpu.CompilerParams(vmem_limit_bytes=VMEM_BYTES),
    )(*operands)


def on_device(momentum, weights):
    order = momentum.shape[3]
    opt, layer = lax.axis_size("opt"), lax.axis_size("layer")
    rest_count = opt // 8
    rest_groups = [[group * rest_count + rest for rest in range(rest_count)] for group in range(8)]
    scale = float(layer * opt * momentum.shape[2])

    def regroup(array, split_axis, concat_axis):
        if rest_count == 1:
            return array
        return lax.all_to_all(
            array,
            "opt",
            split_axis=split_axis,
            concat_axis=concat_axis,
            axis_index_groups=rest_groups,
            tiled=True,
        )

    def swap(arrays, partners, back=False):
        permutes = swaps(opt, layer, partners)
        if back:
            permutes = [[(target, source) for source, target in permute] for permute in permutes]
        return [lax.ppermute(array, AXES, permute) for array, permute in zip(arrays, permutes)]

    spread = regroup(momentum[0], 0, 1)
    experts, row_count, _ = spread.shape
    by_block = (experts // 2, 2, row_count, order)
    blocks = (jax.ShapeDtypeStruct(by_block[2:], spread.dtype),) * (1 + len(ROWS))
    packed, message = packed_shape(order), message_shape(order)
    quarter = jax.ShapeDtypeStruct(packed.shape[1:], packed.dtype)

    own, *dealt = call(
        functools.partial(deal_kernel, rest_count),
        blocks,
        spread.reshape(by_block),
    )
    rows = [own] + swap(dealt, ROWS)
    direction = jax.ShapeDtypeStruct((BF16_TILE, order), jnp.bfloat16)
    early_left, own_direction = call(
        functools.partial(early_gram_kernel, EARLY / len(rows)), (packed, direction), *rows[:EARLY]
    )
    left, *parts = call(
        functools.partial(gram_kernel, rest_count),
        (packed,) + (message,) * 3,
        early_left,
        own_direction,
        *rows[EARLY:],
    )
    total, directions, *rests = call(
        functools.partial(gather_kernel, rest_count, order),
        (quarter, direction) + (message,) * 3,
        left,
        own_direction,
        *swap(parts, OWNERS),
    )
    own_update, *updates = call(
        functools.partial(update_kernel, rest_count, order, scale),
        blocks,
        left,
        total,
        directions,
        *swap(rests, OWNERS),
        *rows,
        scratch=[pltpu.VMEM(packed.shape, packed.dtype)],
    )
    held = regroup(weights[0], 0, 1).reshape(by_block)
    returned = [own_update] + swap(updates, ROWS, back=True)
    numbers = range(len(blocks))
    fresh = new_weights(rest_count, numbers[:EARLY], held, returned[:EARLY])
    fresh = new_weights(rest_count, numbers[EARLY:], held, returned[EARLY:], fresh)
    return regroup(fresh.reshape(experts, row_count, order), 1, 0)[None]


def solution(mesh):
    in_specs = (P("layer", None, "opt", None), P("layer", None, "opt", None))
    out_specs = P("layer", None, "opt", None)
    return jax.shard_map(
        on_device, mesh=mesh, in_specs=in_specs, out_specs=out_specs, check_vma=False
    )
```

```python
import functools
import itertools

import jax
import jax.numpy as jnp
from jax import lax
from jax.experimental import pallas as pl
from jax.experimental.pallas import tpu as pltpu
from jax.sharding import PartitionSpec as P

ITERS = 3
BLOCK = 128
WIDE = 256
F32_TILE = 8
BF16_TILE = 16
SMALLEST = 1e-30
VMEM_BYTES = 48 << 20
EARLY = 5

first_coef = 3.4445
second_coef = -4.775
third_coef = 2.0315
epsilon = 1e-06
step_rate = 0.5
decay_rate = 0.1

AXES = ("opt", "layer")


def flips_of(z, y, x, pair=0, half=0):
    return (half, z, y, 0, x, pair)


def neighbour_steps():
    x, y, z = (0, 0, 1), (0, 1, 0), (1, 0, 0)
    order = [(x, y), (z, x), (y, z)]
    return [tuple(flips_of(*way, pair=cross) for way in step) for cross in (1, 0) for step in order]


ROWS = neighbour_steps() + [(flips_of(0, 0, 0, pair=1),) * 2]
BOTH, ANTIPODE, MIRROR = flips_of(0, 1, 1, half=1), flips_of(1, 1, 1), flips_of(1, 0, 0, half=1)
OWNERS = [(flips,) * 2 for flips in (BOTH, ANTIPODE, MIRROR)]


def colour_step(flips):
    return flips[4] ^ 2 * flips[2] ^ 3 * (flips[1] ^ flips[0])


def quarter_step(flips):
    return flips[4] + 2 * flips[0]


def swaps(opt, layer, partners):
    rest_count = opt // 8
    sizes = (2, 2, 2, rest_count, 2, 2)

    def device(half, z, y, rest, x, pair):
        return (((half * 2 + z) * 2 + y) * rest_count + rest) * layer + x * 2 + pair

    return [
        [
            (device(*spot), device(*(value ^ flip for value, flip in zip(spot, flips[spot[5]]))))
            for spot in itertools.product(*map(range, sizes))
        ]
        for flips in partners
    ]


def by_pair(pair, values):
    return values[0] + pair * (values[1] - values[0])


class Place:
    def __init__(self, rest_count):
        index = lax.axis_index("opt") // rest_count
        x, self.pair = lax.axis_index("layer") // 2, lax.axis_index("layer") % 2
        half, z, y = index // 4, index // 2 % 2, index % 2
        self.colour = x ^ (2 * y) ^ (3 * (z ^ half))
        self.quarter = x + 2 * half

    def block(self, number):
        if number == 0:
            return self.colour, self.pair
        flips = ROWS[number - 1]
        return self.colour ^ by_pair(self.pair, [colour_step(way) for way in flips]), self.pair ^ flips[0][5]

    def quarter_at(self, step):
        return self.quarter ^ by_pair(self.pair, [quarter_step(flips) for flips in OWNERS[step]])


def call(kernel, out_shape, *operands, scratch=()):
    vmem = pl.BlockSpec(memory_space=pltpu.VMEM)
    return pl.pallas_call(
        kernel,
        out_shape=out_shape,
        in_specs=[vmem] * len(operands),
        out_specs=jax.tree.map(lambda _: vmem, out_shape),
        scratch_shapes=list(scratch),
        compiler_params=pltpu.CompilerParams(vmem_limit_bytes=VMEM_BYTES),
    )(*operands)


def product(first, second):
    return jnp.dot(first, second, preferred_element_type=jnp.float32)


def quarters_of(order):
    count = order // BLOCK
    folds = [("fold", i, i + 1) for i in range(0, count, 2)]
    others = [("plain", i, j) for i in range(count) for j in range(i + 1, count)]
    length = (len(folds) + len(others)) // 4
    quarters = []
    for quarter in range(4):
        blocks = folds[quarter::4]
        missing = length - len(blocks)
        quarters.append(blocks + others[:missing])
        others = others[missing:]
    return quarters


def quarter_blocks(order):
    quarters = quarters_of(order)
    return max(sum(kind == "fold" for kind, _, _ in blocks) for blocks in quarters), len(quarters[0])


def packed_shape(order):
    return jax.ShapeDtypeStruct((4, quarter_blocks(order)[1] * BLOCK + F32_TILE, BLOCK), jnp.float32)


def message_shape(order):
    return jax.ShapeDtypeStruct((quarter_blocks(order)[1] * BLOCK + BF16_TILE, BLOCK), jnp.bfloat16)


def grid_ids():
    shape = (BLOCK, BLOCK)
    return lax.broadcasted_iota(jnp.int32, shape, 0), lax.broadcasted_iota(jnp.int32, shape, 1)


def diagonal(block):
    row_ids, column_ids = grid_ids()
    return jnp.sum(jnp.where(row_ids == column_ids, block, 0.0), axis=0, keepdims=True)


def padded(rows, height):
    missing = height - sum(row.shape[0] for row in rows)
    return jnp.concatenate(rows + [jnp.zeros((missing, BLOCK), jnp.float32)], axis=0)


def pack(block, order):
    row_ids, column_ids = grid_ids()
    result = []
    for blocks in quarters_of(order):
        tiles, rows = [], []
        for kind, i, j in blocks:
            if kind == "fold":
                second = block(j, j)
                tiles.append(jnp.where(row_ids <= column_ids, block(i, i), second))
                rows.append(diagonal(second))
            else:
                tiles.append(block(i, j))
        result.append(jnp.concatenate(tiles + [padded(rows, F32_TILE)], axis=0))
    return result


def unpack(quarters, order):
    row_ids, column_ids = grid_ids()
    result = {}
    for blocks, quarter in zip(quarters_of(order), quarters):
        tail = quarter[len(blocks) * BLOCK :]
        for k, (kind, i, j) in enumerate(blocks):
            tile = quarter[k * BLOCK : (k + 1) * BLOCK]
            if kind == "fold":
                mirrored = tile.T
                result[i, i] = jnp.where(row_ids <= column_ids, tile, mirrored)
                second = jnp.where(row_ids > column_ids, tile, mirrored)
                result[j, j] = jnp.where(row_ids == column_ids, tail[k : k + 1], second)
            else:
                result[i, j] = tile
    return result


def to_message(quarter, order, vector=None):
    fold_count, block_count = quarter_blocks(order)
    length = block_count * BLOCK
    body, tail = quarter[:length], quarter[length : length + fold_count]
    rounded_body = body.astype(jnp.bfloat16)
    rows = [
        diagonal(
            body[k * BLOCK : (k + 1) * BLOCK] - rounded_body[k * BLOCK : (k + 1) * BLOCK].astype(jnp.float32)
        )
        for k in range(fold_count)
    ]
    high = tail.astype(jnp.bfloat16).astype(jnp.float32)
    rows += [high, tail - high]
    if vector is not None:
        rows += [vector[:, k : k + BLOCK] for k in range(0, order, BLOCK)]
    return jnp.concatenate([rounded_body, padded(rows, BF16_TILE).astype(jnp.bfloat16)], axis=0)


def from_message(message, order):
    fold_count, block_count = quarter_blocks(order)
    length = block_count * BLOCK
    row_ids, column_ids = grid_ids()
    values = message.astype(jnp.float32)
    body, extra = values[:length], values[length:]
    tiles = [
        body[k * BLOCK : (k + 1) * BLOCK] + jnp.where(row_ids == column_ids, extra[k : k + 1], 0.0)
        for k in range(fold_count)
    ]
    tail = extra[fold_count : 2 * fold_count] + extra[2 * fold_count : 3 * fold_count]
    return jnp.concatenate(tiles + [body[fold_count * BLOCK :], padded([tail], F32_TILE)], axis=0)


def vector_of(message, order):
    fold_count, block_count = quarter_blocks(order)
    start = block_count * BLOCK + 3 * fold_count
    values = message.astype(jnp.float32)
    return jnp.concatenate([values[start + k : start + k + 1] for k in range(order // BLOCK)], axis=1)


def stacked(vectors):
    rows = jnp.concatenate(vectors, axis=0)
    filler = jnp.zeros((BF16_TILE - rows.shape[0], rows.shape[1]), jnp.float32)
    return jnp.concatenate([rows, filler], axis=0).astype(jnp.bfloat16)


def outer_products(vectors):
    order = vectors.shape[1]
    result = {}
    for start in range(0, order, BLOCK):
        band = lax.dot_general(
            vectors[:, start : start + BLOCK],
            vectors[:, start:],
            (((0,), (0,)), ((), ())),
            preferred_element_type=jnp.float32,
        )
        for offset in range(0, order - start, BLOCK):
            place = start // BLOCK, (start + offset) // BLOCK
            result[place] = band[:, offset : offset + BLOCK]
    return result


def main_direction(first_row, share):
    signs = jnp.where(first_row[0][:, :1] < 0.0, -1.0, 1.0)
    rows = [jnp.sum(signs * block, axis=0, keepdims=True) for block in first_row]
    size = jnp.sum(jnp.where(first_row[0][:1, :] < 0.0, -rows[0], rows[0]))
    growth = jnp.where(size > 0.0, lax.rsqrt(jnp.maximum(share * size, SMALLEST)), 0.0)
    return (jnp.concatenate(rows, axis=1) * growth).astype(jnp.bfloat16).astype(jnp.float32)


def deal_kernel(rest_count, momentum_ref, *refs):
    place = Place(rest_count)
    for number, block_ref in enumerate(refs):
        block_ref[...] = momentum_ref[place.block(number)]


def packed_gram(block_refs):
    rows = jnp.concatenate([block_ref[...] for block_ref in block_refs], axis=0)
    order = rows.shape[1]
    tiles = {}
    for row in range(0, order, WIDE):
        for column in range(row, order, WIDE):
            tiles[row, column] = lax.dot_general(
                rows[:, row : row + WIDE],
                rows[:, column : column + WIDE],
                (((0,), (0,)), ((), ())),
                preferred_element_type=jnp.float32,
            )

    def block(i, j):
        row, column = i * BLOCK, j * BLOCK
        tile = tiles[row // WIDE * WIDE, column // WIDE * WIDE]
        return tile[row % WIDE :, column % WIDE :][:BLOCK, :BLOCK]

    return pack(block, order), [block(0, k) for k in range(order // BLOCK)]


def early_gram_kernel(share, *refs):
    block_refs, left_ref, direction_ref = refs[:-2], refs[-2], refs[-1]
    order = block_refs[0].shape[1]
    packed, first_row = packed_gram(block_refs)
    direction = main_direction(first_row, share)
    direction_ref[...] = stacked([direction])
    outer = outer_products(stacked([direction]))
    for quarter, (value, known) in enumerate(zip(packed, pack(lambda i, j: outer[i, j], order))):
        left_ref[quarter] = value - known


def gram_kernel(rest_count, early_ref, direction_ref, *refs):
    block_refs, left_ref, message_refs = refs[:-4], refs[-4], refs[-3:]
    order = block_refs[0].shape[1]
    for quarter, value in enumerate(packed_gram(block_refs)[0]):
        left_ref[quarter] = early_ref[quarter] + value
    place = Place(rest_count)
    direction = direction_ref[...].astype(jnp.float32)[:1]
    for step, message_ref in enumerate(message_refs):
        message_ref[...] = to_message(left_ref[place.quarter_at(step)], order, direction)


def gather_kernel(rest_count, order, left_ref, direction_ref, *refs):
    arrived_refs, total_ref, directions_ref, message_refs = refs[:3], refs[3], refs[4], refs[5:]
    arrived = [from_message(arrived_ref[...], order) for arrived_ref in arrived_refs]
    total = left_ref[Place(rest_count).quarter] + (arrived[0] + (arrived[1] + arrived[2]))
    total_ref[...] = total
    for value, message_ref in zip(arrived, message_refs):
        message_ref[...] = to_message(total - value, order)
    own = direction_ref[...].astype(jnp.float32)[:1]
    directions_ref[...] = stacked([own] + [vector_of(arrived_ref[...], order) for arrived_ref in arrived_refs])


def base_kernel(rest_count, order, left_ref, total_ref, directions_ref, base_ref):
    outer = outer_products(directions_ref[...])
    own = Place(rest_count).quarter
    for quarter, value in enumerate(pack(lambda i, j: outer[i, j], order)):
        base_ref[quarter] = jnp.where(quarter == own, total_ref[...], left_ref[quarter]) + value


def assemble(upper, count):
    return jnp.concatenate(
        [
            jnp.concatenate([upper[i, j] if i <= j else upper[j, i].T for j in range(count)], axis=1)
            for i in range(count)
        ],
        axis=0,
    )


def rounded(upper, count):
    return assemble({key: value.astype(jnp.bfloat16) for key, value in upper.items()}, count)


def symmetric_product(first, second, count):
    size = first.shape[0] // count
    return {
        (i, j): product(first[i * size : (i + 1) * size, :], second[:, j * size : (j + 1) * size])
        for i in range(count)
        for j in range(i, count)
    }


def combine(*terms):
    return {
        key: functools.reduce(jnp.add, [value[key] if factor == 1.0 else factor * value[key] for factor, value in terms])
        for key in terms[0][1]
    }


def square_beside_diagonal(upper, count):
    shape = upper[0, 0].shape
    identity = lax.broadcasted_iota(jnp.int32, shape, 0) == lax.broadcasted_iota(jnp.int32, shape, 1)
    diagonals = [jnp.where(identity, upper[i, i], 0.0) for i in range(count)]
    columns = [jnp.sum(value, axis=1, keepdims=True) for value in diagonals]
    rows = [jnp.sum(value, axis=0, keepdims=True) for value in diagonals]
    beside = {
        (i, j): jnp.where(identity, 0.0, value) if i == j else value for (i, j), value in upper.items()
    }
    beside_high = rounded(beside, count)
    entries = {(i, j): (columns[i] + rows[j]) * value for (i, j), value in beside.items()}
    for i in range(count):
        entries[i, i] = entries[i, i] + diagonals[i] * diagonals[i]
    return combine((1.0, entries), (1.0, symmetric_product(beside_high, beside_high, count)))


def newton(current, count):
    accum_identity, accum = 1.0, None
    for iteration in range(ITERS):
        last = iteration + 1 == ITERS
        current_high = None if last else rounded(current, count)
        if last:
            squared = square_beside_diagonal(current, count)
        else:
            squared = symmetric_product(current_high, current_high, count)
        rest = combine((second_coef, current), (third_coef, squared))
        rest_high = rounded(rest, count)
        if not last:
            inner = symmetric_product(current_high, rest_high, count)
            current = combine(
                (first_coef * first_coef, current),
                (2.0 * first_coef, inner),
                (1.0, symmetric_product(rounded(inner, count), rest_high, count)),
            )
        if accum is None:
            accum = rest
        else:
            accum = combine(
                (accum_identity, rest),
                (first_coef, accum),
                (1.0, symmetric_product(rounded(accum, count), rest_high, count)),
            )
        accum_identity *= first_coef
    return accum_identity, accum


def update_kernel(rest_count, order, scale, base_ref, *refs):
    rest_refs, quarters_ref = refs[:3], refs[-1]
    block_refs, update_refs = refs[3 : 3 + len(refs[4:]) // 2], refs[3 + len(refs[4:]) // 2 : -1]
    place = Place(rest_count)
    quarters_ref[place.quarter] = base_ref[place.quarter]
    for step, rest_ref in enumerate(rest_refs):
        quarter = place.quarter_at(step)
        quarters_ref[quarter] = base_ref[quarter] + from_message(rest_ref[...], order)
    blocks = unpack([quarters_ref[quarter] for quarter in range(4)], order)
    trace_sum = jnp.sum(sum(diagonal(blocks[i, i]) for i in range(order // BLOCK)))
    shrink = 1.0 / (trace_sum + epsilon)
    count, ratio = order // WIDE, WIDE // BLOCK
    current = {}
    for i in range(count):
        for j in range(i, count):
            tile = jnp.concatenate(
                [
                    jnp.concatenate(
                        [
                            blocks[row, column] if row <= column else blocks[column, row].T
                            for column in range(j * ratio, (j + 1) * ratio)
                        ],
                        axis=1,
                    )
                    for row in range(i * ratio, (i + 1) * ratio)
                ],
                axis=0,
            )
            current[i, j] = tile * shrink
    accum_identity, accum = newton(current, count)
    growth = jnp.sqrt(scale / (trace_sum + epsilon))
    shape = (WIDE, WIDE)
    identity = lax.broadcasted_iota(jnp.int32, shape, 0) == lax.broadcasted_iota(jnp.int32, shape, 1)
    factor = rounded(
        {
            (i, j): (value + jnp.where(identity, accum_identity, 0.0) if i == j else value) * growth
            for (i, j), value in accum.items()
        },
        count,
    )
    update = product(jnp.concatenate([block_ref[...] for block_ref in block_refs], axis=0), factor)
    row_count = block_refs[0].shape[0]
    for number, update_ref in enumerate(update_refs):
        update_ref[...] = update[number * row_count : (number + 1) * row_count].astype(update_ref.dtype)


def weights_kernel(rest_count, numbers, weights_ref, *refs):
    out_ref, fresh_ref, semaphores = refs[-3:]
    place = Place(rest_count)
    shrink = 1.0 - step_rate * decay_rate
    copies = []
    for slot, (number, update_ref) in enumerate(zip(numbers, refs)):
        block = place.block(number)
        fresh_ref[slot] = (
            shrink * weights_ref[block].astype(jnp.float32) - step_rate * update_ref[...].astype(jnp.float32)
        ).astype(fresh_ref.dtype)
        copies.append(pltpu.make_async_copy(fresh_ref.at[slot], out_ref.at[block], semaphores.at[slot]))
        copies[-1].start()
    for copy in copies:
        copy.wait()


def new_weights(rest_count, numbers, weights, updates, so_far=None):
    vmem, whole = pl.BlockSpec(memory_space=pltpu.VMEM), pl.BlockSpec(memory_space=pltpu.HBM)
    operands = [weights, *updates] + ([] if so_far is None else [so_far])
    return pl.pallas_call(
        functools.partial(weights_kernel, rest_count, numbers),
        out_shape=jax.ShapeDtypeStruct(weights.shape, weights.dtype),
        in_specs=[vmem] * (1 + len(updates)) + ([] if so_far is None else [whole]),
        out_specs=whole,
        scratch_shapes=[
            pltpu.VMEM((len(numbers),) + weights.shape[2:], weights.dtype),
            pltpu.SemaphoreType.DMA((len(numbers),)),
        ],
        input_output_aliases={} if so_far is None else {len(operands) - 1: 0},
        compiler_params=pltpu.CompilerParams(vmem_limit_bytes=VMEM_BYTES),
    )(*operands)


def on_device(momentum, weights):
    order = momentum.shape[3]
    opt, layer = lax.axis_size("opt"), lax.axis_size("layer")
    rest_count = opt // 8
    rest_groups = [[group * rest_count + rest for rest in range(rest_count)] for group in range(8)]
    scale = float(layer * opt * momentum.shape[2])

    def regroup(array, split_axis, concat_axis):
        if rest_count == 1:
            return array
        return lax.all_to_all(
            array,
            "opt",
            split_axis=split_axis,
            concat_axis=concat_axis,
            axis_index_groups=rest_groups,
            tiled=True,
        )

    def swap(arrays, partners, back=False):
        permutes = swaps(opt, layer, partners)
        if back:
            permutes = [[(target, source) for source, target in permute] for permute in permutes]
        return [lax.ppermute(array, AXES, permute) for array, permute in zip(arrays, permutes)]

    spread = regroup(momentum[0], 0, 1)
    experts, row_count, _ = spread.shape
    by_block = (experts // 2, 2, row_count, order)
    blocks = (jax.ShapeDtypeStruct(by_block[2:], spread.dtype),) * (1 + len(ROWS))
    packed, message = packed_shape(order), message_shape(order)
    quarter = jax.ShapeDtypeStruct(packed.shape[1:], packed.dtype)

    own, *dealt = call(
        functools.partial(deal_kernel, rest_count),
        blocks,
        spread.reshape(by_block),
    )
    rows = [own] + swap(dealt, ROWS)
    direction = jax.ShapeDtypeStruct((BF16_TILE, order), jnp.bfloat16)
    early_left, own_direction = call(
        functools.partial(early_gram_kernel, EARLY / len(rows)), (packed, direction), *rows[:EARLY]
    )
    left, *parts = call(
        functools.partial(gram_kernel, rest_count),
        (packed,) + (message,) * 3,
        early_left,
        own_direction,
        *rows[EARLY:],
    )
    total, directions, *rests = call(
        functools.partial(gather_kernel, rest_count, order),
        (quarter, direction) + (message,) * 3,
        left,
        own_direction,
        *swap(parts, OWNERS),
    )
    base = call(functools.partial(base_kernel, rest_count, order), packed, left, total, directions)
    own_update, *updates = call(
        functools.partial(update_kernel, rest_count, order, scale),
        blocks,
        base,
        *swap(rests, OWNERS),
        *rows,
        scratch=[pltpu.VMEM(packed.shape, packed.dtype)],
    )
    held = regroup(weights[0], 0, 1).reshape(by_block)
    returned = [own_update] + swap(updates, ROWS, back=True)
    numbers = range(len(blocks))
    fresh = new_weights(rest_count, numbers[:EARLY], held, returned[:EARLY])
    fresh = new_weights(rest_count, numbers[EARLY:], held, returned[EARLY:], fresh)
    return regroup(fresh.reshape(experts, row_count, order), 1, 0)[None]


def solution(mesh):
    in_specs = (P("layer", None, "opt", None), P("layer", None, "opt", None))
    out_specs = P("layer", None, "opt", None)
    return jax.shard_map(
        on_device, mesh=mesh, in_specs=in_specs, out_specs=out_specs, check_vma=False
    )
```

```python
import functools
import itertools

import jax
import jax.numpy as jnp
from jax import lax
from jax.experimental import pallas as pl
from jax.experimental.pallas import tpu as pltpu
from jax.sharding import PartitionSpec as P

ITERS = 3
BLOCK = 128
WIDE = 256
F32_TILE = 8
BF16_TILE = 16
SMALLEST = 1e-30
VMEM_BYTES = 48 << 20
EARLY = 5

first_coef = 3.4445
second_coef = -4.775
third_coef = 2.0315
epsilon = 1e-06
step_rate = 0.5
decay_rate = 0.1

AXES = ("opt", "layer")


def flips_of(z, y, x, pair=0, half=0):
    return (half, z, y, 0, x, pair)


def neighbour_steps():
    x, y, z = (0, 0, 1), (0, 1, 0), (1, 0, 0)
    order = [(y, x), (x, z), (z, y)]
    return [tuple(flips_of(*way, pair=cross) for way in step) for cross in (1, 0) for step in order]


ROWS = neighbour_steps() + [(flips_of(0, 0, 0, pair=1),) * 2]
BOTH, ANTIPODE, MIRROR = flips_of(0, 1, 1, half=1), flips_of(1, 1, 1), flips_of(1, 0, 0, half=1)
OWNERS = [(flips,) * 2 for flips in (BOTH, ANTIPODE, MIRROR)]


def colour_step(flips):
    return flips[4] ^ 2 * flips[2] ^ 3 * (flips[1] ^ flips[0])


def quarter_step(flips):
    return flips[4] + 2 * flips[0]


def swaps(opt, layer, partners):
    rest_count = opt // 8
    sizes = (2, 2, 2, rest_count, 2, 2)

    def device(half, z, y, rest, x, pair):
        return (((half * 2 + z) * 2 + y) * rest_count + rest) * layer + x * 2 + pair

    return [
        [
            (device(*spot), device(*(value ^ flip for value, flip in zip(spot, flips[spot[5]]))))
            for spot in itertools.product(*map(range, sizes))
        ]
        for flips in partners
    ]


def by_pair(pair, values):
    return values[0] + pair * (values[1] - values[0])


class Place:
    def __init__(self, rest_count):
        index = lax.axis_index("opt") // rest_count
        x, self.pair = lax.axis_index("layer") // 2, lax.axis_index("layer") % 2
        half, z, y = index // 4, index // 2 % 2, index % 2
        self.colour = x ^ (2 * y) ^ (3 * (z ^ half))
        self.quarter = x + 2 * half

    def block(self, number):
        if number == 0:
            return self.colour, self.pair
        flips = ROWS[number - 1]
        return self.colour ^ by_pair(self.pair, [colour_step(way) for way in flips]), self.pair ^ flips[0][5]

    def quarter_at(self, step):
        return self.quarter ^ by_pair(self.pair, [quarter_step(flips) for flips in OWNERS[step]])


def call(kernel, out_shape, *operands, scratch=()):
    vmem = pl.BlockSpec(memory_space=pltpu.VMEM)
    return pl.pallas_call(
        kernel,
        out_shape=out_shape,
        in_specs=[vmem] * len(operands),
        out_specs=jax.tree.map(lambda _: vmem, out_shape),
        scratch_shapes=list(scratch),
        compiler_params=pltpu.CompilerParams(vmem_limit_bytes=VMEM_BYTES),
    )(*operands)


def product(first, second):
    return jnp.dot(first, second, preferred_element_type=jnp.float32)


def quarters_of(order):
    count = order // BLOCK
    folds = [("fold", i, i + 1) for i in range(0, count, 2)]
    others = [("plain", i, j) for i in range(count) for j in range(i + 1, count)]
    length = (len(folds) + len(others)) // 4
    quarters = []
    for quarter in range(4):
        blocks = folds[quarter::4]
        missing = length - len(blocks)
        quarters.append(blocks + others[:missing])
        others = others[missing:]
    return quarters


def quarter_blocks(order):
    quarters = quarters_of(order)
    return max(sum(kind == "fold" for kind, _, _ in blocks) for blocks in quarters), len(quarters[0])


def packed_shape(order):
    return jax.ShapeDtypeStruct((4, quarter_blocks(order)[1] * BLOCK + F32_TILE, BLOCK), jnp.float32)


def message_shape(order):
    return jax.ShapeDtypeStruct((quarter_blocks(order)[1] * BLOCK + BF16_TILE, BLOCK), jnp.bfloat16)


def grid_ids():
    shape = (BLOCK, BLOCK)
    return lax.broadcasted_iota(jnp.int32, shape, 0), lax.broadcasted_iota(jnp.int32, shape, 1)


def diagonal(block):
    row_ids, column_ids = grid_ids()
    return jnp.sum(jnp.where(row_ids == column_ids, block, 0.0), axis=0, keepdims=True)


def padded(rows, height):
    missing = height - sum(row.shape[0] for row in rows)
    return jnp.concatenate(rows + [jnp.zeros((missing, BLOCK), jnp.float32)], axis=0)


def pack(block, order):
    row_ids, column_ids = grid_ids()
    result = []
    for blocks in quarters_of(order):
        tiles, rows = [], []
        for kind, i, j in blocks:
            if kind == "fold":
                second = block(j, j)
                tiles.append(jnp.where(row_ids <= column_ids, block(i, i), second))
                rows.append(diagonal(second))
            else:
                tiles.append(block(i, j))
        result.append(jnp.concatenate(tiles + [padded(rows, F32_TILE)], axis=0))
    return result


def unpack(quarters, order):
    row_ids, column_ids = grid_ids()
    result = {}
    for blocks, quarter in zip(quarters_of(order), quarters):
        tail = quarter[len(blocks) * BLOCK :]
        for k, (kind, i, j) in enumerate(blocks):
            tile = quarter[k * BLOCK : (k + 1) * BLOCK]
            if kind == "fold":
                mirrored = tile.T
                result[i, i] = jnp.where(row_ids <= column_ids, tile, mirrored)
                second = jnp.where(row_ids > column_ids, tile, mirrored)
                result[j, j] = jnp.where(row_ids == column_ids, tail[k : k + 1], second)
            else:
                result[i, j] = tile
    return result


def to_message(quarter, order, vector=None):
    fold_count, block_count = quarter_blocks(order)
    length = block_count * BLOCK
    body, tail = quarter[:length], quarter[length : length + fold_count]
    rounded_body = body.astype(jnp.bfloat16)
    rows = [
        diagonal(
            body[k * BLOCK : (k + 1) * BLOCK] - rounded_body[k * BLOCK : (k + 1) * BLOCK].astype(jnp.float32)
        )
        for k in range(fold_count)
    ]
    high = tail.astype(jnp.bfloat16).astype(jnp.float32)
    rows += [high, tail - high]
    if vector is not None:
        rows += [vector[:, k : k + BLOCK] for k in range(0, order, BLOCK)]
    return jnp.concatenate([rounded_body, padded(rows, BF16_TILE).astype(jnp.bfloat16)], axis=0)


def from_message(message, order):
    fold_count, block_count = quarter_blocks(order)
    length = block_count * BLOCK
    row_ids, column_ids = grid_ids()
    values = message.astype(jnp.float32)
    body, extra = values[:length], values[length:]
    tiles = [
        body[k * BLOCK : (k + 1) * BLOCK] + jnp.where(row_ids == column_ids, extra[k : k + 1], 0.0)
        for k in range(fold_count)
    ]
    tail = extra[fold_count : 2 * fold_count] + extra[2 * fold_count : 3 * fold_count]
    return jnp.concatenate(tiles + [body[fold_count * BLOCK :], padded([tail], F32_TILE)], axis=0)


def vector_of(message, order):
    fold_count, block_count = quarter_blocks(order)
    start = block_count * BLOCK + 3 * fold_count
    values = message.astype(jnp.float32)
    return jnp.concatenate([values[start + k : start + k + 1] for k in range(order // BLOCK)], axis=1)


def stacked(vectors):
    rows = jnp.concatenate(vectors, axis=0)
    filler = jnp.zeros((BF16_TILE - rows.shape[0], rows.shape[1]), jnp.float32)
    return jnp.concatenate([rows, filler], axis=0).astype(jnp.bfloat16)


def outer_products(vectors):
    order = vectors.shape[1]
    result = {}
    for start in range(0, order, BLOCK):
        band = lax.dot_general(
            vectors[:, start : start + BLOCK],
            vectors[:, start:],
            (((0,), (0,)), ((), ())),
            preferred_element_type=jnp.float32,
        )
        for offset in range(0, order - start, BLOCK):
            place = start // BLOCK, (start + offset) // BLOCK
            result[place] = band[:, offset : offset + BLOCK]
    return result


def main_direction(first_row, share):
    signs = jnp.where(first_row[0][:, :1] < 0.0, -1.0, 1.0)
    rows = [jnp.sum(signs * block, axis=0, keepdims=True) for block in first_row]
    size = jnp.sum(jnp.where(first_row[0][:1, :] < 0.0, -rows[0], rows[0]))
    growth = jnp.where(size > 0.0, lax.rsqrt(jnp.maximum(share * size, SMALLEST)), 0.0)
    return (jnp.concatenate(rows, axis=1) * growth).astype(jnp.bfloat16).astype(jnp.float32)


def deal_kernel(rest_count, momentum_ref, *refs):
    place = Place(rest_count)
    for number, block_ref in enumerate(refs):
        block_ref[...] = momentum_ref[place.block(number)]


def packed_gram(block_refs):
    rows = jnp.concatenate([block_ref[...] for block_ref in block_refs], axis=0)
    order = rows.shape[1]
    tiles = {}
    for row in range(0, order, WIDE):
        for column in range(row, order, WIDE):
            tiles[row, column] = lax.dot_general(
                rows[:, row : row + WIDE],
                rows[:, column : column + WIDE],
                (((0,), (0,)), ((), ())),
                preferred_element_type=jnp.float32,
            )

    def block(i, j):
        row, column = i * BLOCK, j * BLOCK
        tile = tiles[row // WIDE * WIDE, column // WIDE * WIDE]
        return tile[row % WIDE :, column % WIDE :][:BLOCK, :BLOCK]

    return pack(block, order), [block(0, k) for k in range(order // BLOCK)]


def early_gram_kernel(share, *refs):
    block_refs, left_ref, direction_ref = refs[:-2], refs[-2], refs[-1]
    order = block_refs[0].shape[1]
    packed, first_row = packed_gram(block_refs)
    direction = main_direction(first_row, share)
    direction_ref[...] = stacked([direction])
    outer = outer_products(stacked([direction]))
    for quarter, (value, known) in enumerate(zip(packed, pack(lambda i, j: outer[i, j], order))):
        left_ref[quarter] = value - known


def middle_gram_kernel(early_ref, *refs):
    for quarter, value in enumerate(packed_gram(refs[:-1])[0]):
        refs[-1][quarter] = early_ref[quarter] + value


def gram_kernel(rest_count, early_ref, direction_ref, *refs):
    block_refs, left_ref, message_refs = refs[:-4], refs[-4], refs[-3:]
    order = block_refs[0].shape[1]
    for quarter, value in enumerate(packed_gram(block_refs)[0]):
        left_ref[quarter] = early_ref[quarter] + value
    place = Place(rest_count)
    direction = direction_ref[...].astype(jnp.float32)[:1]
    for step, message_ref in enumerate(message_refs):
        message_ref[...] = to_message(left_ref[place.quarter_at(step)], order, direction)


def gather_kernel(rest_count, order, left_ref, direction_ref, *refs):
    arrived_refs, total_ref, directions_ref, message_refs = refs[:3], refs[3], refs[4], refs[5:]
    arrived = [from_message(arrived_ref[...], order) for arrived_ref in arrived_refs]
    total = left_ref[Place(rest_count).quarter] + (arrived[0] + (arrived[1] + arrived[2]))
    total_ref[...] = total
    for value, message_ref in zip(arrived, message_refs):
        message_ref[...] = to_message(total - value, order)
    own = direction_ref[...].astype(jnp.float32)[:1]
    directions_ref[...] = stacked([own] + [vector_of(arrived_ref[...], order) for arrived_ref in arrived_refs])


def base_kernel(rest_count, order, left_ref, total_ref, directions_ref, base_ref):
    outer = outer_products(directions_ref[...])
    own = Place(rest_count).quarter
    for quarter, value in enumerate(pack(lambda i, j: outer[i, j], order)):
        base_ref[quarter] = jnp.where(quarter == own, total_ref[...], left_ref[quarter]) + value


def assemble(upper, count):
    return jnp.concatenate(
        [
            jnp.concatenate([upper[i, j] if i <= j else upper[j, i].T for j in range(count)], axis=1)
            for i in range(count)
        ],
        axis=0,
    )


def rounded(upper, count):
    return assemble({key: value.astype(jnp.bfloat16) for key, value in upper.items()}, count)


def symmetric_product(first, second, count):
    size = first.shape[0] // count
    return {
        (i, j): product(first[i * size : (i + 1) * size, :], second[:, j * size : (j + 1) * size])
        for i in range(count)
        for j in range(i, count)
    }


def combine(*terms):
    return {
        key: functools.reduce(jnp.add, [value[key] if factor == 1.0 else factor * value[key] for factor, value in terms])
        for key in terms[0][1]
    }


def square_beside_diagonal(upper, count):
    shape = upper[0, 0].shape
    identity = lax.broadcasted_iota(jnp.int32, shape, 0) == lax.broadcasted_iota(jnp.int32, shape, 1)
    diagonals = [jnp.where(identity, upper[i, i], 0.0) for i in range(count)]
    columns = [jnp.sum(value, axis=1, keepdims=True) for value in diagonals]
    rows = [jnp.sum(value, axis=0, keepdims=True) for value in diagonals]
    beside = {
        (i, j): jnp.where(identity, 0.0, value) if i == j else value for (i, j), value in upper.items()
    }
    beside_high = rounded(beside, count)
    entries = {(i, j): (columns[i] + rows[j]) * value for (i, j), value in beside.items()}
    for i in range(count):
        entries[i, i] = entries[i, i] + diagonals[i] * diagonals[i]
    return combine((1.0, entries), (1.0, symmetric_product(beside_high, beside_high, count)))


def newton(current, count):
    accum_identity, accum = 1.0, None
    for iteration in range(ITERS):
        last = iteration + 1 == ITERS
        current_high = None if last else rounded(current, count)
        if last:
            squared = square_beside_diagonal(current, count)
        else:
            squared = symmetric_product(current_high, current_high, count)
        rest = combine((second_coef, current), (third_coef, squared))
        rest_high = rounded(rest, count)
        if not last:
            inner = symmetric_product(current_high, rest_high, count)
            current = combine(
                (first_coef * first_coef, current),
                (2.0 * first_coef, inner),
                (1.0, symmetric_product(rounded(inner, count), rest_high, count)),
            )
        if accum is None:
            accum = rest
        else:
            accum = combine(
                (accum_identity, rest),
                (first_coef, accum),
                (1.0, symmetric_product(rounded(accum, count), rest_high, count)),
            )
        accum_identity *= first_coef
    return accum_identity, accum


def update_kernel(rest_count, order, scale, base_ref, *refs):
    rest_refs, quarters_ref = refs[:3], refs[-1]
    block_refs, update_refs = refs[3 : 3 + len(refs[4:]) // 2], refs[3 + len(refs[4:]) // 2 : -1]
    place = Place(rest_count)
    quarters_ref[place.quarter] = base_ref[place.quarter]
    for step, rest_ref in enumerate(rest_refs):
        quarter = place.quarter_at(step)
        quarters_ref[quarter] = base_ref[quarter] + from_message(rest_ref[...], order)
    blocks = unpack([quarters_ref[quarter] for quarter in range(4)], order)
    trace_sum = jnp.sum(sum(diagonal(blocks[i, i]) for i in range(order // BLOCK)))
    shrink = 1.0 / (trace_sum + epsilon)
    count, ratio = order // WIDE, WIDE // BLOCK
    current = {}
    for i in range(count):
        for j in range(i, count):
            tile = jnp.concatenate(
                [
                    jnp.concatenate(
                        [
                            blocks[row, column] if row <= column else blocks[column, row].T
                            for column in range(j * ratio, (j + 1) * ratio)
                        ],
                        axis=1,
                    )
                    for row in range(i * ratio, (i + 1) * ratio)
                ],
                axis=0,
            )
            current[i, j] = tile * shrink
    accum_identity, accum = newton(current, count)
    growth = jnp.sqrt(scale / (trace_sum + epsilon))
    shape = (WIDE, WIDE)
    identity = lax.broadcasted_iota(jnp.int32, shape, 0) == lax.broadcasted_iota(jnp.int32, shape, 1)
    factor = rounded(
        {
            (i, j): (value + jnp.where(identity, accum_identity, 0.0) if i == j else value) * growth
            for (i, j), value in accum.items()
        },
        count,
    )
    update = product(jnp.concatenate([block_ref[...] for block_ref in block_refs], axis=0), factor)
    row_count = block_refs[0].shape[0]
    for number, update_ref in enumerate(update_refs):
        update_ref[...] = update[number * row_count : (number + 1) * row_count].astype(update_ref.dtype)


def weights_kernel(rest_count, numbers, weights_ref, *refs):
    out_ref, fresh_ref, semaphores = refs[-3:]
    place = Place(rest_count)
    shrink = 1.0 - step_rate * decay_rate
    copies = []
    for slot, (number, update_ref) in enumerate(zip(numbers, refs)):
        block = place.block(number)
        fresh_ref[slot] = (
            shrink * weights_ref[block].astype(jnp.float32) - step_rate * update_ref[...].astype(jnp.float32)
        ).astype(fresh_ref.dtype)
        copies.append(pltpu.make_async_copy(fresh_ref.at[slot], out_ref.at[block], semaphores.at[slot]))
        copies[-1].start()
    for copy in copies:
        copy.wait()


def new_weights(rest_count, numbers, weights, updates, so_far=None):
    vmem, whole = pl.BlockSpec(memory_space=pltpu.VMEM), pl.BlockSpec(memory_space=pltpu.HBM)
    operands = [weights, *updates] + ([] if so_far is None else [so_far])
    return pl.pallas_call(
        functools.partial(weights_kernel, rest_count, numbers),
        out_shape=jax.ShapeDtypeStruct(weights.shape, weights.dtype),
        in_specs=[vmem] * (1 + len(updates)) + ([] if so_far is None else [whole]),
        out_specs=whole,
        scratch_shapes=[
            pltpu.VMEM((len(numbers),) + weights.shape[2:], weights.dtype),
            pltpu.SemaphoreType.DMA((len(numbers),)),
        ],
        input_output_aliases={} if so_far is None else {len(operands) - 1: 0},
        compiler_params=pltpu.CompilerParams(vmem_limit_bytes=VMEM_BYTES),
    )(*operands)


def on_device(momentum, weights):
    order = momentum.shape[3]
    opt, layer = lax.axis_size("opt"), lax.axis_size("layer")
    rest_count = opt // 8
    rest_groups = [[group * rest_count + rest for rest in range(rest_count)] for group in range(8)]
    scale = float(layer * opt * momentum.shape[2])

    def regroup(array, split_axis, concat_axis):
        if rest_count == 1:
            return array
        return lax.all_to_all(
            array,
            "opt",
            split_axis=split_axis,
            concat_axis=concat_axis,
            axis_index_groups=rest_groups,
            tiled=True,
        )

    def swap(arrays, partners, back=False):
        permutes = swaps(opt, layer, partners)
        if back:
            permutes = [[(target, source) for source, target in permute] for permute in permutes]
        return [lax.ppermute(array, AXES, permute) for array, permute in zip(arrays, permutes)]

    spread = regroup(momentum[0], 0, 1)
    experts, row_count, _ = spread.shape
    by_block = (experts // 2, 2, row_count, order)
    blocks = (jax.ShapeDtypeStruct(by_block[2:], spread.dtype),) * (1 + len(ROWS))
    packed, message = packed_shape(order), message_shape(order)
    quarter = jax.ShapeDtypeStruct(packed.shape[1:], packed.dtype)

    own, *dealt = call(
        functools.partial(deal_kernel, rest_count),
        blocks,
        spread.reshape(by_block),
    )
    rows = [own] + swap(dealt, ROWS)
    direction = jax.ShapeDtypeStruct((BF16_TILE, order), jnp.bfloat16)
    early_left, own_direction = call(
        functools.partial(early_gram_kernel, EARLY / len(rows)), (packed, direction), *rows[:EARLY]
    )
    early_left = call(middle_gram_kernel, packed, early_left, *[rows[number] for number in (5,)])
    left, *parts = call(
        functools.partial(gram_kernel, rest_count),
        (packed,) + (message,) * 3,
        early_left,
        own_direction,
        *[rows[number] for number in (6, 7)],
    )
    total, directions, *rests = call(
        functools.partial(gather_kernel, rest_count, order),
        (quarter, direction) + (message,) * 3,
        left,
        own_direction,
        *swap(parts, OWNERS),
    )
    base = call(functools.partial(base_kernel, rest_count, order), packed, left, total, directions)
    own_update, *updates = call(
        functools.partial(update_kernel, rest_count, order, scale),
        blocks,
        base,
        *swap(rests, OWNERS),
        *rows,
        scratch=[pltpu.VMEM(packed.shape, packed.dtype)],
    )
    held = regroup(weights[0], 0, 1).reshape(by_block)
    returned = [own_update] + swap(updates, ROWS, back=True)
    numbers = range(len(blocks))
    fresh = new_weights(rest_count, numbers[:EARLY], held, returned[:EARLY])
    fresh = new_weights(rest_count, numbers[EARLY:], held, returned[EARLY:], fresh)
    return regroup(fresh.reshape(experts, row_count, order), 1, 0)[None]


def solution(mesh):
    in_specs = (P("layer", None, "opt", None), P("layer", None, "opt", None))
    out_specs = P("layer", None, "opt", None)
    return jax.shard_map(
        on_device, mesh=mesh, in_specs=in_specs, out_specs=out_specs, check_vma=False
    )
```

```python
import functools
import itertools

import jax
import jax.numpy as jnp
from jax import lax
from jax.experimental import pallas as pl
from jax.experimental.pallas import tpu as pltpu
from jax.sharding import PartitionSpec as P

ITERS = 3
BLOCK = 128
WIDE = 256
F32_TILE = 8
BF16_TILE = 16
SMALLEST = 1e-30
VMEM_BYTES = 48 << 20
EARLY = 5

first_coef = 3.4445
second_coef = -4.775
third_coef = 2.0315
epsilon = 1e-06
step_rate = 0.5
decay_rate = 0.1

AXES = ("opt", "layer")


def flips_of(z, y, x, pair=0, half=0):
    return (half, z, y, 0, x, pair)


def neighbour_steps():
    x, y, z = (0, 0, 1), (0, 1, 0), (1, 0, 0)
    order = [(y, x), (x, z), (z, y)]
    return [tuple(flips_of(*way, pair=cross) for way in step) for cross in (1, 0) for step in order]


ROWS = neighbour_steps() + [(flips_of(0, 0, 0, pair=1),) * 2]
BOTH, ANTIPODE, MIRROR = flips_of(0, 1, 1, half=1), flips_of(1, 1, 1), flips_of(1, 0, 0, half=1)
OWNERS = [(flips,) * 2 for flips in (BOTH, ANTIPODE, MIRROR)]


def colour_step(flips):
    return flips[4] ^ 2 * flips[2] ^ 3 * (flips[1] ^ flips[0])


def quarter_step(flips):
    return flips[4] + 2 * flips[0]


def swaps(opt, layer, partners):
    rest_count = opt // 8
    sizes = (2, 2, 2, rest_count, 2, 2)

    def device(half, z, y, rest, x, pair):
        return (((half * 2 + z) * 2 + y) * rest_count + rest) * layer + x * 2 + pair

    return [
        [
            (device(*spot), device(*(value ^ flip for value, flip in zip(spot, flips[spot[5]]))))
            for spot in itertools.product(*map(range, sizes))
        ]
        for flips in partners
    ]


def by_pair(pair, values):
    return values[0] + pair * (values[1] - values[0])


class Place:
    def __init__(self, rest_count):
        index = lax.axis_index("opt") // rest_count
        x, self.pair = lax.axis_index("layer") // 2, lax.axis_index("layer") % 2
        half, z, y = index // 4, index // 2 % 2, index % 2
        self.colour = x ^ (2 * y) ^ (3 * (z ^ half))
        self.quarter = x + 2 * half

    def block(self, number):
        if number == 0:
            return self.colour, self.pair
        flips = ROWS[number - 1]
        return self.colour ^ by_pair(self.pair, [colour_step(way) for way in flips]), self.pair ^ flips[0][5]

    def quarter_at(self, step):
        return self.quarter ^ by_pair(self.pair, [quarter_step(flips) for flips in OWNERS[step]])


def call(kernel, out_shape, *operands, scratch=()):
    vmem = pl.BlockSpec(memory_space=pltpu.VMEM)
    return pl.pallas_call(
        kernel,
        out_shape=out_shape,
        in_specs=[vmem] * len(operands),
        out_specs=jax.tree.map(lambda _: vmem, out_shape),
        scratch_shapes=list(scratch),
        compiler_params=pltpu.CompilerParams(vmem_limit_bytes=VMEM_BYTES),
    )(*operands)


def product(first, second):
    return jnp.dot(first, second, preferred_element_type=jnp.float32)


def quarters_of(order):
    count = order // BLOCK
    folds = [("fold", i, i + 1) for i in range(0, count, 2)]
    others = [("plain", i, j) for i in range(count) for j in range(i + 1, count)]
    length = (len(folds) + len(others)) // 4
    quarters = []
    for quarter in range(4):
        blocks = folds[quarter::4]
        missing = length - len(blocks)
        quarters.append(blocks + others[:missing])
        others = others[missing:]
    return quarters


def quarter_blocks(order):
    quarters = quarters_of(order)
    return max(sum(kind == "fold" for kind, _, _ in blocks) for blocks in quarters), len(quarters[0])


def packed_shape(order):
    return jax.ShapeDtypeStruct((4, quarter_blocks(order)[1] * BLOCK + F32_TILE, BLOCK), jnp.float32)


def message_shape(order):
    return jax.ShapeDtypeStruct((quarter_blocks(order)[1] * BLOCK + BF16_TILE, BLOCK), jnp.bfloat16)


def grid_ids():
    shape = (BLOCK, BLOCK)
    return lax.broadcasted_iota(jnp.int32, shape, 0), lax.broadcasted_iota(jnp.int32, shape, 1)


def diagonal(block):
    row_ids, column_ids = grid_ids()
    return jnp.sum(jnp.where(row_ids == column_ids, block, 0.0), axis=0, keepdims=True)


def padded(rows, height):
    missing = height - sum(row.shape[0] for row in rows)
    return jnp.concatenate(rows + [jnp.zeros((missing, BLOCK), jnp.float32)], axis=0)


def pack(block, order):
    row_ids, column_ids = grid_ids()
    result = []
    for blocks in quarters_of(order):
        tiles, rows = [], []
        for kind, i, j in blocks:
            if kind == "fold":
                second = block(j, j)
                tiles.append(jnp.where(row_ids <= column_ids, block(i, i), second))
                rows.append(diagonal(second))
            else:
                tiles.append(block(i, j))
        result.append(jnp.concatenate(tiles + [padded(rows, F32_TILE)], axis=0))
    return result


def unpack(quarters, order):
    row_ids, column_ids = grid_ids()
    result = {}
    for blocks, quarter in zip(quarters_of(order), quarters):
        tail = quarter[len(blocks) * BLOCK :]
        for k, (kind, i, j) in enumerate(blocks):
            tile = quarter[k * BLOCK : (k + 1) * BLOCK]
            if kind == "fold":
                mirrored = tile.T
                result[i, i] = jnp.where(row_ids <= column_ids, tile, mirrored)
                second = jnp.where(row_ids > column_ids, tile, mirrored)
                result[j, j] = jnp.where(row_ids == column_ids, tail[k : k + 1], second)
            else:
                result[i, j] = tile
    return result


def to_message(quarter, order, vector=None):
    fold_count, block_count = quarter_blocks(order)
    length = block_count * BLOCK
    body, tail = quarter[:length], quarter[length : length + fold_count]
    rounded_body = body.astype(jnp.bfloat16)
    rows = [
        diagonal(
            body[k * BLOCK : (k + 1) * BLOCK] - rounded_body[k * BLOCK : (k + 1) * BLOCK].astype(jnp.float32)
        )
        for k in range(fold_count)
    ]
    high = tail.astype(jnp.bfloat16).astype(jnp.float32)
    rows += [high, tail - high]
    if vector is not None:
        rows += [vector[:, k : k + BLOCK] for k in range(0, order, BLOCK)]
    return jnp.concatenate([rounded_body, padded(rows, BF16_TILE).astype(jnp.bfloat16)], axis=0)


def from_message(message, order):
    fold_count, block_count = quarter_blocks(order)
    length = block_count * BLOCK
    row_ids, column_ids = grid_ids()
    values = message.astype(jnp.float32)
    body, extra = values[:length], values[length:]
    tiles = [
        body[k * BLOCK : (k + 1) * BLOCK] + jnp.where(row_ids == column_ids, extra[k : k + 1], 0.0)
        for k in range(fold_count)
    ]
    tail = extra[fold_count : 2 * fold_count] + extra[2 * fold_count : 3 * fold_count]
    return jnp.concatenate(tiles + [body[fold_count * BLOCK :], padded([tail], F32_TILE)], axis=0)


def vector_of(message, order):
    fold_count, block_count = quarter_blocks(order)
    start = block_count * BLOCK + 3 * fold_count
    values = message.astype(jnp.float32)
    return jnp.concatenate([values[start + k : start + k + 1] for k in range(order // BLOCK)], axis=1)


def stacked(vectors):
    rows = jnp.concatenate(vectors, axis=0)
    filler = jnp.zeros((BF16_TILE - rows.shape[0], rows.shape[1]), jnp.float32)
    return jnp.concatenate([rows, filler], axis=0).astype(jnp.bfloat16)


def outer_products(vectors):
    order = vectors.shape[1]
    result = {}
    for start in range(0, order, BLOCK):
        band = lax.dot_general(
            vectors[:, start : start + BLOCK],
            vectors[:, start:],
            (((0,), (0,)), ((), ())),
            preferred_element_type=jnp.float32,
        )
        for offset in range(0, order - start, BLOCK):
            place = start // BLOCK, (start + offset) // BLOCK
            result[place] = band[:, offset : offset + BLOCK]
    return result


def main_direction(first_row, share):
    signs = jnp.where(first_row[0][:, :1] < 0.0, -1.0, 1.0)
    rows = [jnp.sum(signs * block, axis=0, keepdims=True) for block in first_row]
    size = jnp.sum(jnp.where(first_row[0][:1, :] < 0.0, -rows[0], rows[0]))
    growth = jnp.where(size > 0.0, lax.rsqrt(jnp.maximum(share * size, SMALLEST)), 0.0)
    return (jnp.concatenate(rows, axis=1) * growth).astype(jnp.bfloat16).astype(jnp.float32)


def deal_kernel(rest_count, momentum_ref, *refs):
    place = Place(rest_count)
    for number, block_ref in enumerate(refs):
        block_ref[...] = momentum_ref[place.block(number)]


def packed_gram(block_refs):
    rows = jnp.concatenate([block_ref[...] for block_ref in block_refs], axis=0)
    order = rows.shape[1]
    tiles = {}
    for row in range(0, order, WIDE):
        for column in range(row, order, WIDE):
            tiles[row, column] = lax.dot_general(
                rows[:, row : row + WIDE],
                rows[:, column : column + WIDE],
                (((0,), (0,)), ((), ())),
                preferred_element_type=jnp.float32,
            )

    def block(i, j):
        row, column = i * BLOCK, j * BLOCK
        tile = tiles[row // WIDE * WIDE, column // WIDE * WIDE]
        return tile[row % WIDE :, column % WIDE :][:BLOCK, :BLOCK]

    return pack(block, order), [block(0, k) for k in range(order // BLOCK)]


def early_gram_kernel(share, *refs):
    block_refs, left_ref, direction_ref = refs[:-2], refs[-2], refs[-1]
    order = block_refs[0].shape[1]
    packed, first_row = packed_gram(block_refs)
    direction = main_direction(first_row, share)
    direction_ref[...] = stacked([direction])
    outer = outer_products(stacked([direction]))
    for quarter, (value, known) in enumerate(zip(packed, pack(lambda i, j: outer[i, j], order))):
        left_ref[quarter] = value - known


def gram_kernel(rest_count, early_ref, direction_ref, *refs):
    block_refs, left_ref, message_refs = refs[:-4], refs[-4], refs[-3:]
    order = block_refs[0].shape[1]
    for quarter, value in enumerate(packed_gram(block_refs)[0]):
        left_ref[quarter] = early_ref[quarter] + value
    place = Place(rest_count)
    direction = direction_ref[...].astype(jnp.float32)[:1]
    for step, message_ref in enumerate(message_refs):
        message_ref[...] = to_message(left_ref[place.quarter_at(step)], order, direction)


def gather_kernel(rest_count, order, left_ref, direction_ref, *refs):
    arrived_refs, total_ref, directions_ref, message_refs = refs[:3], refs[3], refs[4], refs[5:]
    arrived = [from_message(arrived_ref[...], order) for arrived_ref in arrived_refs]
    total = left_ref[Place(rest_count).quarter] + (arrived[0] + (arrived[1] + arrived[2]))
    total_ref[...] = total
    for value, message_ref in zip(arrived, message_refs):
        message_ref[...] = to_message(total - value, order)
    own = direction_ref[...].astype(jnp.float32)[:1]
    directions_ref[...] = stacked([own] + [vector_of(arrived_ref[...], order) for arrived_ref in arrived_refs])


def base_kernel(rest_count, order, left_ref, total_ref, directions_ref, base_ref):
    outer = outer_products(directions_ref[...])
    own = Place(rest_count).quarter
    for quarter, value in enumerate(pack(lambda i, j: outer[i, j], order)):
        base_ref[quarter] = jnp.where(quarter == own, total_ref[...], left_ref[quarter]) + value


def assemble(upper, count):
    return jnp.concatenate(
        [
            jnp.concatenate([upper[i, j] if i <= j else upper[j, i].T for j in range(count)], axis=1)
            for i in range(count)
        ],
        axis=0,
    )


def rounded(upper, count):
    return assemble({key: value.astype(jnp.bfloat16) for key, value in upper.items()}, count)


def symmetric_product(first, second, count):
    size = first.shape[0] // count
    return {
        (i, j): product(first[i * size : (i + 1) * size, :], second[:, j * size : (j + 1) * size])
        for i in range(count)
        for j in range(i, count)
    }


def combine(*terms):
    return {
        key: functools.reduce(jnp.add, [value[key] if factor == 1.0 else factor * value[key] for factor, value in terms])
        for key in terms[0][1]
    }


def square_beside_diagonal(upper, count):
    shape = upper[0, 0].shape
    identity = lax.broadcasted_iota(jnp.int32, shape, 0) == lax.broadcasted_iota(jnp.int32, shape, 1)
    diagonals = [jnp.where(identity, upper[i, i], 0.0) for i in range(count)]
    columns = [jnp.sum(value, axis=1, keepdims=True) for value in diagonals]
    rows = [jnp.sum(value, axis=0, keepdims=True) for value in diagonals]
    beside = {
        (i, j): jnp.where(identity, 0.0, value) if i == j else value for (i, j), value in upper.items()
    }
    beside_high = rounded(beside, count)
    entries = {(i, j): (columns[i] + rows[j]) * value for (i, j), value in beside.items()}
    for i in range(count):
        entries[i, i] = entries[i, i] + diagonals[i] * diagonals[i]
    return combine((1.0, entries), (1.0, symmetric_product(beside_high, beside_high, count)))


def newton(current, count):
    accum_identity, accum = 1.0, None
    for iteration in range(ITERS):
        last = iteration + 1 == ITERS
        current_high = None if last else rounded(current, count)
        if last:
            squared = square_beside_diagonal(current, count)
        else:
            squared = symmetric_product(current_high, current_high, count)
        rest = combine((second_coef, current), (third_coef, squared))
        rest_high = rounded(rest, count)
        if not last:
            inner = symmetric_product(current_high, rest_high, count)
            current = combine(
                (first_coef * first_coef, current),
                (2.0 * first_coef, inner),
                (1.0, symmetric_product(rounded(inner, count), rest_high, count)),
            )
        if accum is None:
            accum = rest
        else:
            accum = combine(
                (accum_identity, rest),
                (first_coef, accum),
                (1.0, symmetric_product(rounded(accum, count), rest_high, count)),
            )
        accum_identity *= first_coef
    return accum_identity, accum


def update_kernel(rest_count, order, scale, base_ref, *refs):
    rest_refs, quarters_ref = refs[:3], refs[-1]
    block_refs, update_refs = refs[3 : 3 + len(refs[4:]) // 2], refs[3 + len(refs[4:]) // 2 : -1]
    place = Place(rest_count)
    quarters_ref[place.quarter] = base_ref[place.quarter]
    for step, rest_ref in enumerate(rest_refs):
        quarter = place.quarter_at(step)
        quarters_ref[quarter] = base_ref[quarter] + from_message(rest_ref[...], order)
    blocks = unpack([quarters_ref[quarter] for quarter in range(4)], order)
    trace_sum = jnp.sum(sum(diagonal(blocks[i, i]) for i in range(order // BLOCK)))
    shrink = 1.0 / (trace_sum + epsilon)
    count, ratio = order // WIDE, WIDE // BLOCK
    current = {}
    for i in range(count):
        for j in range(i, count):
            tile = jnp.concatenate(
                [
                    jnp.concatenate(
                        [
                            blocks[row, column] if row <= column else blocks[column, row].T
                            for column in range(j * ratio, (j + 1) * ratio)
                        ],
                        axis=1,
                    )
                    for row in range(i * ratio, (i + 1) * ratio)
                ],
                axis=0,
            )
            current[i, j] = tile * shrink
    accum_identity, accum = newton(current, count)
    growth = jnp.sqrt(scale / (trace_sum + epsilon))
    shape = (WIDE, WIDE)
    identity = lax.broadcasted_iota(jnp.int32, shape, 0) == lax.broadcasted_iota(jnp.int32, shape, 1)
    factor = rounded(
        {
            (i, j): (value + jnp.where(identity, accum_identity, 0.0) if i == j else value) * growth
            for (i, j), value in accum.items()
        },
        count,
    )
    update = product(jnp.concatenate([block_ref[...] for block_ref in block_refs], axis=0), factor)
    row_count = block_refs[0].shape[0]
    for number, update_ref in enumerate(update_refs):
        update_ref[...] = update[number * row_count : (number + 1) * row_count].astype(update_ref.dtype)


def weights_kernel(rest_count, numbers, weights_ref, *refs):
    out_ref, fresh_ref, semaphores = refs[-3:]
    place = Place(rest_count)
    shrink = 1.0 - step_rate * decay_rate
    copies = []
    for slot, (number, update_ref) in enumerate(zip(numbers, refs)):
        block = place.block(number)
        fresh_ref[slot] = (
            shrink * weights_ref[block].astype(jnp.float32) - step_rate * update_ref[...].astype(jnp.float32)
        ).astype(fresh_ref.dtype)
        copies.append(pltpu.make_async_copy(fresh_ref.at[slot], out_ref.at[block], semaphores.at[slot]))
        copies[-1].start()
    for copy in copies:
        copy.wait()


def new_weights(rest_count, numbers, weights, updates, so_far=None):
    vmem, whole = pl.BlockSpec(memory_space=pltpu.VMEM), pl.BlockSpec(memory_space=pltpu.HBM)
    operands = [weights, *updates] + ([] if so_far is None else [so_far])
    return pl.pallas_call(
        functools.partial(weights_kernel, rest_count, numbers),
        out_shape=jax.ShapeDtypeStruct(weights.shape, weights.dtype),
        in_specs=[vmem] * (1 + len(updates)) + ([] if so_far is None else [whole]),
        out_specs=whole,
        scratch_shapes=[
            pltpu.VMEM((len(numbers),) + weights.shape[2:], weights.dtype),
            pltpu.SemaphoreType.DMA((len(numbers),)),
        ],
        input_output_aliases={} if so_far is None else {len(operands) - 1: 0},
        compiler_params=pltpu.CompilerParams(vmem_limit_bytes=VMEM_BYTES),
    )(*operands)


def on_device(momentum, weights):
    order = momentum.shape[3]
    opt, layer = lax.axis_size("opt"), lax.axis_size("layer")
    rest_count = opt // 8
    rest_groups = [[group * rest_count + rest for rest in range(rest_count)] for group in range(8)]
    scale = float(layer * opt * momentum.shape[2])

    def regroup(array, split_axis, concat_axis):
        if rest_count == 1:
            return array
        return lax.all_to_all(
            array,
            "opt",
            split_axis=split_axis,
            concat_axis=concat_axis,
            axis_index_groups=rest_groups,
            tiled=True,
        )

    def swap(arrays, partners, back=False):
        permutes = swaps(opt, layer, partners)
        if back:
            permutes = [[(target, source) for source, target in permute] for permute in permutes]
        return [lax.ppermute(array, AXES, permute) for array, permute in zip(arrays, permutes)]

    spread = regroup(momentum[0], 0, 1)
    experts, row_count, _ = spread.shape
    by_block = (experts // 2, 2, row_count, order)
    blocks = (jax.ShapeDtypeStruct(by_block[2:], spread.dtype),) * (1 + len(ROWS))
    packed, message = packed_shape(order), message_shape(order)
    quarter = jax.ShapeDtypeStruct(packed.shape[1:], packed.dtype)

    own, *dealt = call(
        functools.partial(deal_kernel, rest_count),
        blocks,
        spread.reshape(by_block),
    )
    rows = [own] + swap(dealt, ROWS)
    direction = jax.ShapeDtypeStruct((BF16_TILE, order), jnp.bfloat16)
    early_left, own_direction = call(
        functools.partial(early_gram_kernel, EARLY / len(rows)), (packed, direction), *rows[:EARLY]
    )
    left, *parts = call(
        functools.partial(gram_kernel, rest_count),
        (packed,) + (message,) * 3,
        early_left,
        own_direction,
        *rows[EARLY:],
    )
    total, directions, *rests = call(
        functools.partial(gather_kernel, rest_count, order),
        (quarter, direction) + (message,) * 3,
        left,
        own_direction,
        *swap(parts, OWNERS),
    )
    base = call(functools.partial(base_kernel, rest_count, order), packed, left, total, directions)
    own_update, *updates = call(
        functools.partial(update_kernel, rest_count, order, scale),
        blocks,
        base,
        *swap(rests, OWNERS),
        *rows,
        scratch=[pltpu.VMEM(packed.shape, packed.dtype)],
    )
    held = regroup(weights[0], 0, 1).reshape(by_block)
    returned = [own_update] + swap(updates, ROWS, back=True)
    numbers = range(len(blocks))
    fresh = new_weights(rest_count, numbers[:EARLY], held, returned[:EARLY])
    fresh = new_weights(rest_count, numbers[EARLY:], held, returned[EARLY:], fresh)
    return regroup(fresh.reshape(experts, row_count, order), 1, 0)[None]


def solution(mesh):
    in_specs = (P("layer", None, "opt", None), P("layer", None, "opt", None))
    out_specs = P("layer", None, "opt", None)
    return jax.shard_map(
        on_device, mesh=mesh, in_specs=in_specs, out_specs=out_specs, check_vma=False
    )
```
